32 devices in a mesh: dp: 16 (over z, x, core), chan: 2 (over y).
Axes of the slice: x: 2, y: 2, z: 4, core: 2. Of those that a mesh axis runs over, the one named last changes fastest.
Arguments:
- tokens: bfloat16 [256, 512, 256], P('dp', 'chan'), may hold values from -6 to 6
- lengths: int32 [256], P('dp'), may hold values from 42 to 256
- frame_mask: int32 [256, 256], P('dp'), may hold values 0 or 1
- code_ids: int32 [256, 4, 256], P('dp'), may hold values from 0 to 1023
- cotangent: bfloat16 [256, 512, 256], P('dp', 'chan'), may hold values from -6 to 6
- enc_res_weight: bfloat16 [3, 512, 512], P(None, 'chan'), may hold values from -0.15625 to 0.15625
- enc_res_bias: float32 [512], P('chan'), may hold values from -1.75 to 1.75
- enc_mix_weight: bfloat16 [1, 512, 512], P(None, 'chan'), may hold values from -0.25 to 0.25
- enc_mix_bias: float32 [512], P('chan'), may hold values from -1.75 to 1.75
- enc_out_weight: bfloat16 [3, 512, 512], P(None, 'chan'), may hold values from -0.15625 to 0.15625
- enc_out_bias: float32 [512], P('chan'), may hold values from -1.75 to 1.75
- dec_in_weight: bfloat16 [7, 512, 512], P(None, 'chan'), may hold values from -0.09375 to 0.09375
- dec_in_bias: float32 [512], P('chan'), may hold values from -1.75 to 1.75
- dec_res_weight: bfloat16 [3, 512, 512], P(None, 'chan'), may hold values from -0.15625 to 0.15625
- dec_res_bias: float32 [512], P('chan'), may hold values from -1.75 to 1.75
- dec_mix_weight: bfloat16 [1, 512, 512], P(None, 'chan'), may hold values from -0.25 to 0.25
- dec_mix_bias: float32 [512], P('chan'), may hold values from -1.75 to 1.75
- codebook: bfloat16 [2, 512, 1024], P(None, 'chan'), may hold values from -4 to 4
Outputs:
- output: bfloat16 [256, 512, 256], P('dp', 'chan')
- tokens_grad: float32 [256, 512, 256], P('dp', 'chan')
- enc_res_weight_grad: float32 [3, 512, 512], P(None, 'chan')
- enc_res_bias_grad: float32 [512], P('chan')
- enc_mix_weight_grad: float32 [1, 512, 512], P(None, 'chan')
- enc_mix_bias_grad: float32 [512], P('chan')
- enc_out_weight_grad: float32 [3, 512, 512], P(None, 'chan')
- enc_out_bias_grad: float32 [512], P('chan')
- dec_in_weight_grad: float32 [7, 512, 512], P(None, 'chan')
- dec_in_bias_grad: float32 [512], P('chan')
- dec_res_weight_grad: float32 [3, 512, 512], P(None, 'chan')
- dec_res_bias_grad: float32 [512], P('chan')
- dec_mix_weight_grad: float32 [1, 512, 512], P(None, 'chan')
- dec_mix_bias_grad: float32 [512], P('chan')
- codebook_grad: float32 [2, 512, 1024], P(None, 'chan')
The draws below stay inside these ranges and needn't reach their ends.
All inputs are finite; a program needn't handle non-finite values. No bound on the sum of `frame_mask` on one device may be relied on, other than what follows from the above.
Results may differ from the reference program's by a relative error of at most 0.0063.
Values may be sent and summed in bfloat16 or wider, within the bound.
No kernel may reach another device: no remote copies, remote signals or barrier semaphores. Data moves between devices by JAX's collectives and lax.ppermute only.
A program may use at most 192 MiB of HBM per device.

```python
import jax
import jax.numpy as jnp
from jax import lax

D = 512
GROUPS = 2
GW = 256
LEVELS = 2
CODES = 1024
K_RES = 3
K_IN = 7
CLIP_LEN = 256
CLIPS = 256
N_DP = 16


def set_ends(entries, key, smallest, top_value):
    longest = entries.shape.index(max(entries.shape))
    spots = []
    for shift in (0, 1):
        where = [jax.random.randint(jax.random.fold_in(key, axis), (), 0, length) for axis, length in enumerate(entries.shape)]
        where[longest] = (where[longest] + shift) % entries.shape[longest]
        spots.append(tuple(where))
    return entries.at[spots[0]].set(smallest).at[spots[1]].set(top_value)


def steps_of(own_key, dims, split, smallest, high):
    def one(position, shards_of):
        draws = jax.random.uniform(jax.random.fold_in(jax.random.fold_in(own_key, 6), position), (shards_of,), jnp.float32, smallest / len(split), high / len(split))
        return jnp.repeat(jnp.exp(draws), dims[position] // shards_of).reshape((-1,) + (1,) * (len(dims) - position - 1))

    loudness = one(*split[0])
    for cut in split[1:]:
        loudness = loudness * one(*cut)
    return loudness


def bell_draw(rng, dims, deviation, bound, split=(), held_as=jnp.bfloat16):
    values = deviation * jax.random.normal(rng, dims, jnp.float32)
    if split:
        values = values * steps_of(rng, dims, split, -0.22, 0.18)
    return jnp.clip(values, -bound, bound).astype(held_as)


def setup_inputs(seed: int = 0) -> dict:
    arg_keys = jax.random.split(jax.random.key(seed), 19)
    tokens = bell_draw(arg_keys[0], (CLIPS, D, CLIP_LEN), 1.0, 6.0, ((0, 16), (1, 2)))
    lengths = set_ends(jax.random.randint(arg_keys[1], (CLIPS,), CLIP_LEN // 6, CLIP_LEN + 1), jax.random.fold_in(arg_keys[1], 1), CLIP_LEN // 6, CLIP_LEN).astype(jnp.int32)
    frame_mask = set_ends((jax.random.randint(arg_keys[2], (CLIPS, CLIP_LEN), 0, 4) < 3).astype(jnp.int32), jax.random.fold_in(arg_keys[2], 1), 0, 1)
    code_ids = set_ends(jax.random.randint(arg_keys[3], (CLIPS, GROUPS * LEVELS, CLIP_LEN), 0, CODES), jax.random.fold_in(arg_keys[3], 1), 0, CODES - 1).astype(jnp.int32)
    cotangent = bell_draw(arg_keys[4], (CLIPS, D, CLIP_LEN), 1.0, 6.0, ((0, 16), (1, 2)))
    enc_res_weight = bell_draw(arg_keys[5], (K_RES, D, D), (K_RES * D) ** -0.5, 0.15625, ((1, 2),))
    enc_res_bias = bell_draw(arg_keys[6], (D,), 0.3, 1.75, ((0, 2),), jnp.float32)
    enc_mix_weight = bell_draw(arg_keys[7], (1, D, D), D ** -0.5, 0.25, ((1, 2),))
    enc_mix_bias = bell_draw(arg_keys[8], (D,), 0.3, 1.75, ((0, 2),), jnp.float32)
    enc_out_weight = bell_draw(arg_keys[9], (K_RES, D, D), (K_RES * D) ** -0.5, 0.15625, ((1, 2),))
    enc_out_bias = bell_draw(arg_keys[10], (D,), 0.3, 1.75, ((0, 2),), jnp.float32)
    dec_in_weight = bell_draw(arg_keys[11], (K_IN, D, D), (K_IN * D) ** -0.5, 0.09375, ((1, 2),))
    dec_in_bias = bell_draw(arg_keys[12], (D,), 0.3, 1.75, ((0, 2),), jnp.float32)
    dec_res_weight = bell_draw(arg_keys[13], (K_RES, D, D), (K_RES * D) ** -0.5, 0.15625, ((1, 2),))
    dec_res_bias = bell_draw(arg_keys[14], (D,), 0.3, 1.75, ((0, 2),), jnp.float32)
    dec_mix_weight = bell_draw(arg_keys[15], (1, D, D), D ** -0.5, 0.25, ((1, 2),))
    dec_mix_bias = bell_draw(arg_keys[16], (D,), 0.3, 1.75, ((0, 2),), jnp.float32)
    codebook = bell_draw(arg_keys[17], (LEVELS, D, CODES), 0.7, 4.0, ((1, 2),))
    return {"tokens": tokens, "lengths": lengths, "frame_mask": frame_mask, "code_ids": code_ids, "cotangent": cotangent, "enc_res_weight": enc_res_weight, "enc_res_bias": enc_res_bias, "enc_mix_weight": enc_mix_weight, "enc_mix_bias": enc_mix_bias, "enc_out_weight": enc_out_weight, "enc_out_bias": enc_out_bias, "dec_in_weight": dec_in_weight, "dec_in_bias": dec_in_bias, "dec_res_weight": dec_res_weight, "dec_res_bias": dec_res_bias, "dec_mix_weight": dec_mix_weight, "dec_mix_bias": dec_mix_bias, "codebook": codebook}


HIGH = lax.Precision.HIGHEST
BETA = 0.25

@jax.custom_vjp
def low(v):
    return lax.optimization_barrier(v.astype(jnp.bfloat16)).astype(jnp.float32)

@jax.custom_vjp
def low_back(v):
    return v

def low_keep(v):
    return (low(v), None)

def low_pass(kept, grad):
    return (grad,)

def back_keep(v):
    return (v, None)

def back_low(kept, grad):
    return (low(grad),)
low.defvjp(low_keep, low_pass)
low_back.defvjp(back_keep, back_low)

def convolve(source, weight, bias):
    kernel_taps = weight.shape[0]
    margin = kernel_taps // 2
    frames = source.shape[2]
    padded = jnp.pad(source, ((0, 0), (0, 0), (margin, margin)))
    result = jnp.zeros((source.shape[0], weight.shape[1], frames), jnp.float32) + bias[:, None]
    for offset in range(kernel_taps):
        result = result + jnp.einsum('ed,cdl->cel', weight[offset], padded[:, :, offset:offset + frames], precision=HIGH)
    return result

def layer(source, inside, weight, bias):
    return low_back(convolve(low(inside * source), weight, bias))

def encode(feats, inside, params):
    start = inside * feats
    enc_first = layer(jax.nn.elu(start), inside, params[0], params[1])
    enc_second = layer(jax.nn.elu(enc_first), inside, params[2], params[3])
    hidden = inside * (start + enc_second)
    return layer(jax.nn.elu(hidden), inside, params[4], params[5])

def lookup(one_hot, level_index, table):
    pieces = []
    for group_index in range(GROUPS):
        pieces.append(jnp.einsum('ckl,dk->cdl', one_hot[:, group_index * LEVELS + level_index], table[level_index][group_index * GW:(group_index + 1) * GW, :], precision=HIGH))
    return jnp.concatenate(pieces, axis=1)

def reference(tokens, lengths, frame_mask, code_ids, cotangent, enc_res_weight, enc_res_bias, enc_mix_weight, enc_mix_bias, enc_out_weight, enc_out_bias, dec_in_weight, dec_in_bias, dec_res_weight, dec_res_bias, dec_mix_weight, dec_mix_bias, codebook):
    params = tuple((a.astype(jnp.float32) for a in (enc_res_weight, enc_res_bias, enc_mix_weight, enc_mix_bias, enc_out_weight, enc_out_bias, dec_in_weight, dec_in_bias, dec_res_weight, dec_res_bias, dec_mix_weight, dec_mix_bias)))
    table = codebook.astype(jnp.float32)
    per_group = CLIPS // N_DP
    positions = jnp.arange(CLIP_LEN, dtype=jnp.int32)
    code_range = jnp.arange(CODES, dtype=jnp.int32)

    def group_step(totals, item):
        feats, clip_lengths, mask_rows, ids, cot = item
        feats = feats.astype(jnp.float32)
        cot = cot.astype(jnp.float32)
        inside = (positions[None, :] < clip_lengths[:, None]).astype(jnp.float32)[:, None, :]
        counted = inside * mask_rows.astype(jnp.float32)[:, None, :]
        one_hot = (ids[:, :, None, :] == code_range[None, None, :, None]).astype(jnp.float32)
        latent_const = encode(feats, inside, params)
        first_const = lookup(one_hot, 0, table)
        quant_const = first_const + lookup(one_hot, 1, table)

        def loss_fn(weights, feats_in, books):
            latent = encode(feats_in, inside, weights)
            quant_first = low_back(lookup(one_hot, 0, books))
            quant_second = low_back(lookup(one_hot, 1, books))
            through = quant_const + (latent - latent_const)
            dec_first = layer(through, inside, weights[6], weights[7])
            dec_second = layer(jax.nn.elu(dec_first), inside, weights[8], weights[9])
            dec_third = layer(jax.nn.elu(dec_second), inside, weights[10], weights[11])
            result = inside * (dec_first + dec_third)
            book_loss = jnp.sum(counted * ((latent_const - quant_first) ** 2 + (latent_const - first_const - quant_second) ** 2))
            commit = BETA * jnp.sum(counted * (latent - quant_const) ** 2)
            return (jnp.sum(cot * result) + book_loss + commit, result)
        loss_value, pull, result = jax.vjp(loss_fn, params, feats, table, has_aux=True)
        weight_grads, feats_grad, book_grad = pull(jnp.float32(1.0))
        totals = tuple((a + b for a, b in zip(totals, weight_grads + (book_grad,))))
        return (totals, (result.astype(jnp.bfloat16), feats_grad))
    shaped = lambda a: a.reshape((N_DP, per_group) + a.shape[1:])
    start_totals = tuple((jnp.zeros(a.shape, jnp.float32) for a in params + (table,)))
    totals, (results, feats_grads) = lax.scan(group_step, start_totals, (shaped(tokens), shaped(lengths), shaped(frame_mask), shaped(code_ids), shaped(cotangent)))
    output = results.reshape((CLIPS, D, CLIP_LEN))
    tokens_grad = feats_grads.reshape((CLIPS, D, CLIP_LEN))
    return (output, tokens_grad, totals[0], totals[1], totals[2], totals[3], totals[4], totals[5], totals[6], totals[7], totals[8], totals[9], totals[10], totals[11], totals[12])
```

```python
import functools

import jax
import jax.numpy as jnp
from jax import lax
from jax.experimental import pallas as pl
from jax.experimental.pallas import tpu as pltpu
from jax.sharding import PartitionSpec as P

LEVELS = 2
GW = 256
BETA = 0.25
F32 = jnp.float32
BF16 = jnp.bfloat16
VMEM_LIMIT = 56 * 1024 * 1024

ANY = pl.BlockSpec(memory_space=pl.ANY)
VMEM = pl.BlockSpec(memory_space=pltpu.VMEM)
SMEM = pl.BlockSpec(memory_space=pltpu.SMEM)


def elu(value):
    return jnp.where(value > 0, value, jnp.exp(jnp.minimum(value, 0.0)) - 1.0)


def slope_of(activated):
    act = activated.astype(F32)
    return jnp.where(act > 0, 1.0, 1.0 + act)


def shifted(value, step):
    if step == 0:
        return value
    edge = jnp.zeros((value.shape[0], abs(step)), value.dtype)
    if step > 0:
        return jnp.concatenate([value[:, step:], edge], axis=1)
    return jnp.concatenate([edge, value[:, :step]], axis=1)


def lanes(blocks):
    return blocks[0] if len(blocks) == 1 else jnp.concatenate(blocks, axis=1)


class Copies:
    def __init__(self, sems):
        self.sems = sems
        self.used = 0
        self.open = []

    def start(self, source, target):
        copy = pltpu.make_async_copy(source, target, self.sems.at[self.used])
        self.used += 1
        copy.start()
        return copy

    def out(self, source, target):
        self.open.append(self.start(source, target))

    def finish(self):
        for copy in self.open:
            copy.wait()


def wait_all(copies):
    for copy in copies:
        copy.wait()


class Parts:
    def __init__(self, arrays, starts, clip_start=None):
        self.arrays = arrays
        self.starts = starts
        self.clip_start = clip_start

    def load(self, copies, refs, meta, scratch, clips=None):
        begun = []
        for number, (ref, start) in enumerate(zip(refs, self.starts)):
            rows = ref.shape[1]
            row = 0 if start is None else pl.multiple_of(meta[start], 16)
            source = ref
            if clips is not None and ref.shape[0] != clips:
                source = ref.at[pl.ds(meta[self.clip_start], clips)]
            begun.append(copies.start(source, scratch.at[:, pl.ds(row, rows), :]))
        return begun


def kernel_call(body, outs, operands, scratch, copies, flops):
    arrays = [array for array, _ in operands]
    specs = [spec for _, spec in operands]
    moved = sum(a.size * a.dtype.itemsize for a in arrays)
    moved += sum(o.size * o.dtype.itemsize for o in outs)
    return pl.pallas_call(
        body,
        out_shape=tuple(outs),
        in_specs=specs,
        out_specs=tuple(ANY for _ in outs),
        scratch_shapes=list(scratch) + [pltpu.SemaphoreType.DMA((copies,))],
        compiler_params=pltpu.CompilerParams(vmem_limit_bytes=VMEM_LIMIT),
        cost_estimate=pl.CostEstimate(
            flops=int(flops), bytes_accessed=int(moved), transcendentals=0
        ),
    )(*arrays)


def struct(shape, dtype):
    return jax.ShapeDtypeStruct(shape, dtype)


def groups_of(clips):
    per = min(4, clips)
    return [tuple(range(first, first + per)) for first in range(0, clips, per)]


def span(clip_numbers, frames):
    return slice(clip_numbers[0] * frames, (clip_numbers[-1] + 1) * frames)


def mask_of(len_ref, clip_numbers, frames):
    position = lax.broadcasted_iota(jnp.int32, (1, frames), 1)
    return lanes([(position < len_ref[clip]).astype(F32) for clip in clip_numbers])


def conv_forward(weight_ref, source_ref, clip_numbers, frames):
    taps = weight_ref.shape[0]
    blocks = [source_ref[:, span((clip,), frames)] for clip in clip_numbers]
    total = None
    for tap in range(taps):
        moved = lanes([shifted(block, tap - taps // 2) for block in blocks])
        term = jnp.dot(weight_ref[tap], moved, preferred_element_type=F32)
        total = term if total is None else total + term
    return total


def conv_backward(weight_ref, grad_ref, clip_numbers, frames):
    taps = weight_ref.shape[0]
    blocks = [grad_ref[:, span((clip,), frames)] for clip in clip_numbers]
    total = None
    for tap in range(taps):
        moved = lanes([shifted(block, taps // 2 - tap) for block in blocks])
        term = lax.dot_general(
            weight_ref[tap], moved, (((0,), (0,)), ((), ())), preferred_element_type=F32
        )
        total = term if total is None else total + term
    return total


def encoder_forward(meta, lens, tokens, weights, bias, clips, frames, dim):
    counts = [len(tokens.arrays)] + [len(w.arrays) for w in weights]

    def body(meta_ref, len_ref, bias_ref, *refs):
        take = iter(refs)
        part_refs = [[next(take) for _ in range(count)] for count in counts]
        u0, u1, u2, latent = (next(take) for _ in range(4))
        tok, w0, w1, w2, s0, s1, s2, s3, sems = take
        copies = Copies(sems)
        loads = [weights[0].load(copies, part_refs[1], meta_ref, w0)]
        loads.append(tokens.load(copies, part_refs[0], meta_ref, tok, clips))
        loads.append(weights[1].load(copies, part_refs[2], meta_ref, w1))
        loads.append(weights[2].load(copies, part_refs[3], meta_ref, w2))
        wait_all(loads[1])
        for clip in range(clips):
            inside = mask_of(len_ref, (clip,), frames)
            s0[:, span((clip,), frames)] = elu(inside * tok[clip].astype(F32)).astype(BF16)
        copies.out(s0, u0)
        wait_all(loads[0])
        for number, group in enumerate(groups_of(clips)):
            here = span(group, frames)
            inside = mask_of(len_ref, group, frames)
            first = conv_forward(w0, s0, group, frames) + bias_ref[:, 0:1]
            s1[:, here] = (inside * elu(first)).astype(BF16)
            if number == 0:
                wait_all(loads[2])
            second = conv_forward(w1, s1, group, frames) + bias_ref[:, 1:2]
            start = lanes([tok[clip].astype(F32) for clip in group])
            s2[:, here] = elu(inside * (start + second)).astype(BF16)
            if number == 0:
                wait_all(loads[3])
            s3[:, here] = conv_forward(w2, s2, group, frames) + bias_ref[:, 2:3]
        copies.out(s1, u1)
        copies.out(s2, u2)
        copies.out(s3, latent)
        copies.finish()

    wide = (dim, clips * frames)
    operands = [(meta, SMEM), (lens, SMEM), (bias, VMEM)]
    operands += [(array, ANY) for part in [tokens] + list(weights) for array in part.arrays]
    taps = [w.arrays[0].shape[0] for w in weights]
    return kernel_call(
        body,
        [struct(wide, BF16)] * 3 + [struct(wide, F32)],
        operands,
        [pltpu.VMEM((clips, dim, frames), BF16)]
        + [pltpu.VMEM((count, dim, dim), BF16) for count in taps]
        + [pltpu.VMEM(wide, BF16)] * 3
        + [pltpu.VMEM(wide, F32)],
        sum(counts) + 4,
        2 * sum(taps) * dim * dim * clips * frames,
    )


def quantizer(meta, lens, ids, mask, codebook, latent, clips, frames, dim):
    count = len(codebook.arrays)
    codes = codebook.arrays[0].shape[2]
    wide = (dim, clips * frames)

    def body(meta_ref, len_ref, ids_ref, mask_ref, *refs):
        take = iter(refs)
        book_refs = [next(take) for _ in range(count)]
        latent_ref, u3, extra, grads = (next(take) for _ in range(4))
        book, lat, hot0, hot1, s3, sx, sg, sems = take
        copies = Copies(sems)
        loads = codebook.load(copies, book_refs, meta_ref, book)
        loaded = copies.start(latent_ref, lat)
        every = tuple(range(clips))
        inside = mask_of(len_ref, every, frames)
        counted = inside * lanes([mask_ref[clip : clip + 1, :].astype(F32) for clip in every])
        number = lax.broadcasted_iota(jnp.int32, (codes, frames), 0).astype(jnp.int16)
        one = jnp.ones((), BF16)
        zero = jnp.zeros((), BF16)
        for group in range(dim // GW):
            rows = slice(group * GW, (group + 1) * GW)
            for level, hot in ((0, hot0), (1, hot1)):
                for clip in every:
                    at = clip * LEVELS * (dim // GW) + group * LEVELS + level
                    row = ids_ref[at : at + 1, :].astype(jnp.int16)
                    hot[:, span((clip,), frames)] = jnp.where(number == row, one, zero)
            if group == 0:
                wait_all(loads)
            first = jnp.dot(book[0, rows, :], hot0[...], preferred_element_type=F32)
            second = jnp.dot(book[1, rows, :], hot1[...], preferred_element_type=F32)
            if group == 0:
                loaded.wait()
            value = lat[rows, :]
            quantized = first + second
            s3[rows, :] = (inside * quantized).astype(BF16)
            sx[rows, :] = (2.0 * BETA) * counted * (value - quantized)
            grad0 = (2.0 * counted * (first - value)).astype(BF16)
            grad1 = (2.0 * counted * (second - value + first)).astype(BF16)
            for level, hot, grad in ((0, hot0, grad0), (1, hot1, grad1)):
                sg[rows, level * codes : (level + 1) * codes] = lax.dot_general(
                    grad, hot[...], (((1,), (1,)), ((), ())), preferred_element_type=F32
                ).astype(BF16)
        copies.out(s3, u3)
        copies.out(sx, extra)
        copies.out(sg, grads)
        copies.finish()

    operands = [(meta, SMEM), (lens, SMEM), (ids, VMEM), (mask, VMEM)]
    operands += [(array, ANY) for array in codebook.arrays] + [(latent, ANY)]
    return kernel_call(
        body,
        [struct(wide, BF16), struct(wide, F32), struct((dim, LEVELS * codes), BF16)],
        operands,
        [
            pltpu.VMEM((LEVELS, dim, codes), BF16),
            pltpu.VMEM(wide, F32),
            pltpu.VMEM((codes, clips * frames), BF16),
            pltpu.VMEM((codes, clips * frames), BF16),
            pltpu.VMEM(wide, BF16),
            pltpu.VMEM(wide, F32),
            pltpu.VMEM((dim, LEVELS * codes), BF16),
        ],
        count + 4,
        4 * LEVELS * dim * codes * clips * frames,
    )


def decoder_forward(meta, lens, u3, weights, bias, out_rows, clips, frames, dim):
    counts = [len(w.arrays) for w in weights]
    wide = (dim, clips * frames)

    def body(meta_ref, len_ref, bias_ref, u3_ref, *refs):
        take = iter(refs)
        part_refs = [[next(take) for _ in range(count)] for count in counts]
        u4, u5 = next(take), next(take)
        out_refs = [next(take) for _ in out_rows]
        w3, w4, w5, s3, s4, s5, sf, so, sems = take
        copies = Copies(sems)
        loaded = copies.start(u3_ref, s3)
        loads = [
            weight.load(copies, refs_of, meta_ref, scratch)
            for weight, refs_of, scratch in zip(weights, part_refs, (w3, w4, w5))
        ]
        loaded.wait()
        wait_all(loads[0])
        for number, group in enumerate(groups_of(clips)):
            here = span(group, frames)
            inside = mask_of(len_ref, group, frames)
            first = conv_forward(w3, s3, group, frames) + bias_ref[:, 3:4]
            sf[:, here] = first
            s4[:, here] = (inside * elu(first)).astype(BF16)
            if number == 0:
                wait_all(loads[1])
            second = conv_forward(w4, s4, group, frames) + bias_ref[:, 4:5]
            s5[:, here] = (inside * elu(second)).astype(BF16)
            if number == 0:
                wait_all(loads[2])
            third = conv_forward(w5, s5, group, frames) + bias_ref[:, 5:6]
            result = (inside * (sf[:, here] + third)).astype(BF16)
            for place, clip in enumerate(group):
                so[clip] = result[:, place * frames : (place + 1) * frames]
        copies.out(s4, u4)
        copies.out(s5, u5)
        for ref, (start, rows) in zip(out_refs, out_rows):
            row = 0 if start is None else pl.multiple_of(meta_ref[start], 16)
            copies.out(so.at[:, pl.ds(row, rows), :], ref)
        copies.finish()

    operands = [(meta, SMEM), (lens, SMEM), (bias, VMEM), (u3, ANY)]
    operands += [(array, ANY) for part in weights for array in part.arrays]
    taps = [w.arrays[0].shape[0] for w in weights]
    return kernel_call(
        body,
        [struct(wide, BF16)] * 2
        + [struct((clips, rows, frames), BF16) for _, rows in out_rows],
        operands,
        [pltpu.VMEM((count, dim, dim), BF16) for count in taps]
        + [pltpu.VMEM(wide, BF16)] * 3
        + [pltpu.VMEM(wide, F32), pltpu.VMEM((clips, dim, frames), BF16)],
        sum(counts) + 3 + len(out_rows),
        2 * sum(taps) * dim * dim * clips * frames,
    )


def decoder_backward(meta, lens, cotangent, u4, u5, weights, clips, frames, dim):
    counts = [len(cotangent.arrays)] + [len(w.arrays) for w in weights]
    wide = (dim, clips * frames)

    def body(meta_ref, len_ref, u4_ref, u5_ref, *refs):
        take = iter(refs)
        part_refs = [[next(take) for _ in range(count)] for count in counts]
        g5, g4, g3 = (next(take) for _ in range(3))
        cot, w4, w5, s4, s5, d5, d4, d3, sems = take
        copies = Copies(sems)
        loads = [
            cotangent.load(copies, part_refs[0], meta_ref, cot, clips),
            weights[1].load(copies, part_refs[2], meta_ref, w5),
            [copies.start(u5_ref, s5)],
            weights[0].load(copies, part_refs[1], meta_ref, w4) + [copies.start(u4_ref, s4)],
        ]
        wait_all(loads[0])
        for clip in range(clips):
            inside = mask_of(len_ref, (clip,), frames)
            d5[:, span((clip,), frames)] = (inside * cot[clip].astype(F32)).astype(BF16)
        copies.out(d5, g5)
        wait_all(loads[1])
        wait_all(loads[2])
        for number, group in enumerate(groups_of(clips)):
            here = span(group, frames)
            inside = mask_of(len_ref, group, frames)
            back = conv_backward(w5, d5, group, frames)
            d4[:, here] = (back * inside * slope_of(s5[:, here])).astype(BF16)
            if number == 0:
                wait_all(loads[3])
            back = conv_backward(w4, d4, group, frames)
            total = d5[:, here].astype(F32) + back * inside * slope_of(s4[:, here])
            d3[:, here] = total.astype(BF16)
        copies.out(d4, g4)
        copies.out(d3, g3)
        copies.finish()

    operands = [(meta, SMEM), (lens, SMEM), (u4, ANY), (u5, ANY)]
    operands += [(array, ANY) for part in [cotangent] + list(weights) for array in part.arrays]
    taps = [w.arrays[0].shape[0] for w in weights]
    return kernel_call(
        body,
        [struct(wide, BF16)] * 3,
        operands,
        [pltpu.VMEM((clips, dim, frames), BF16)]
        + [pltpu.VMEM((count, dim, dim), BF16) for count in taps]
        + [pltpu.VMEM(wide, BF16)] * 5,
        sum(counts) + 5,
        2 * sum(taps) * dim * dim * clips * frames,
    )


def weight_grads(layers, clips, frames, dim):
    wide = (dim, clips * frames)
    offsets = []
    columns = 0
    for _, _, taps in layers:
        offsets.append(columns)
        columns += taps * dim + 128

    def body(*refs):
        take = iter(refs)
        in_refs = [(next(take), next(take)) for _ in layers]
        grads = next(take)
        scratch = [(next(take), next(take)) for _ in layers]
        work, result, sems = take
        copies = Copies(sems)
        loads = [
            [copies.start(ref, where) for ref, where in zip(pair, places)]
            for pair, places in zip(in_refs, scratch)
        ]
        for (_, _, taps), begun, (g, u), offset in zip(layers, loads, scratch, offsets):
            wait_all(begun)
            for tap in range(taps):
                step = taps // 2 - tap
                if step == 0:
                    left = g[...]
                else:
                    for clip in range(clips):
                        at = span((clip,), frames)
                        work[:, at] = shifted(g[:, at], step)
                    left = work[...]
                at = slice(offset + tap * dim, offset + (tap + 1) * dim)
                result[:, at] = lax.dot_general(
                    left, u[...], (((1,), (1,)), ((), ())), preferred_element_type=F32
                ).astype(BF16)
                copies.out(result.at[:, at], grads.at[:, at])
            total = jnp.sum(g[...].astype(F32), axis=1, keepdims=True)
            at = slice(offset + taps * dim, offset + taps * dim + 128)
            result[:, at] = jnp.broadcast_to(total, (dim, 128)).astype(BF16)
            copies.out(result.at[:, at], grads.at[:, at])
        copies.finish()

    operands = [(array, ANY) for g, u, _ in layers for array in (g, u)]
    taps = sum(count for _, _, count in layers)
    return kernel_call(
        body,
        [struct((dim, columns), BF16)],
        operands,
        [pltpu.VMEM(wide, BF16)] * (2 * len(layers))
        + [pltpu.VMEM(wide, BF16), pltpu.VMEM((dim, columns), BF16)],
        2 * len(layers) + taps + len(layers),
        2 * taps * dim * dim * clips * frames,
    )[0]


def latent_backward(meta, lens, g3, weight, extra, clips, frames, dim):
    count = len(weight.arrays)
    wide = (dim, clips * frames)

    def body(meta_ref, len_ref, g3_ref, extra_ref, *refs):
        take = iter(refs)
        part_refs = [next(take) for _ in range(count)]
        g2 = next(take)
        w3, s3, sx, s2, sems = take
        copies = Copies(sems)
        loads = [copies.start(g3_ref, s3)] + weight.load(copies, part_refs, meta_ref, w3)
        later = copies.start(extra_ref, sx)
        wait_all(loads)
        for number, group in enumerate(groups_of(clips)):
            here = span(group, frames)
            inside = mask_of(len_ref, group, frames)
            back = conv_backward(w3, s3, group, frames)
            if number == 0:
                later.wait()
            s2[:, here] = (back * inside + sx[:, here]).astype(BF16)
        copies.out(s2, g2)
        copies.finish()

    taps = weight.arrays[0].shape[0]
    operands = [(meta, SMEM), (lens, SMEM), (g3, ANY), (extra, ANY)]
    operands += [(array, ANY) for array in weight.arrays]
    return kernel_call(
        body,
        [struct(wide, BF16)],
        operands,
        [
            pltpu.VMEM((taps, dim, dim), BF16),
            pltpu.VMEM(wide, BF16),
            pltpu.VMEM(wide, F32),
            pltpu.VMEM(wide, BF16),
        ],
        count + 3,
        2 * taps * dim * dim * clips * frames,
    )[0]


def encoder_backward(meta, lens, g2, u2, u1, weights, clips, frames, dim):
    counts = [len(w.arrays) for w in weights]
    wide = (dim, clips * frames)

    def body(meta_ref, len_ref, g2_ref, u2_ref, u1_ref, *refs):
        take = iter(refs)
        part_refs = [[next(take) for _ in range(count)] for count in counts]
        gh, g1, g0 = (next(take) for _ in range(3))
        w1, w2, s1, s2, d2, dh, d1, d0, sems = take
        copies = Copies(sems)
        loads = [copies.start(g2_ref, d2), copies.start(u2_ref, s2)]
        loads += weights[1].load(copies, part_refs[1], meta_ref, w2)
        later = weights[0].load(copies, part_refs[0], meta_ref, w1)
        later.append(copies.start(u1_ref, s1))
        wait_all(loads)
        for number, group in enumerate(groups_of(clips)):
            here = span(group, frames)
            inside = mask_of(len_ref, group, frames)
            back = conv_backward(w2, d2, group, frames)
            hidden = back * inside * slope_of(s2[:, here])
            dh[:, here] = hidden
            d1[:, here] = hidden.astype(BF16)
            if number == 0:
                wait_all(later)
            back = conv_backward(w1, d1, group, frames)
            d0[:, here] = (back * inside * slope_of(s1[:, here])).astype(BF16)
        copies.out(dh, gh)
        copies.out(d1, g1)
        copies.out(d0, g0)
        copies.finish()

    operands = [(meta, SMEM), (lens, SMEM), (g2, ANY), (u2, ANY), (u1, ANY)]
    operands += [(array, ANY) for part in weights for array in part.arrays]
    taps = [w.arrays[0].shape[0] for w in weights]
    return kernel_call(
        body,
        [struct(wide, F32), struct(wide, BF16), struct(wide, BF16)],
        operands,
        [pltpu.VMEM((count, dim, dim), BF16) for count in taps]
        + [pltpu.VMEM(wide, BF16)] * 3
        + [pltpu.VMEM(wide, F32)]
        + [pltpu.VMEM(wide, BF16)] * 2,
        sum(counts) + 6,
        2 * sum(taps) * dim * dim * clips * frames,
    )


def tokens_backward(meta, lens, g0, u0, gh, weight, out_rows, clips, frames, dim):
    count = len(weight.arrays)
    wide = (dim, clips * frames)

    def body(meta_ref, len_ref, g0_ref, u0_ref, gh_ref, *refs):
        take = iter(refs)
        part_refs = [next(take) for _ in range(count)]
        out_refs = [next(take) for _ in out_rows]
        w0, d0, s0, dh, so, sems = take
        copies = Copies(sems)
        loads = [copies.start(g0_ref, d0)] + weight.load(copies, part_refs, meta_ref, w0)
        later = [copies.start(u0_ref, s0), copies.start(gh_ref, dh)]
        wait_all(loads)
        for number, group in enumerate(groups_of(clips)):
            here = span(group, frames)
            inside = mask_of(len_ref, group, frames)
            back = conv_backward(w0, d0, group, frames)
            if number == 0:
                wait_all(later)
            total = inside * (dh[:, here] + back * inside * slope_of(s0[:, here]))
            total = total.astype(BF16)
            for place, clip in enumerate(group):
                so[clip] = total[:, place * frames : (place + 1) * frames]
        for ref, (start, rows) in zip(out_refs, out_rows):
            row = 0 if start is None else pl.multiple_of(meta_ref[start], 16)
            copies.out(so.at[:, pl.ds(row, rows), :], ref)
        copies.finish()

    taps = weight.arrays[0].shape[0]
    operands = [(meta, SMEM), (lens, SMEM), (g0, ANY), (u0, ANY), (gh, ANY)]
    operands += [(array, ANY) for array in weight.arrays]
    return kernel_call(
        body,
        [struct((clips, rows, frames), BF16) for _, rows in out_rows],
        operands,
        [
            pltpu.VMEM((taps, dim, dim), BF16),
            pltpu.VMEM(wide, BF16),
            pltpu.VMEM(wide, BF16),
            pltpu.VMEM(wide, F32),
            pltpu.VMEM((clips, dim, frames), BF16),
        ],
        count + 3 + len(out_rows),
        2 * taps * dim * dim * clips * frames,
    )


class Pairs:
    BITS = {"core": 1, "x": 2, "zl": 4, "zh": 8}

    def __init__(self):
        self.chan = lax.axis_index("chan")
        self.dp = lax.axis_index("dp")
        self.core = self.dp & 1

    def bit(self, name):
        if name == "chan":
            return self.chan
        return (self.dp & self.BITS[name]) // self.BITS[name]

    def swap(self, value, name):
        if name == "chan":
            return lax.ppermute(value, "chan", [(0, 1), (1, 0)])
        mask = self.BITS[name]
        return lax.ppermute(value, "dp", [(i, i ^ mask) for i in range(16)])

    def meta(self, clips, rows):
        other = (1 - self.chan) * rows
        quarter = rows // 2
        return jnp.stack(
            [
                self.chan * clips,
                self.chan * rows,
                other,
                other + self.core * quarter,
                other + (1 - self.core) * quarter,
            ]
        ).astype(jnp.int32)

    def share(self, own):
        quarter = own.shape[1] // 2
        mine = lax.dynamic_slice_in_dim(own, self.core * quarter, quarter, 1)
        near = self.swap(mine, "chan")
        return Parts((own, near, self.swap(near, "core")), (1, 3, 4))

    def biases(self, own):
        came = self.swap(own, "chan")
        first = self.chan == 0
        return jnp.concatenate([jnp.where(first, own, came), jnp.where(first, came, own)])

    def clips_in(self, own, clips):
        sent = lax.dynamic_slice_in_dim(own, (1 - self.chan) * clips, clips, 0)
        return Parts((own, self.swap(sent, "chan")), (1, 2), 0)

    def clips_out(self, own, other, dtype):
        came = self.swap(other, "chan")
        own, came = own.astype(dtype), came.astype(dtype)
        first = self.chan == 0
        return jnp.concatenate([jnp.where(first, own, came), jnp.where(first, came, own)])

    def out_rows(self, rows):
        return ((1, rows), (2, rows))

    def reduce(self, grads, order):
        names = ["chan", "core", "x", "zh", "zl"]
        columns = grads.shape[1]
        value = grads.reshape((2,) * 5 + (grads.shape[0] // 32, columns))
        for name in ("core",) + order:
            axis = names.index(name)
            bit = self.bit(name)
            own = lax.dynamic_index_in_dim(value, bit, axis, keepdims=False)
            sent = lax.dynamic_index_in_dim(value, 1 - bit, axis, keepdims=False)
            came = self.swap(sent, name)
            value = (own.astype(F32) + came.astype(F32)).astype(BF16)
            names.remove(name)
        full = ["core", "x", "zh", "zl"]
        for name in tuple(n for n in reversed(order) if n != "chan") + ("core",):
            came = self.swap(value, name)
            names = [n for n in full if n in names or n == name]
            axis = names.index(name)
            first = self.bit(name) == 0
            value = jnp.stack(
                [jnp.where(first, value, came), jnp.where(first, came, value)], axis
            )
        return value.reshape((grads.shape[0] // 2, columns))


class Plain:
    def __init__(self):
        self.chan = lax.axis_index("chan")

    def meta(self, clips, rows):
        return jnp.zeros((5,), jnp.int32)

    def share(self, own):
        return Parts((lax.all_gather(own, "chan", axis=1, tiled=True),), (None,))

    def biases(self, own):
        return lax.all_gather(own, "chan", axis=0, tiled=True)

    def clips_in(self, own, clips):
        return Parts((lax.all_to_all(own, "chan", 0, 1, tiled=True),), (None,))

    def clips_out(self, own, dtype):
        return lax.all_to_all(own, "chan", 1, 0, tiled=True).astype(dtype)

    def out_rows(self, rows):
        return ((None, rows * lax.axis_size("chan")),)

    def reduce(self, grads, order):
        part = lax.psum_scatter(grads.astype(F32), "chan", scatter_dimension=0, tiled=True)
        return lax.psum(part, "dp")


def on_device(
    paired,
    tokens,
    lengths,
    frame_mask,
    code_ids,
    cotangent,
    enc_res_weight,
    enc_res_bias,
    enc_mix_weight,
    enc_mix_bias,
    enc_out_weight,
    enc_out_bias,
    dec_in_weight,
    dec_in_bias,
    dec_res_weight,
    dec_res_bias,
    dec_mix_weight,
    dec_mix_bias,
    codebook,
):
    links = Pairs() if paired else Plain()
    rows = tokens.shape[1]
    frames = tokens.shape[2]
    chan = lax.axis_size("chan")
    dim = rows * chan
    clips = tokens.shape[0] // chan
    sizes = (clips, frames, dim)
    meta = links.meta(clips, rows)

    def mine(array):
        return lax.dynamic_slice_in_dim(array, links.chan * clips, clips, 0)

    lens = mine(lengths)
    mask = mine(frame_mask)
    ids = mine(code_ids).reshape(-1, frames)
    w0 = links.share(enc_res_weight)
    tok = links.clips_in(tokens, clips)
    biases = (enc_res_bias, enc_mix_bias, enc_out_bias, dec_in_bias, dec_res_bias, dec_mix_bias)
    bias = jnp.stack(biases + (jnp.zeros_like(enc_res_bias),) * 2, axis=1)
    bias = links.biases(bias)
    w1 = links.share(enc_mix_weight)
    w2 = links.share(enc_out_weight)
    book = links.share(codebook)
    w3 = links.share(dec_in_weight)
    w4 = links.share(dec_res_weight)
    w5 = links.share(dec_mix_weight)
    cot = links.clips_in(cotangent, clips)

    u0, u1, u2, latent = encoder_forward(meta, lens, tok, (w0, w1, w2), bias, *sizes)
    u3, extra, book_grad = quantizer(meta, lens, ids, mask, book, latent, *sizes)
    out_rows = links.out_rows(rows)
    u4, u5, *outs = decoder_forward(meta, lens, u3, (w3, w4, w5), bias, out_rows, *sizes)
    output = links.clips_out(*outs, BF16)
    g5, g4, g3 = decoder_backward(meta, lens, cot, u4, u5, (w4, w5), *sizes)
    grads3 = weight_grads([(g3, u3, w3.arrays[0].shape[0])], *sizes)
    grads45 = weight_grads(
        [(g4, u4, w4.arrays[0].shape[0]), (g5, u5, w5.arrays[0].shape[0])], *sizes
    )
    g2 = latent_backward(meta, lens, g3, w3, extra, *sizes)
    grads2 = weight_grads([(g2, u2, w2.arrays[0].shape[0])], *sizes)
    gh, g1, g0 = encoder_backward(meta, lens, g2, u2, u1, (w1, w2), *sizes)
    grads01 = weight_grads(
        [(g0, u0, w0.arrays[0].shape[0]), (g1, u1, w1.arrays[0].shape[0])], *sizes
    )
    outs = tokens_backward(meta, lens, g0, u0, gh, w0, out_rows, *sizes)
    tokens_grad = links.clips_out(*outs, F32)

    yx = ("chan", "x", "zl", "zh")
    zy = ("zl", "zh", "chan", "x")
    xy = ("x", "chan", "zl", "zh")
    books = links.reduce(book_grad, zy)
    sum3 = links.reduce(grads3, xy)
    sum45 = links.reduce(grads45, zy)
    sum2 = links.reduce(grads2, xy)
    sum01 = links.reduce(grads01, yx)

    def unpack(total, weight, offset):
        taps = weight.shape[0]
        block = total[:, offset : offset + taps * dim].reshape(-1, taps, dim)
        end = offset + taps * dim
        return (
            jnp.transpose(block, (1, 0, 2)).astype(F32),
            total[:, end].astype(F32),
            end + 128,
        )

    res_w, res_b, at = unpack(sum01, enc_res_weight, 0)
    mix_w, mix_b, _ = unpack(sum01, enc_mix_weight, at)
    out_w, out_b, _ = unpack(sum2, enc_out_weight, 0)
    din_w, din_b, _ = unpack(sum3, dec_in_weight, 0)
    dres_w, dres_b, at = unpack(sum45, dec_res_weight, 0)
    dmix_w, dmix_b, _ = unpack(sum45, dec_mix_weight, at)
    books = books.reshape(rows, LEVELS, -1).transpose(1, 0, 2).astype(F32)
    return (
        output,
        tokens_grad,
        res_w,
        res_b,
        mix_w,
        mix_b,
        out_w,
        out_b,
        din_w,
        din_b,
        dres_w,
        dres_b,
        dmix_w,
        dmix_b,
        books,
    )


def solution(mesh):
    paired = mesh.shape["chan"] == 2 and mesh.shape["dp"] == 16
    weight = P(None, "chan", None)
    vector = P("chan")
    clip_rows = P("dp", "chan", None)
    in_specs = (
        (clip_rows, P("dp"), P("dp", None), P("dp", None, None), clip_rows)
        + (weight, vector) * 6
        + (weight,)
    )
    out_specs = (clip_rows, clip_rows) + (weight, vector) * 6 + (weight,)
    return jax.shard_map(
        functools.partial(on_device, paired),
        mesh=mesh,
        in_specs=in_specs,
        out_specs=out_specs,
        check_vma=False,
    )
```

```python
import functools
import types

import jax
import jax.numpy as jnp
from jax import lax
from jax.experimental import pallas as pl
from jax.experimental.pallas import tpu as pltpu
from jax.sharding import PartitionSpec as P

LEVELS = 2
GW = 256
BETA = 0.25
F32 = jnp.float32
BF16 = jnp.bfloat16
MIB = 1024 * 1024
LIMIT = 40 * MIB

ANY = pl.BlockSpec(memory_space=pl.ANY)
VMEM = pl.BlockSpec(memory_space=pltpu.VMEM)
SMEM = pl.BlockSpec(memory_space=pltpu.SMEM)


def elu(value):
    return jnp.where(value > 0, value, jnp.exp(jnp.minimum(value, 0.0)) - 1.0)


def slope_of(activated):
    act = activated.astype(F32)
    return jnp.where(act > 0, 1.0, 1.0 + act)


def shifted(value, step):
    if step == 0:
        return value
    edge = jnp.zeros((value.shape[0], abs(step)), value.dtype)
    if step > 0:
        return jnp.concatenate([value[:, step:], edge], axis=1)
    return jnp.concatenate([edge, value[:, :step]], axis=1)


def lanes(blocks):
    return blocks[0] if len(blocks) == 1 else jnp.concatenate(blocks, axis=1)


def tie(value, *earlier):
    earlier = [array for array in earlier if array is not None]
    if not earlier:
        return value
    return lax.optimization_barrier((value, tuple(earlier)))[0]


def struct(shape, dtype):
    return jax.ShapeDtypeStruct(shape, dtype)


class Copies:
    def __init__(self, sems):
        self.sems = sems
        self.used = 0
        self.open = []

    def start(self, source, target):
        copy = pltpu.make_async_copy(source, target, self.sems.at[self.used])
        self.used += 1
        copy.start()
        return copy

    def out(self, source, target):
        self.open.append(self.start(source, target))

    def finish(self):
        for copy in self.open:
            copy.wait()


def wait_all(copies):
    for copy in copies:
        copy.wait()


class Piece:
    def __init__(self, array, row=None, source=0, target=0, count=None, clip=None):
        self.array = array
        self.row = row
        self.source = source
        self.target = target
        self.count = array.shape[0] if count is None else count
        self.clip = clip

    def load(self, copies, ref, meta_ref, scratch):
        rows = ref.shape[1]
        row = 0 if self.row is None else pl.multiple_of(meta_ref[self.row], 16)
        first = self.source if self.clip is None else meta_ref[self.clip]
        return copies.start(
            ref.at[pl.ds(first, self.count)],
            scratch.at[pl.ds(self.target, self.count), pl.ds(row, rows), :],
        )


def load_pieces(copies, pieces, refs, meta_ref, scratch):
    return [p.load(copies, ref, meta_ref, scratch) for p, ref in zip(pieces, refs)]


def arrays_of(pieces):
    return [piece.array for piece in pieces]


def run(body, meta, lens, near, far, outs, scratch, sems, flops=0):
    names, arrays, specs, spread = ["meta", "lens"], [meta, lens], [SMEM, SMEM], {}
    for name, array in near.items():
        names.append(name)
        arrays.append(array)
        specs.append(VMEM)
    for name, group in far.items():
        many = isinstance(group, (list, tuple))
        spread[name] = len(group) if many else None
        for number, array in enumerate(group if many else [group]):
            names.append((name, number))
            arrays.append(pltpu.with_memory_space_constraint(array, pltpu.HBM))
            specs.append(ANY)
    shapes, out_specs = [], []
    for name, (shape, dtype, stays) in outs.items():
        names.append(name)
        shapes.append(pltpu.VMEM(shape, dtype) if stays else pltpu.HBM(shape, dtype))
        out_specs.append(VMEM if stays else ANY)
    names += list(scratch) + ["sems"]

    def kernel(*refs):
        found = dict(zip(names, refs))
        for name, count in spread.items():
            if count is None:
                found[name] = found[(name, 0)]
            else:
                found[name] = [found[(name, number)] for number in range(count)]
        found = {name: ref for name, ref in found.items() if isinstance(name, str)}
        copies = Copies(found["sems"])
        body(types.SimpleNamespace(**found), copies)
        copies.finish()

    moved = sum(a.size * a.dtype.itemsize for a in arrays)
    results = pl.pallas_call(
        kernel,
        out_shape=tuple(shapes),
        in_specs=specs,
        out_specs=tuple(out_specs),
        scratch_shapes=[pltpu.VMEM(shape, dtype) for shape, dtype in scratch.values()]
        + [pltpu.SemaphoreType.DMA((sems,))],
        compiler_params=pltpu.CompilerParams(vmem_limit_bytes=LIMIT),
        cost_estimate=pl.CostEstimate(
            flops=3 * int(flops), bytes_accessed=int(moved), transcendentals=0
        ),
    )(*arrays)
    return types.SimpleNamespace(**dict(zip(outs, results)))


def groups_of(clips):
    per = min(4, clips)
    return [tuple(range(first, first + per)) for first in range(0, clips, per)]


def span(clip_numbers, frames):
    return slice(clip_numbers[0] * frames, (clip_numbers[-1] + 1) * frames)


def mask_of(len_ref, clip_numbers, frames):
    position = lax.broadcasted_iota(jnp.int32, (1, frames), 1)
    return lanes([(position < len_ref[clip]).astype(F32) for clip in clip_numbers])


def counted_of(len_ref, mask_ref, clip_numbers, frames):
    inside = mask_of(len_ref, clip_numbers, frames)
    return inside * lanes([mask_ref[clip : clip + 1, :].astype(F32) for clip in clip_numbers])


def conv_forward(weight_ref, source_ref, clip_numbers, frames, taps, at=0, waits=()):
    blocks = [source_ref[:, span((clip,), frames)] for clip in clip_numbers]
    total = None
    waits = dict(waits)
    for tap in range(taps):
        wait_all(waits.get(tap, ()))
        moved = lanes([shifted(block, tap - taps // 2) for block in blocks])
        term = jnp.dot(weight_ref[at + tap], moved, preferred_element_type=F32)
        total = term if total is None else total + term
    return total


def conv_backward(weight_ref, grad_ref, clip_numbers, frames, taps, at=0, waits=()):
    blocks = [grad_ref[:, span((clip,), frames)] for clip in clip_numbers]
    total = None
    waits = dict(waits)
    for tap in range(taps):
        wait_all(waits.get(tap, ()))
        moved = lanes([shifted(block, taps // 2 - tap) for block in blocks])
        term = lax.dot_general(
            weight_ref[at + tap],
            moved,
            (((0,), (0,)), ((), ())),
            preferred_element_type=F32,
        )
        total = term if total is None else total + term
    return total


def lookup(meta, lens, ids, book, clips, frames, dim):
    codes = book[0].array.shape[2]
    wide = (dim, clips * frames)

    def body(r, copies):
        loads = load_pieces(copies, book, r.book, r.meta, r.table)
        every = tuple(range(clips))
        inside = mask_of(r.lens, every, frames)
        for group in range(dim // GW):
            rows = slice(group * GW, (group + 1) * GW)
            found = []
            for level, far in ((0, r.q0), (1, r.q1)):
                hot = r.hot.at[level]
                one_hot(r.ids, hot, level, group, clips, frames, dim)
                if group == 0 and level == 0:
                    wait_all(loads)
                value = jnp.dot(r.table[level, rows, :], hot[...], preferred_element_type=F32)
                r.found[level, rows, :] = value.astype(BF16)
                copies.out(r.found.at[level, rows], far.at[rows])
                found.append(value)
            r.u3[rows, :] = (inside * (found[0] + found[1])).astype(BF16)
        copies.out(r.u3, r.u3_far)

    return run(
        body,
        meta,
        lens,
        {"ids": ids},
        {"book": arrays_of(book)},
        {
            "u3": (wide, BF16, True),
            "u3_far": (wide, BF16, False),
            "q0": (wide, BF16, False),
            "q1": (wide, BF16, False),
        },
        {
            "table": ((LEVELS, dim, codes), BF16),
            "hot": ((LEVELS, codes, clips * frames), BF16),
            "found": ((LEVELS,) + wide, BF16),
        },
        len(book) + 2 * LEVELS * (dim // GW) + 1,
        2 * LEVELS * dim * codes * clips * frames,
    )


def one_hot(ids_ref, hot, level, group, clips, frames, dim):
    number = lax.broadcasted_iota(jnp.int32, (hot.shape[0], frames), 0).astype(jnp.int16)
    one = jnp.ones((), BF16)
    zero = jnp.zeros((), BF16)
    for clip in range(clips):
        at = clip * LEVELS * (dim // GW) + group * LEVELS + level
        row = ids_ref[at : at + 1, :].astype(jnp.int16)
        hot[:, span((clip,), frames)] = jnp.where(number == row, one, zero)


def put_clips(copies, meta_ref, scratch, group, value, frames, refs, rows):
    for place, clip in enumerate(group):
        scratch[clip] = value[:, place * frames : (place + 1) * frames]
    at = pl.ds(group[0], len(group))
    for ref, (start, count) in zip(refs, rows):
        row = 0 if start is None else pl.multiple_of(meta_ref[start], 16)
        copies.out(scratch.at[at, pl.ds(row, count), :], ref.at[at])


def decoder_forward(meta, lens, u3, w3, w45, bias, out_rows, clips, frames, dim):
    wide = (dim, clips * frames)
    taps3 = w3[0].array.shape[0]
    taps4 = sum(p.count for p in w45 if p.row == w45[0].row) - 1
    outs = {"u4": (wide, BF16, True), "u5": (wide, BF16, True)}
    for number, (_, count) in enumerate(out_rows):
        outs["out%d" % number] = ((clips, count, frames), BF16, False)

    def body(r, copies):
        loads3 = load_pieces(copies, w3, r.w3, r.meta, r.t3)
        loads4 = load_pieces(copies, w45, r.w45, r.meta, r.t45)
        refs = [getattr(r, "out%d" % number) for number in range(len(out_rows))]
        for number, group in enumerate(groups_of(clips)):
            here = span(group, frames)
            inside = mask_of(r.lens, group, frames)
            waits = waits_of(w3, loads3) if number == 0 else ()
            first = conv_forward(r.t3, r.u3, group, frames, taps3, 0, waits) + r.bias[:, 3:4]
            r.u4[:, here] = (inside * elu(first)).astype(BF16)
            if number == 0:
                wait_all(loads4)
            second = conv_forward(r.t45, r.u4, group, frames, taps4) + r.bias[:, 4:5]
            r.u5[:, here] = (inside * elu(second)).astype(BF16)
            third = conv_forward(r.t45, r.u5, group, frames, 1, taps4) + r.bias[:, 5:6]
            result = (inside * (first + third)).astype(BF16)
            put_clips(copies, r.meta, r.work, group, result, frames, refs, out_rows)

    return run(
        body,
        meta,
        lens,
        {"u3": u3, "bias": bias},
        {"w3": arrays_of(w3), "w45": arrays_of(w45)},
        outs,
        {
            "t3": ((taps3, dim, dim), BF16),
            "t45": ((taps4 + 1, dim, dim), BF16),
            "work": ((clips, dim, frames), BF16),
        },
        len(w3) + len(w45) + len(out_rows) * len(groups_of(clips)),
        2 * (taps3 + taps4 + 1) * dim * dim * clips * frames,
    )


def waits_of(pieces, loads):
    waits = {}
    for piece, load in zip(pieces, loads):
        waits.setdefault(piece.target, []).append(load)
    return waits


class Rows:
    def __init__(self, dim, paired):
        self.dim = dim
        self.paired = paired
        self.count = 2 if paired else 1
        self.height = dim // self.count

    def outs(self, columns):
        return {
            "sums%d" % number: ((self.height, columns), BF16, self.paired)
            for number in range(self.count)
        }

    def scratch(self, columns):
        return {} if self.paired else {"sums": ((self.dim, columns), BF16)}

    def put(self, r, copies, at, value):
        if not self.paired:
            r.sums[:, at] = value
            copies.out(r.sums.at[:, at], r.sums0.at[:, at])
            return
        run_of = self.dim // 8
        first = r.meta[1] == 0
        for i in range(2):
            for j in range(2):
                row = (j * 4 + i) * run_of
                zero = value[row : row + run_of]
                row = (i * 4 + 2 + j) * run_of
                one = value[row : row + run_of]
                row = (i * 2 + j) * run_of
                r.sums0[row : row + run_of, at] = jnp.where(first, zero, one)
                r.sums1[row : row + run_of, at] = jnp.where(first, one, zero)


def weight_grads(r, copies, rows, g, u, taps, offset, clips, frames, dim):
    for tap in range(taps):
        step = taps // 2 - tap
        left = g[...]
        if step != 0:
            for clip in range(clips):
                at = span((clip,), frames)
                r.work[:, at] = shifted(g[:, at], step)
            left = r.work[...]
        value = lax.dot_general(
            left, u[...], (((1,), (1,)), ((), ())), preferred_element_type=F32
        )
        rows.put(r, copies, slice(offset, offset + dim), value.astype(BF16))
        offset += dim
    total = jnp.sum(g[...].astype(F32), axis=1, keepdims=True)
    total = jnp.broadcast_to(total, (dim, 128)).astype(BF16)
    rows.put(r, copies, slice(offset, offset + 128), total)
    return offset + 128


def decoder_backward(
    meta, lens, cotangent, u3, u4, u5, w45, taps3, rows, clips, frames, dim
):
    wide = (dim, clips * frames)
    taps4 = sum(p.count for p in w45 if p.row == w45[0].row) - 1
    columns = (taps3 + taps4 + 1) * dim + 3 * 128

    def body(r, copies):
        loads = load_pieces(copies, cotangent, r.cot, r.meta, r.clips)
        loads += load_pieces(copies, w45, r.w45, r.meta, r.t45)
        late = copies.start(r.u3, r.s3)
        wait_all(loads)
        for group in groups_of(clips):
            here = span(group, frames)
            inside = mask_of(r.lens, group, frames)
            out = lanes([r.clips[clip] for clip in group])
            out = jnp.where(inside > 0, out, jnp.zeros((), BF16))
            r.g5[:, here] = out
            back = conv_backward(r.t45, r.g5, group, frames, 1, taps4)
            r.g4[:, here] = (back * inside * slope_of(r.u5[:, here])).astype(BF16)
            back = conv_backward(r.t45, r.g4, group, frames, taps4)
            total = out.astype(F32) + back * inside * slope_of(r.u4[:, here])
            r.s_g3[:, here] = total.astype(BF16)
            copies.out(r.s_g3.at[:, here], r.g3.at[:, here])
        sizes = (clips, frames, dim)
        at = weight_grads(r, copies, rows, r.g5, r.u5, 1, 0, *sizes)
        at = weight_grads(r, copies, rows, r.g4, r.u4, taps4, at, *sizes)
        late.wait()
        weight_grads(r, copies, rows, r.s_g3, r.s3, taps3, at, *sizes)

    return run(
        body,
        meta,
        lens,
        {"u4": u4, "u5": u5},
        {"cot": arrays_of(cotangent), "w45": arrays_of(w45), "u3": u3},
        {"g3": (wide, BF16, False), **rows.outs(columns)},
        {
            "clips": ((clips, dim, frames), BF16),
            "t45": ((taps4 + 1, dim, dim), BF16),
            "s3": (wide, BF16),
            "g5": (wide, BF16),
            "g4": (wide, BF16),
            "s_g3": (wide, BF16),
            "work": (wide, BF16),
            **rows.scratch(columns),
        },
        len(cotangent) + len(w45) + 1 + len(groups_of(clips)) + rows.count * (taps3 + taps4 + 4),
        2 * (taps3 + 2 * taps4 + 2) * dim * dim * clips * frames,
    )


def encoder_forward(meta, lens, mask, tokens, w012, bias, q0, q1, taps0, clips, frames, dim):
    wide = (dim, clips * frames)
    groups = groups_of(clips)

    def body(r, copies):
        loads = load_pieces(copies, tokens, r.tokens, r.meta, r.clips)
        loads_w = load_pieces(copies, w012, r.w012, r.meta, r.t)
        late = [copies.start(r.q0, r.s_q0), copies.start(r.q1, r.s_q1)]
        wait_all(loads)
        for number, group in enumerate(groups):
            here = span(group, frames)
            inside = mask_of(r.lens, group, frames)
            start = inside * lanes([r.clips[clip] for clip in group]).astype(F32)
            r.s0[:, here] = elu(start).astype(BF16)
            copies.out(r.s0.at[:, here], r.u0.at[:, here])
            if number == 0:
                wait_all(loads_w)
            first = conv_forward(r.t, r.s0, group, frames, taps0) + r.bias[:, 0:1]
            r.s1[:, here] = (inside * elu(first)).astype(BF16)
            copies.out(r.s1.at[:, here], r.u1.at[:, here])
            second = conv_forward(r.t, r.s1, group, frames, 1, taps0) + r.bias[:, 1:2]
            r.s2[:, here] = elu(inside * (start + second)).astype(BF16)
            copies.out(r.s2.at[:, here], r.u2.at[:, here])
            latent = conv_forward(r.t, r.s2, group, frames, taps0, taps0 + 1)
            latent = latent + r.bias[:, 2:3]
            if number == 0:
                wait_all(late)
            double = 2.0 * counted_of(r.lens, r.mask, group, frames)
            miss = r.s_q0[:, here].astype(F32) - latent
            r.s_q0[:, here] = (double * miss).astype(BF16)
            copies.out(r.s_q0.at[:, here], r.gq0.at[:, here])
            r.s_q1[:, here] = (double * (miss + r.s_q1[:, here].astype(F32))).astype(BF16)
            copies.out(r.s_q1.at[:, here], r.gq1.at[:, here])

    names = ("u0", "u1", "u2", "gq0", "gq1")
    return run(
        body,
        meta,
        lens,
        {"mask": mask, "bias": bias},
        {"tokens": arrays_of(tokens), "w012": arrays_of(w012), "q0": q0, "q1": q1},
        {name: (wide, BF16, False) for name in names},
        {
            "clips": ((clips, dim, frames), BF16),
            "t": ((2 * taps0 + 1, dim, dim), BF16),
            **{name: (wide, BF16) for name in ("s0", "s1", "s2", "s_q0", "s_q1")},
        },
        len(tokens) + len(w012) + 2 + 5 * len(groups),
        2 * (2 * taps0 + 1) * dim * dim * clips * frames,
    )


def latent_backward(
    meta, lens, ids, g3, w3, gq0, gq1, u2, taps2, codes, rows, clips, frames, dim
):
    wide = (dim, clips * frames)
    taps3 = w3[0].array.shape[0]
    columns = taps2 * dim + 128 + LEVELS * codes

    def body(r, copies):
        loads = [copies.start(r.g3, r.s_g3)]
        loads_w = load_pieces(copies, w3, r.w3, r.meta, r.t3)
        second = copies.start(r.gq1, r.s_gq.at[1])
        first = copies.start(r.gq0, r.s_gq.at[0])
        late = copies.start(r.u2, r.s_u2)
        wait_all(loads)
        for number, group in enumerate(groups_of(clips)):
            here = span(group, frames)
            inside = mask_of(r.lens, group, frames)
            waits = waits_of(w3, loads_w) if number == 0 else ()
            back = conv_backward(r.t3, r.s_g3, group, frames, taps3, 0, waits)
            if number == 0:
                second.wait()
            extra = BETA * r.s_gq[1, :, here].astype(F32)
            r.g2[:, here] = (back * inside - extra).astype(BF16)
        late.wait()
        sizes = (clips, frames, dim)
        offset = weight_grads(r, copies, rows, r.g2, r.s_u2, taps2, 0, *sizes)
        first.wait()
        for level in range(LEVELS):
            values = []
            for group in range(dim // GW):
                at = slice(group * GW, (group + 1) * GW)
                one_hot(r.ids, r.hot, level, group, clips, frames, dim)
                values.append(
                    lax.dot_general(
                        r.s_gq[level, at, :],
                        r.hot[...],
                        (((1,), (1,)), ((), ())),
                        preferred_element_type=F32,
                    ).astype(BF16)
                )
            value = jnp.concatenate(values, axis=0)
            rows.put(r, copies, slice(offset, offset + codes), value)
            offset += codes

    return run(
        body,
        meta,
        lens,
        {"ids": ids},
        {"g3": g3, "w3": arrays_of(w3), "gq0": gq0, "gq1": gq1, "u2": u2},
        {"g2": (wide, BF16, True), **rows.outs(columns)},
        {
            "t3": ((taps3, dim, dim), BF16),
            "s_g3": (wide, BF16),
            "s_gq": ((LEVELS,) + wide, BF16),
            "s_u2": (wide, BF16),
            "hot": ((codes, clips * frames), BF16),
            "work": (wide, BF16),
            **rows.scratch(columns),
        },
        len(w3) + 4 + rows.count * (taps2 + 1 + LEVELS),
        2 * ((taps3 + taps2) * dim + LEVELS * codes) * dim * clips * frames,
    )


def encoder_backward(
    meta, lens, g2, u2, u1, u0, w12, taps0, rows, clips, frames, dim
):
    wide = (dim, clips * frames)
    columns = (taps0 + 1) * dim + 2 * 128

    def body(r, copies):
        loads = load_pieces(copies, w12, r.w12, r.meta, r.t)
        second = copies.start(r.u2, r.s2)
        first = copies.start(r.u1, r.s1)
        late = copies.start(r.u0, r.s0)
        wait_all(loads)
        for number, group in enumerate(groups_of(clips)):
            here = span(group, frames)
            inside = mask_of(r.lens, group, frames)
            back = conv_backward(r.t, r.g2, group, frames, taps0, 1)
            if number == 0:
                second.wait()
            r.g1[:, here] = (back * inside * slope_of(r.s2[:, here])).astype(BF16)
            back = conv_backward(r.t, r.g1, group, frames, 1)
            if number == 0:
                first.wait()
            r.g0[:, here] = (back * inside * slope_of(r.s1[:, here])).astype(BF16)
        late.wait()
        sizes = (clips, frames, dim)
        at = weight_grads(r, copies, rows, r.g0, r.s0, taps0, 0, *sizes)
        weight_grads(r, copies, rows, r.g1, r.s1, 1, at, *sizes)

    return run(
        body,
        meta,
        lens,
        {"g2": g2},
        {"w12": arrays_of(w12), "u2": u2, "u1": u1, "u0": u0},
        {"g1": (wide, BF16, True), "g0": (wide, BF16, True), **rows.outs(columns)},
        {
            "t": ((taps0 + 1, dim, dim), BF16),
            "s2": (wide, BF16),
            "s1": (wide, BF16),
            "s0": (wide, BF16),
            "work": (wide, BF16),
            **rows.scratch(columns),
        },
        len(w12) + 3 + rows.count * (taps0 + 3),
        2 * (2 * taps0 + 2) * dim * dim * clips * frames,
    )


def tokens_backward(meta, lens, g0, u0, g1, w0, taps0, out_rows, clips, frames, dim):
    wide = (dim, clips * frames)
    outs = {}
    for number, (_, count) in enumerate(out_rows):
        outs["out%d" % number] = ((clips, count, frames), BF16, False)

    def body(r, copies):
        loads = load_pieces(copies, w0, r.w0, r.meta, r.t)
        late = copies.start(r.u0, r.s0)
        refs = [getattr(r, "out%d" % number) for number in range(len(out_rows))]
        wait_all(loads)
        for number, group in enumerate(groups_of(clips)):
            here = span(group, frames)
            inside = mask_of(r.lens, group, frames)
            back = conv_backward(r.t, r.g0, group, frames, taps0)
            if number == 0:
                late.wait()
            total = r.g1[:, here].astype(F32) + back * inside * slope_of(r.s0[:, here])
            total = (inside * total).astype(BF16)
            put_clips(copies, r.meta, r.work, group, total, frames, refs, out_rows)

    result = run(
        body,
        meta,
        lens,
        {"g0": g0, "g1": g1},
        {"w0": arrays_of(w0), "u0": u0},
        outs,
        {
            "t": ((taps0, dim, dim), BF16),
            "s0": (wide, BF16),
            "work": ((clips, dim, frames), BF16),
        },
        len(w0) + 1 + len(out_rows) * len(groups_of(clips)),
        2 * taps0 * dim * dim * clips * frames,
    )
    return [getattr(result, "out%d" % number) for number in range(len(out_rows))]


def unpack(meta, pieces, blocks, half):
    outs = []
    for taps, width, has_bias in blocks:
        outs.append(struct((taps, half, width), F32))
        if has_bias:
            outs.append(struct((1, half), F32))

    def body(meta_ref, mine_ref, other_ref, *refs):
        take = iter(refs)
        first = meta_ref[1] == 0

        def columns(at):
            mine, other = mine_ref[:, at], other_ref[:, at]
            return jnp.concatenate(
                [jnp.where(first, mine, other), jnp.where(first, other, mine)], axis=0
            ).astype(F32)

        offset = 0
        for taps, width, has_bias in blocks:
            out = next(take)
            for tap in range(taps):
                out[tap] = columns(slice(offset, offset + width))
                offset += width
            if has_bias:
                next(take)[...] = columns(slice(offset, offset + 128)).T[0:1]
                offset += 128

    return pl.pallas_call(
        body,
        out_shape=tuple(outs),
        in_specs=[SMEM, VMEM, VMEM],
        out_specs=tuple(VMEM for _ in outs),
        compiler_params=pltpu.CompilerParams(vmem_limit_bytes=LIMIT),
    )(meta, *pieces)


class Pairs:
    BITS = {"core": 1, "x": 2, "zl": 4, "zh": 8}

    def __init__(self, rows, clips):
        self.chan = lax.axis_index("chan")
        self.dp = lax.axis_index("dp")
        self.core = self.bit("core")
        x = self.bit("x")
        other = (1 - self.chan) * rows
        piece = rows // 4
        here = [(self.core, x), (self.core, 1 - x), (1 - self.core, x), (1 - self.core, 1 - x)]
        self.piece = (self.core * 2 + x) * piece
        self.meta = jnp.stack(
            [self.chan, self.core, self.chan * rows, other]
            + [other + (c * 2 + b) * piece for c, b in here]
            + [self.chan * clips]
        ).astype(jnp.int32)

    def bit(self, name):
        if name == "chan":
            return self.chan
        return (self.dp & self.BITS[name]) // self.BITS[name]

    def swap(self, value, name):
        if name == "chan":
            return lax.ppermute(value, "chan", [(0, 1), (1, 0)])
        mask = self.BITS[name]
        return lax.ppermute(value, "dp", [(i, i ^ mask) for i in range(16)])

    def swap_by_core(self, value, names):
        if names[0] == names[1]:
            return self.swap(value, names[0])
        pairs = []
        for place in range(32):
            name = names[(place // 2) & 1]
            pairs.append((place, place ^ (1 if name == "chan" else 2 * self.BITS[name])))
        return lax.ppermute(value, ("dp", "chan"), pairs)

    def bit_by_core(self, names):
        return jnp.where(self.core == 0, self.bit(names[0]), self.bit(names[1]))

    def piece_of(self, own):
        return lax.dynamic_slice_in_dim(own, self.piece, own.shape[1] // 4, 1)

    def spread(self, near):
        far = self.swap(near, "x")
        return near, far, self.swap(near, "core"), self.swap(far, "core")

    def ordered(self, own, came):
        first = self.chan == 0
        return jnp.concatenate([jnp.where(first, own, came), jnp.where(first, came, own)])

    def start(self, grads):
        kept, sent = grads
        return Reduction(self, kept, self.swap(sent, "core"))


class Reduction:
    ORDERS = (("x", "chan", "zl", "zh"), ("chan", "zl", "zh", "x"))

    def __init__(self, links, kept, came):
        self.links = links
        self.todo = list(zip(*self.ORDERS))
        gather = [[name for name in reversed(order) if name != "chan"] for order in self.ORDERS]
        self.back = list(zip(*gather)) + [("core", "core")]
        self.terms = [kept]
        self.bits = []
        self.came = came
        self.value = None
        self.last = None

    @property
    def done(self):
        return not self.back

    def total(self, bits):
        sums = None
        for number, term in enumerate(self.terms):
            mine = bits[max(number - 1, 0) :]
            columns = term.shape[-1]
            block = term.reshape((2,) * len(mine) + (-1, columns))
            start = tuple(mine) + (0, 0)
            size = (1,) * len(mine) + block.shape[len(mine) :]
            piece = lax.dynamic_slice(block, start, size).reshape(-1, columns).astype(F32)
            sums = piece if sums is None else sums + piece
        return sums.astype(BF16)

    def step(self):
        links = self.links
        if self.value is None:
            self.terms.append(self.came)
        if self.todo:
            names = self.todo.pop(0)
            bit = links.bit_by_core(names)
            sent = self.total(self.bits + [1 - bit])
            self.bits.append(bit)
        else:
            names = self.back.pop(0)
            if self.value is None:
                sent = self.total(self.bits)
            else:
                first = links.bit_by_core(self.last) == 0
                mine, other = self.value, self.came
                sent = jnp.concatenate(
                    [jnp.where(first, mine, other), jnp.where(first, other, mine)]
                )
            self.value = sent
            self.last = names
        self.came = links.swap_by_core(sent, names)
        return sent

    @property
    def result(self):
        return [self.value, self.came]


def advance(after, *reductions):
    came = lax.optimization_barrier((tuple(r.came for r in reductions), tuple(after)))[0]
    for reduction, array in zip(reductions, came):
        reduction.came = array
    return [reduction.step() for reduction in reductions]


def on_pairs(
    tokens,
    lengths,
    frame_mask,
    code_ids,
    cotangent,
    weights,
    biases,
    codebook,
):
    chan = 2
    rows = tokens.shape[1]
    frames = tokens.shape[2]
    dim = rows * chan
    clips = tokens.shape[0] // chan
    codes = codebook.shape[2]
    sizes = (clips, frames, dim)
    links = Pairs(rows, clips)
    meta = links.meta
    mine = functools.partial(
        lax.dynamic_slice_in_dim, start_index=links.chan * clips, slice_size=clips, axis=0
    )
    others = functools.partial(
        lax.dynamic_slice_in_dim, start_index=(1 - links.chan) * clips, slice_size=clips, axis=0
    )
    taps = [w.shape[0] for w in weights]
    own, other, pieces = 2, 3, (4, 5, 6, 7)

    split = (taps[3] + 1) // 2
    near_book = links.swap(links.piece_of(codebook), "chan")
    near3a = links.swap(links.piece_of(weights[3][:split]), "chan")
    near3b = links.swap(links.piece_of(weights[3][split:]), "chan")
    lens = mine(lengths)
    mask = mine(frame_mask)
    ids = mine(code_ids).reshape(-1, frames)
    far_book = links.spread(near_book)
    dec = jnp.concatenate([weights[4], weights[5]])
    enc = jnp.concatenate([weights[0], weights[1], weights[2]])
    bias = jnp.stack(biases + (jnp.zeros_like(biases[0]),) * 2, axis=1)
    bias = links.ordered(bias, links.swap(tie(bias, near_book), "chan"))
    dec_piece = tie(links.piece_of(dec), near_book)
    near45 = links.swap(dec_piece, "chan")
    enc_piece = tie(links.piece_of(enc), near3b, dec_piece)
    near012 = links.swap(enc_piece, "chan")
    book = [Piece(codebook, own)] + [Piece(a, s) for a, s in zip(far_book, pieces)]
    found = lookup(meta, lens, ids, book, *sizes)
    cot_send = others(tie(cotangent, far_book[3]))
    cot_other = links.swap(tie(cot_send, near45), "chan")
    far3a = links.spread(near3a)
    far3b = links.spread(near3b)
    far45 = links.spread(tie(near45, far3b[1]))
    w3 = [Piece(weights[3], own, 0, 0, split)]
    w3 += [Piece(a, s) for a, s in zip(far3a, pieces)]
    w3 += [Piece(weights[3], own, split, split, taps[3] - split)]
    w3 += [Piece(a, s, 0, split) for a, s in zip(far3b, pieces)]
    w45 = [Piece(weights[4], own), Piece(weights[5], own, 0, taps[4])]
    w45 += [Piece(a, s) for a, s in zip(far45, pieces)]
    far012 = links.spread(tie(near012, far45[1], found.u3))
    out_rows = ((own, rows), (other, rows))
    dec_out = decoder_forward(
        meta, lens, tie(found.u3, cot_send), w3, w45, bias, out_rows, *sizes
    )
    tok_send = tie(others(tokens), cot_other, dec_out.u4)
    tok_other = links.swap(tok_send, "chan")
    rows_of = Rows(dim, True)
    cot = [Piece(cotangent, own, clip=8, count=clips)]
    cot.append(Piece(tie(cot_other, tok_send, *far012), other))
    dec_back = decoder_backward(
        meta,
        lens,
        cot,
        found.u3_far,
        dec_out.u4,
        dec_out.u5,
        w45,
        taps[3],
        rows_of,
        *sizes,
    )
    red_a = links.start([dec_back.sums0, tie(dec_back.sums1, tok_other)])
    out_send = tie(dec_out.out1, tok_other)
    out_came = links.swap(out_send, "chan")

    def enc_pieces(which):
        listed = []
        place = 0
        for number in which:
            listed.append(Piece(weights[number], own, 0, place))
            place += taps[number]
        start = sum(taps[: which[0]])
        listed += [Piece(a, s, start, 0, place) for a, s in zip(far012, pieces)]
        return listed

    tok = [Piece(tokens, own, clip=8, count=clips)]
    tok.append(Piece(tie(tok_other, dec_back.g3, out_send), other))
    enc_out = encoder_forward(
        meta,
        lens,
        mask,
        tok,
        enc_pieces([0, 1, 2]),
        bias,
        found.q0,
        found.q1,
        taps[0],
        *sizes,
    )
    sent = advance([enc_out.u2], red_a)
    lat = latent_backward(
        meta,
        lens,
        ids,
        tie(dec_back.g3, out_came, *sent),
        w3,
        enc_out.gq0,
        enc_out.gq1,
        enc_out.u2,
        taps[2],
        codes,
        rows_of,
        *sizes,
    )
    red_c = links.start([lat.sums0, lat.sums1])
    sent = advance([lat.g2], red_a)
    output = links.ordered(dec_out.out0, tie(out_came, lat.g2))
    enc_back = encoder_backward(
        meta,
        lens,
        lat.g2,
        tie(enc_out.u2, *sent),
        enc_out.u1,
        enc_out.u0,
        enc_pieces([1, 2]),
        taps[0],
        rows_of,
        *sizes,
    )
    red_d = links.start([enc_back.sums0, enc_back.sums1])
    sent = advance([enc_back.g0], red_a, red_c)
    grad_own, grad_other = tokens_backward(
        meta,
        lens,
        enc_back.g0,
        tie(enc_out.u0, *sent),
        enc_back.g1,
        enc_pieces([0]),
        taps[0],
        out_rows,
        *sizes,
    )
    grad_came = links.swap(grad_other, "chan")
    sent = advance([grad_other], red_a, red_c, red_d)
    shapes = {
        red_a: [(1, dim, True), (taps[4], dim, True), (taps[3], dim, True)],
        red_c: [(taps[2], dim, True), (LEVELS, codes, False)],
        red_d: [(taps[0], dim, True), (1, dim, True)],
    }
    results = {}
    while not red_d.done:
        if len(red_d.back) == 3 and red_d.todo == []:
            sent = list(sent) + [grad_came]
        active = [r for r in (red_a, red_c, red_d) if not r.done]
        ready = [r for r in (red_a, red_c) if r.done and r not in results]
        for r in ready:
            mine_rows, other_rows = r.result
            results[r] = unpack(meta, [tie(mine_rows, *sent), other_rows], shapes[r], rows)
            sent = list(sent) + list(results[r][:1])
        sent = advance(sent, *active)
    tokens_grad = links.ordered(
        grad_own.astype(F32), tie(grad_came, *sent).astype(F32)
    )
    for r in (red_c, red_d):
        if r not in results:
            results[r] = unpack(meta, r.result, shapes[r], rows)
    a, c, d = results[red_a], results[red_c], results[red_d]
    w_grads = [d[0], d[2], c[0], a[4], a[2], a[0]]
    b_grads = [v.reshape(rows) for v in (d[1], d[3], c[1], a[5], a[3], a[1])]
    grads = [g for pair in zip(w_grads, b_grads) for g in pair]
    return (output, tokens_grad, *grads, c[2])


def on_others(
    tokens,
    lengths,
    frame_mask,
    code_ids,
    cotangent,
    weights,
    biases,
    codebook,
):
    chan = lax.axis_size("chan")
    place = lax.axis_index("chan")
    rows = tokens.shape[1]
    frames = tokens.shape[2]
    dim = rows * chan
    clips = tokens.shape[0] // chan
    codes = codebook.shape[2]
    sizes = (clips, frames, dim)
    meta = jnp.zeros((9,), jnp.int32)
    mine = functools.partial(
        lax.dynamic_slice_in_dim, start_index=place * clips, slice_size=clips, axis=0
    )
    taps = [w.shape[0] for w in weights]

    def gathered(*arrays):
        return [Piece(lax.all_gather(jnp.concatenate(arrays), "chan", axis=1, tiled=True))]

    def part(pieces, start, count):
        return [Piece(pieces[0].array, None, start, 0, count)]

    def clips_in(array):
        return [Piece(lax.all_to_all(array, "chan", 0, 1, tiled=True))]

    def clips_out(array):
        return lax.all_to_all(array, "chan", 1, 0, tiled=True)

    def reduced(grads):
        part = lax.psum_scatter(grads.astype(F32), "chan", scatter_dimension=0, tiled=True)
        return lax.psum(part, "dp")

    def columns(total, offset, count, width):
        block = total[:, offset : offset + count * width].reshape(rows, count, width)
        return jnp.transpose(block, (1, 0, 2))

    bias = jnp.stack(biases + (jnp.zeros_like(biases[0]),) * 2, axis=1)
    bias = lax.all_gather(bias, "chan", axis=0, tiled=True)
    lens = mine(lengths)
    mask = mine(frame_mask)
    ids = mine(code_ids).reshape(-1, frames)
    w3 = gathered(weights[3])
    w45 = gathered(weights[4], weights[5])
    w012 = gathered(weights[0], weights[1], weights[2])
    rows_of = Rows(dim, False)
    out_rows = ((None, dim),)
    found = lookup(meta, lens, ids, gathered(codebook), *sizes)
    dec_out = decoder_forward(meta, lens, found.u3, w3, w45, bias, out_rows, *sizes)
    dec_back = decoder_backward(
        meta,
        lens,
        clips_in(cotangent),
        found.u3_far,
        dec_out.u4,
        dec_out.u5,
        w45,
        taps[3],
        rows_of,
        *sizes,
    )
    enc_out = encoder_forward(
        meta, lens, mask, clips_in(tokens), w012, bias, found.q0, found.q1, taps[0], *sizes
    )
    lat = latent_backward(
        meta,
        lens,
        ids,
        dec_back.g3,
        w3,
        enc_out.gq0,
        enc_out.gq1,
        enc_out.u2,
        taps[2],
        codes,
        rows_of,
        *sizes,
    )
    enc_back = encoder_backward(
        meta,
        lens,
        lat.g2,
        enc_out.u2,
        enc_out.u1,
        enc_out.u0,
        part(w012, taps[0], 1 + taps[2]),
        taps[0],
        rows_of,
        *sizes,
    )
    (grad,) = tokens_backward(
        meta,
        lens,
        enc_back.g0,
        enc_out.u0,
        enc_back.g1,
        part(w012, 0, taps[0]),
        taps[0],
        out_rows,
        *sizes,
    )
    a, c, d = (reduced(x.sums0) for x in (dec_back, lat, enc_back))
    placed = (
        (d, 0, taps[0]),
        (d, taps[0] * dim + 128, 1),
        (c, 0, taps[2]),
        (a, (1 + taps[4]) * dim + 256, taps[3]),
        (a, dim + 128, taps[4]),
        (a, 0, 1),
    )
    grads = []
    for total, start, count in placed:
        grads.append(columns(total, start, count, dim))
        grads.append(total[:, start + count * dim])
    books = columns(c, taps[2] * dim + 128, LEVELS, codes)
    return (clips_out(dec_out.out0), clips_out(grad).astype(F32), *grads, books)


def on_device(step, tokens, lengths, frame_mask, code_ids, cotangent, *params):
    weights, biases = params[0:12:2], params[1:12:2]
    return step(
        tokens, lengths, frame_mask, code_ids, cotangent, weights, biases, params[12]
    )


def solution(mesh):
    paired = mesh.shape["chan"] == 2 and mesh.shape["dp"] == 16
    weight = P(None, "chan", None)
    vector = P("chan")
    clip_rows = P("dp", "chan", None)
    in_specs = (
        (clip_rows, P("dp"), P("dp", None), P("dp", None, None), clip_rows)
        + (weight, vector) * 6
        + (weight,)
    )
    out_specs = (clip_rows, clip_rows) + (weight, vector) * 6 + (weight,)
    return jax.shard_map(
        functools.partial(on_device, on_pairs if paired else on_others),
        mesh=mesh,
        in_specs=in_specs,
        out_specs=out_specs,
        check_vma=False,
    )
```

```python
import functools
import types

import jax
import jax.numpy as jnp
from jax import lax
from jax.experimental import pallas as pl
from jax.experimental.pallas import tpu as pltpu
from jax.sharding import PartitionSpec as P

LEVELS = 2
GW = 256
BETA = 0.25
F32 = jnp.float32
BF16 = jnp.bfloat16
MIB = 1024 * 1024
LIMIT = 28 * MIB
GRAD_SLOTS = ((1, 3), (2, 4))
OUT_SLOTS = (3, 7)
COVER = {
    "lookup": 0.01,
    "decoder_first": 0.01,
    "decoder_rest": 0.01,
    "decoder_backward": 0.01,
    "encoder_forward": 10,
    "latent_backward": 10,
    "encoder_backward": 10,
    "encoder_grads": 10,
    "tokens_backward": 10,
    "advance": 0,
}

ANY = pl.BlockSpec(memory_space=pl.ANY)
VMEM = pl.BlockSpec(memory_space=pltpu.VMEM)
SMEM = pl.BlockSpec(memory_space=pltpu.SMEM)


def elu(value):
    return jnp.where(value > 0, value, jnp.exp(jnp.minimum(value, 0.0)) - 1.0)


def slope_of(activated):
    act = activated.astype(F32)
    return jnp.where(act > 0, 1.0, 1.0 + act)


def shifted(value, step):
    if step == 0:
        return value
    edge = jnp.zeros((value.shape[0], abs(step)), value.dtype)
    if step > 0:
        return jnp.concatenate([value[:, step:], edge], axis=1)
    return jnp.concatenate([edge, value[:, :step]], axis=1)


def lanes(blocks):
    return blocks[0] if len(blocks) == 1 else jnp.concatenate(blocks, axis=1)


def tie(value, *earlier):
    earlier = [array for array in earlier if array is not None]
    if not earlier:
        return value
    return lax.optimization_barrier((value, tuple(earlier)))[0]


def held(array):
    return pltpu.with_memory_space_constraint(array, pltpu.VMEM)


def struct(shape, dtype):
    return jax.ShapeDtypeStruct(shape, dtype)


class Copies:
    def __init__(self, sems):
        self.sems = sems
        self.used = 0
        self.open = []

    def start(self, source, target):
        copy = pltpu.make_async_copy(source, target, self.sems.at[self.used])
        self.used += 1
        copy.start()
        return copy

    def out(self, source, target):
        self.open.append(self.start(source, target))

    def finish(self):
        for copy in self.open:
            copy.wait()


def wait_all(copies):
    for copy in copies:
        copy.wait()


class Piece:
    def __init__(self, array, row=None, source=0, target=0, count=None, clip=None):
        self.array = array
        self.row = row
        self.source = source
        self.target = target
        self.count = array.shape[0] if count is None else count
        self.clip = clip

    def load(self, copies, ref, meta_ref, scratch):
        rows = ref.shape[1]
        row = 0 if self.row is None else pl.multiple_of(meta_ref[self.row], 16)
        first = self.source if self.clip is None else meta_ref[self.clip]
        return copies.start(
            ref.at[pl.ds(first, self.count)],
            scratch.at[pl.ds(self.target, self.count), pl.ds(row, rows), :],
        )


def load_pieces(copies, pieces, refs, meta_ref, scratch):
    return [p.load(copies, ref, meta_ref, scratch) for p, ref in zip(pieces, refs)]


def load_clips(copies, pieces, refs, meta_ref, scratch, groups):
    loads = []
    for group in groups:
        begun = []
        for p, ref in zip(pieces, refs):
            part = Piece(p.array, p.row, group[0], group[0], len(group))
            if p.clip is not None:
                start = meta_ref[p.clip]
                ref = ref.at[pl.ds(start, scratch.shape[0])]
            begun.append(part.load(copies, ref, meta_ref, scratch))
        loads.append(begun)
    return loads


def taps_of(pieces):
    return max(piece.target + piece.count for piece in pieces)


def arrays_of(pieces):
    return [piece.array for piece in pieces]


def run(kind, body, meta, lens, near, far, outs, scratch, sems, flops=0):
    names, arrays, specs, spread = ["meta", "lens"], [meta, lens], [SMEM, SMEM], {}
    for name, array in near.items():
        names.append(name)
        arrays.append(held(array) if array.size >= MIB else array)
        specs.append(VMEM)
    for name, group in far.items():
        many = isinstance(group, (list, tuple))
        spread[name] = len(group) if many else None
        for number, array in enumerate(group if many else [group]):
            names.append((name, number))
            arrays.append(pltpu.with_memory_space_constraint(array, pltpu.HBM))
            specs.append(ANY)
    shapes, out_specs = [], []
    for name, (shape, dtype, stays) in outs.items():
        names.append(name)
        shapes.append(pltpu.VMEM(shape, dtype) if stays else pltpu.HBM(shape, dtype))
        out_specs.append(VMEM if stays else ANY)
    names += list(scratch) + ["sems"]

    def kernel(*refs):
        found = dict(zip(names, refs))
        for name, count in spread.items():
            if count is None:
                found[name] = found[(name, 0)]
            else:
                found[name] = [found[(name, number)] for number in range(count)]
        found = {name: ref for name, ref in found.items() if isinstance(name, str)}
        copies = Copies(found["sems"])
        body(types.SimpleNamespace(**found), copies)
        copies.finish()

    moved = sum(a.size * a.dtype.itemsize for a in arrays)
    cover = COVER[kind]
    results = pl.pallas_call(
        kernel,
        out_shape=tuple(shapes),
        in_specs=specs,
        out_specs=tuple(out_specs),
        scratch_shapes=[pltpu.VMEM(shape, dtype) for shape, dtype in scratch.values()]
        + [pltpu.SemaphoreType.DMA((sems,))],
        compiler_params=pltpu.CompilerParams(vmem_limit_bytes=LIMIT),
        cost_estimate=pl.CostEstimate(
            flops=max(int(cover * flops), 1), bytes_accessed=int(cover * moved), transcendentals=0
        ),
    )(*arrays)
    return types.SimpleNamespace(**dict(zip(outs, results)))


def groups_of(clips):
    per = min(4, clips)
    return [tuple(range(first, first + per)) for first in range(0, clips, per)]


def span(clip_numbers, frames):
    return slice(clip_numbers[0] * frames, (clip_numbers[-1] + 1) * frames)


def mask_of(len_ref, clip_numbers, frames):
    position = lax.broadcasted_iota(jnp.int32, (1, frames), 1)
    return lanes([(position < len_ref[clip]).astype(F32) for clip in clip_numbers])


def counted_of(len_ref, mask_ref, clip_numbers, frames):
    inside = mask_of(len_ref, clip_numbers, frames)
    return inside * lanes([mask_ref[clip : clip + 1, :].astype(F32) for clip in clip_numbers])


def conv_forward(weight_ref, source_ref, clip_numbers, frames, taps, at=0, waits=()):
    blocks = [source_ref[:, span((clip,), frames)] for clip in clip_numbers]
    total = None
    waits = dict(waits)
    for tap in range(taps):
        wait_all(waits.get(tap, ()))
        moved = lanes([shifted(block, tap - taps // 2) for block in blocks])
        term = jnp.dot(weight_ref[at + tap], moved, preferred_element_type=F32)
        total = term if total is None else total + term
    return total


def conv_backward(weight_ref, grad_ref, clip_numbers, frames, taps, at=0, waits=()):
    blocks = [grad_ref[:, span((clip,), frames)] for clip in clip_numbers]
    total = None
    waits = dict(waits)
    for tap in range(taps):
        wait_all(waits.get(tap, ()))
        moved = lanes([shifted(block, taps // 2 - tap) for block in blocks])
        term = lax.dot_general(
            weight_ref[at + tap],
            moved,
            (((0,), (0,)), ((), ())),
            preferred_element_type=F32,
        )
        total = term if total is None else total + term
    return total


def lookup(meta, lens, ids, book, clips, frames, dim):
    codes = book[0].array.shape[2]
    wide = (dim, clips * frames)

    def body(r, copies):
        loads = load_pieces(copies, book, r.book, r.meta, r.table)
        every = tuple(range(clips))
        inside = mask_of(r.lens, every, frames)
        for group in range(dim // GW):
            rows = slice(group * GW, (group + 1) * GW)
            found = []
            for level, far in ((0, r.q0), (1, r.q1)):
                hot = r.hot.at[level]
                one_hot(r.ids, hot, level, group, clips, frames, dim)
                if group == 0 and level == 0:
                    wait_all(loads)
                value = jnp.dot(r.table[level, rows, :], hot[...], preferred_element_type=F32)
                r.found[level, rows, :] = value.astype(BF16)
                copies.out(r.found.at[level, rows], far.at[rows])
                found.append(value)
            r.u3[rows, :] = (inside * (found[0] + found[1])).astype(BF16)
            copies.out(r.u3.at[rows], r.u3_far.at[rows])

    return run(
        "lookup",
        body,
        meta,
        lens,
        {"ids": ids},
        {"book": arrays_of(book)},
        {
            "u3": (wide, BF16, True),
            "u3_far": (wide, BF16, False),
            "q0": (wide, BF16, False),
            "q1": (wide, BF16, False),
        },
        {
            "table": ((LEVELS, dim, codes), BF16),
            "hot": ((LEVELS, codes, clips * frames), BF16),
            "found": ((LEVELS,) + wide, BF16),
        },
        len(book) + 3 * LEVELS * (dim // GW),
        2 * LEVELS * dim * codes * clips * frames,
    )


def one_hot(ids_ref, hot, level, group, clips, frames, dim):
    number = lax.broadcasted_iota(jnp.int32, (hot.shape[0], frames), 0).astype(jnp.int16)
    one = jnp.ones((), BF16)
    zero = jnp.zeros((), BF16)
    for clip in range(clips):
        at = clip * LEVELS * (dim // GW) + group * LEVELS + level
        row = ids_ref[at : at + 1, :].astype(jnp.int16)
        hot[:, span((clip,), frames)] = jnp.where(number == row, one, zero)


def clip_outs(out_rows, clips, frames):
    return {
        "out%d_%d" % (number, group): ((len(members), count, frames), BF16, False)
        for number, (_, count) in enumerate(out_rows)
        for group, members in enumerate(groups_of(clips))
    }


def clip_results(result, out_rows, clips):
    groups = range(len(groups_of(clips)))
    return [
        [getattr(result, "out%d_%d" % (number, group)) for group in groups]
        for number in range(len(out_rows))
    ]


def put_clips(copies, r, scratch, number, group, value, frames, rows):
    for place, clip in enumerate(group):
        scratch[clip] = value[:, place * frames : (place + 1) * frames]
    at = pl.ds(group[0], len(group))
    for place, (start, count) in enumerate(rows):
        row = 0 if start is None else pl.multiple_of(r.meta[start], 16)
        ref = getattr(r, "out%d_%d" % (place, number))
        copies.out(scratch.at[at, pl.ds(row, count), :], ref)


def decoder_first(meta, lens, u3, w3, bias, clips, frames, dim):
    wide = (dim, clips * frames)
    taps3 = taps_of(w3)

    def body(r, copies):
        loads = load_pieces(copies, w3, r.w3, r.meta, r.t3)
        for number, group in enumerate(groups_of(clips)):
            here = span(group, frames)
            inside = mask_of(r.lens, group, frames)
            waits = waits_of(w3, loads) if number == 0 else ()
            first = conv_forward(r.t3, r.u3, group, frames, taps3, 0, waits) + r.bias[:, 3:4]
            r.first[:, here] = first
            r.u4[:, here] = (inside * elu(first)).astype(BF16)

    return run(
        "decoder_first",
        body,
        meta,
        lens,
        {"u3": u3, "bias": bias},
        {"w3": arrays_of(w3)},
        {"first": (wide, F32, True), "u4": (wide, BF16, True)},
        {"t3": ((taps3, dim, dim), BF16)},
        len(w3),
        2 * taps3 * dim * dim * clips * frames,
    )


def decoder_rest(meta, lens, first, u4, w45, bias, out_rows, clips, frames, dim):
    wide = (dim, clips * frames)
    taps4 = taps_of(w45) - 1
    outs = {"u5": (wide, BF16, True)}
    outs["t45"] = ((taps4 + 1, dim, dim), BF16, True)
    outs.update(clip_outs(out_rows, clips, frames))

    def body(r, copies):
        loads = load_pieces(copies, w45, r.w45, r.meta, r.t45)
        wait_all(loads)
        for number, group in enumerate(groups_of(clips)):
            here = span(group, frames)
            inside = mask_of(r.lens, group, frames)
            second = conv_forward(r.t45, r.u4, group, frames, taps4) + r.bias[:, 4:5]
            r.u5[:, here] = (inside * elu(second)).astype(BF16)
            third = conv_forward(r.t45, r.u5, group, frames, 1, taps4) + r.bias[:, 5:6]
            result = (inside * (r.first[:, here] + third)).astype(BF16)
            put_clips(copies, r, r.work, number, group, result, frames, out_rows)

    return run(
        "decoder_rest",
        body,
        meta,
        lens,
        {"first": first, "u4": u4, "bias": bias},
        {"w45": arrays_of(w45)},
        outs,
        {"work": ((clips, dim, frames), BF16)},
        len(w45) + len(out_rows) * len(groups_of(clips)),
        2 * (taps4 + 1) * dim * dim * clips * frames,
    )


def waits_of(pieces, loads):
    waits = {}
    for piece, load in zip(pieces, loads):
        waits.setdefault(piece.target, []).append(load)
    return waits


class Rows:
    def __init__(self, dim, paired):
        self.dim = dim
        self.paired = paired
        self.count = 2 if paired else 1
        self.height = dim // self.count

    def outs(self, columns):
        return {
            "sums%d" % number: ((self.height, columns), BF16, self.paired)
            for number in range(self.count)
        }

    def scratch(self, columns):
        return {} if self.paired else {"sums": ((self.dim, columns), BF16)}

    def put(self, r, copies, at, value):
        if not self.paired:
            r.sums[:, at] = value
            copies.out(r.sums.at[:, at], r.sums0.at[:, at])
            return
        quarter = self.dim // 4
        run_of = quarter // 4
        first = r.meta[1] == 0
        for half in range(2):
            for block in range(4):
                row = half * 2 * quarter + block * run_of
                zero = value[row : row + run_of]
                one = value[row + quarter : row + quarter + run_of]
                row = (block * 2 + half) * run_of
                r.sums0[row : row + run_of, at] = jnp.where(first, zero, one)
                r.sums1[row : row + run_of, at] = jnp.where(first, one, zero)


def weight_grads(r, copies, rows, g, u, taps, offset, clips, frames, dim):
    for tap in range(taps):
        step = taps // 2 - tap
        left = g[...]
        if step != 0:
            for clip in range(clips):
                at = span((clip,), frames)
                r.work[:, at] = shifted(g[:, at], step)
            left = r.work[...]
        value = lax.dot_general(
            left, u[...], (((1,), (1,)), ((), ())), preferred_element_type=F32
        )
        rows.put(r, copies, slice(offset, offset + dim), value.astype(BF16))
        offset += dim
    total = jnp.sum(g[...].astype(F32), axis=1, keepdims=True)
    total = jnp.broadcast_to(total, (dim, 128)).astype(BF16)
    rows.put(r, copies, slice(offset, offset + 128), total)
    return offset + 128


def decoder_backward(
    meta, lens, cotangent, u3, u4, u5, t45, taps3, rows, clips, frames, dim
):
    wide = (dim, clips * frames)
    taps4 = t45.shape[0] - 1
    columns = (taps3 + taps4 + 1) * dim + 3 * 128

    def body(r, copies):
        loads = load_clips(copies, cotangent, r.cot, r.meta, r.clips, groups_of(clips))
        late = copies.start(r.u3, r.s3)
        for group, begun in zip(groups_of(clips), loads):
            here = span(group, frames)
            wait_all(begun)
            inside = mask_of(r.lens, group, frames)
            out = lanes([r.clips[clip] for clip in group])
            out = jnp.where(inside > 0, out, jnp.zeros((), BF16))
            r.g5[:, here] = out
            back = conv_backward(r.t45, r.g5, group, frames, 1, taps4)
            r.g4[:, here] = (back * inside * slope_of(r.u5[:, here])).astype(BF16)
            back = conv_backward(r.t45, r.g4, group, frames, taps4)
            total = out.astype(F32) + back * inside * slope_of(r.u4[:, here])
            r.s_g3[:, here] = total.astype(BF16)
            copies.out(r.s_g3.at[:, here], r.g3.at[:, here])
        sizes = (clips, frames, dim)
        at = weight_grads(r, copies, rows, r.g5, r.u5, 1, 0, *sizes)
        at = weight_grads(r, copies, rows, r.g4, r.u4, taps4, at, *sizes)
        late.wait()
        weight_grads(r, copies, rows, r.s_g3, r.s3, taps3, at, *sizes)

    return run(
        "decoder_backward",
        body,
        meta,
        lens,
        {"u4": u4, "u5": u5, "t45": t45},
        {"cot": arrays_of(cotangent), "u3": u3},
        {"g3": (wide, BF16, False), **rows.outs(columns)},
        {
            "clips": ((clips, dim, frames), BF16),
            "s3": (wide, BF16),
            "g5": (wide, BF16),
            "g4": (wide, BF16),
            "s_g3": (wide, BF16),
            "work": (wide, BF16),
            **rows.scratch(columns),
        },
        (len(cotangent) + 1) * len(groups_of(clips))
        + 1
        + rows.count * (taps3 + taps4 + 4),
        2 * (taps3 + 2 * taps4 + 2) * dim * dim * clips * frames,
    )


def encoder_forward(
    meta, lens, mask, tokens, w012, bias, q0, q1, ahead, g3, clips, frames, dim
):
    wide = (dim, clips * frames)
    groups = groups_of(clips)
    taps0 = taps_of(w012[0])
    weights = [piece for layer in w012 for piece in layer]
    places = (0, taps0, taps0 + 1)

    def body(r, copies):
        loads = load_clips(copies, tokens, r.tokens, r.meta, r.clips, groups[:1])
        begun, refs = [], iter(r.w012)
        for place, layer in zip(places, w012):
            target = r.t.at[pl.ds(place, taps_of(layer))]
            begun.append([p.load(copies, next(refs), r.meta, target) for p in layer])
        loads += load_clips(copies, tokens, r.tokens, r.meta, r.clips, groups[1:])
        late = [copies.start(r.q0, r.s_q0), copies.start(r.q1, r.s_q1)]
        copies.open += load_pieces(copies, ahead, r.ahead, r.meta, r.next)
        copies.out(r.g3, r.g3_near)
        for number, group in enumerate(groups):
            here = span(group, frames)
            wait_all(loads[number])
            inside = mask_of(r.lens, group, frames)
            start = inside * lanes([r.clips[clip] for clip in group]).astype(F32)
            r.s0[:, here] = elu(start).astype(BF16)
            copies.out(r.s0.at[:, here], r.u0.at[:, here])
            if number == 0:
                wait_all(begun[0])
            first = conv_forward(r.t, r.s0, group, frames, taps0) + r.bias[:, 0:1]
            r.s1[:, here] = (inside * elu(first)).astype(BF16)
            copies.out(r.s1.at[:, here], r.u1.at[:, here])
            if number == 0:
                wait_all(begun[1])
                wait_all(begun[2])
            second = conv_forward(r.t, r.s1, group, frames, 1, taps0) + r.bias[:, 1:2]
            r.u2_near[:, here] = elu(inside * (start + second)).astype(BF16)
            copies.out(r.u2_near.at[:, here], r.u2.at[:, here])
            latent = conv_forward(r.t, r.u2_near, group, frames, taps0, taps0 + 1)
            latent = latent + r.bias[:, 2:3]
            if number == 0:
                wait_all(late)
            double = 2.0 * counted_of(r.lens, r.mask, group, frames)
            miss = r.s_q0[:, here].astype(F32) - latent
            r.gq0[:, here] = (double * miss).astype(BF16)
            r.gq1[:, here] = (double * (miss + r.s_q1[:, here].astype(F32))).astype(BF16)

    return run(
        "encoder_forward",
        body,
        meta,
        lens,
        {"mask": mask, "bias": bias},
        {
            "tokens": arrays_of(tokens),
            "w012": arrays_of(weights),
            "q0": q0,
            "q1": q1,
            "ahead": arrays_of(ahead),
            "g3": g3,
        },
        {
            "u0": (wide, BF16, False),
            "u1": (wide, BF16, False),
            "u2": (wide, BF16, False),
            "u2_near": (wide, BF16, True),
            "gq0": (wide, BF16, True),
            "gq1": (wide, BF16, True),
            "next": ((taps_of(ahead), dim, dim), BF16, True),
            "g3_near": (wide, BF16, True),
        },
        {
            "clips": ((clips, dim, frames), BF16),
            "t": ((2 * taps0 + 1, dim, dim), BF16),
            **{name: (wide, BF16) for name in ("s0", "s1", "s_q0", "s_q1")},
        },
        (len(tokens) + 3) * len(groups) + len(ahead) + len(weights) + 3,
        2 * (2 * taps0 + 1) * dim * dim * clips * frames,
    )


def latent_backward(
    meta, lens, ids, g3, t3, gq0, gq1, u2, taps2, codes, ahead, rows, clips, frames, dim
):
    wide = (dim, clips * frames)
    taps3 = t3.shape[0]
    columns = taps2 * dim + 128 + LEVELS * codes

    def body(r, copies):
        copies.open += load_pieces(copies, ahead, r.ahead, r.meta, r.next)
        for group in groups_of(clips):
            here = span(group, frames)
            inside = mask_of(r.lens, group, frames)
            back = conv_backward(r.t3, r.g3, group, frames, taps3)
            extra = BETA * r.gq1[:, here].astype(F32)
            r.g2[:, here] = (back * inside - extra).astype(BF16)
        sizes = (clips, frames, dim)
        offset = weight_grads(r, copies, rows, r.g2, r.u2, taps2, 0, *sizes)
        for level, grad in enumerate((r.gq0, r.gq1)):
            values = []
            for group in range(dim // GW):
                at = slice(group * GW, (group + 1) * GW)
                one_hot(r.ids, r.hot, level, group, clips, frames, dim)
                values.append(
                    lax.dot_general(
                        grad[at, :],
                        r.hot[...],
                        (((1,), (1,)), ((), ())),
                        preferred_element_type=F32,
                    ).astype(BF16)
                )
            value = jnp.concatenate(values, axis=0)
            rows.put(r, copies, slice(offset, offset + codes), value)
            offset += codes

    return run(
        "latent_backward",
        body,
        meta,
        lens,
        {"ids": ids, "g3": g3, "t3": t3, "gq0": gq0, "gq1": gq1, "u2": u2},
        {"ahead": arrays_of(ahead)},
        {
            "g2": (wide, BF16, True),
            "next": ((taps_of(ahead), dim, dim), BF16, True),
            **rows.outs(columns),
        },
        {
            "hot": ((codes, clips * frames), BF16),
            "work": (wide, BF16),
            **rows.scratch(columns),
        },
        len(ahead) + rows.count * (taps2 + 1 + LEVELS),
        2 * ((taps3 + taps2) * dim + LEVELS * codes) * dim * clips * frames,
    )


def encoder_backward(meta, lens, g2, u2, u1, u0, t, taps0, ahead, clips, frames, dim):
    wide = (dim, clips * frames)

    def body(r, copies):
        second = copies.start(r.u2, r.s2)
        first = copies.start(r.u1, r.u1_near)
        copies.out(r.u0, r.u0_near)
        copies.open += load_pieces(copies, ahead, r.ahead, r.meta, r.next)
        for number, group in enumerate(groups_of(clips)):
            here = span(group, frames)
            inside = mask_of(r.lens, group, frames)
            back = conv_backward(r.t, r.g2, group, frames, taps0, 1)
            if number == 0:
                second.wait()
            r.g1[:, here] = (back * inside * slope_of(r.s2[:, here])).astype(BF16)
            back = conv_backward(r.t, r.g1, group, frames, 1)
            if number == 0:
                first.wait()
            r.g0[:, here] = (back * inside * slope_of(r.u1_near[:, here])).astype(BF16)

    names = ("g1", "g0", "u1_near", "u0_near")
    return run(
        "encoder_backward",
        body,
        meta,
        lens,
        {"g2": g2, "t": t},
        {"u2": u2, "u1": u1, "u0": u0, "ahead": arrays_of(ahead)},
        {
            **{name: (wide, BF16, True) for name in names},
            "next": ((taps_of(ahead), dim, dim), BF16, True),
        },
        {"s2": (wide, BF16)},
        len(ahead) + 3,
        2 * (taps0 + 1) * dim * dim * clips * frames,
    )


def encoder_grads(meta, lens, g0, u0, g1, u1, taps0, rows, clips, frames, dim):
    columns = (taps0 + 1) * dim + 2 * 128

    def body(r, copies):
        sizes = (clips, frames, dim)
        at = weight_grads(r, copies, rows, r.g0, r.u0, taps0, 0, *sizes)
        weight_grads(r, copies, rows, r.g1, r.u1, 1, at, *sizes)

    return run(
        "encoder_grads",
        body,
        meta,
        lens,
        {"g0": g0, "u0": u0, "g1": g1, "u1": u1},
        {},
        rows.outs(columns),
        {"work": ((dim, clips * frames), BF16), **rows.scratch(columns)},
        1 + rows.count * (taps0 + 3),
        2 * (taps0 + 1) * dim * dim * clips * frames,
    )


def tokens_backward(meta, lens, g0, u0, g1, t, out_rows, clips, frames, dim):
    taps0 = t.shape[0]

    def body(r, copies):
        for number, group in enumerate(groups_of(clips)):
            here = span(group, frames)
            inside = mask_of(r.lens, group, frames)
            back = conv_backward(r.t, r.g0, group, frames, taps0)
            total = r.g1[:, here].astype(F32) + back * inside * slope_of(r.u0[:, here])
            total = (inside * total).astype(BF16)
            put_clips(copies, r, r.work, number, group, total, frames, out_rows)

    result = run(
        "tokens_backward",
        body,
        meta,
        lens,
        {"g0": g0, "g1": g1, "u0": u0, "t": t},
        {},
        clip_outs(out_rows, clips, frames),
        {"work": ((clips, dim, frames), BF16)},
        len(out_rows) * len(groups_of(clips)),
        2 * taps0 * dim * dim * clips * frames,
    )
    return clip_results(result, out_rows, clips)


def unpack(meta, pieces, blocks, half):
    outs = []
    for taps, width, has_bias in blocks:
        outs.append(struct((taps, half, width), F32))
        if has_bias:
            outs.append(struct((1, half), F32))

    def body(meta_ref, mine_ref, other_ref, *refs):
        take = iter(refs)
        first = meta_ref[1] == 0

        def columns(at):
            mine, other = mine_ref[:, at], other_ref[:, at]
            return jnp.concatenate(
                [jnp.where(first, mine, other), jnp.where(first, other, mine)], axis=0
            ).astype(F32)

        offset = 0
        for taps, width, has_bias in blocks:
            out = next(take)
            for tap in range(taps):
                out[tap] = columns(slice(offset, offset + width))
                offset += width
            if has_bias:
                next(take)[...] = columns(slice(offset, offset + 128)).T[0:1]
                offset += 128

    return pl.pallas_call(
        body,
        out_shape=tuple(outs),
        in_specs=[SMEM, VMEM, VMEM],
        out_specs=tuple(VMEM for _ in outs),
        compiler_params=pltpu.CompilerParams(vmem_limit_bytes=LIMIT),
    )(meta, *pieces)


def in_three(array, rows, columns):
    terms = []
    for _ in range(3):
        term = lax.reduce_precision(array, exponent_bits=8, mantissa_bits=7)
        terms.append(term.astype(BF16).reshape(-1))
        array = array - term
    terms = jnp.concatenate(terms)
    return jnp.pad(terms, (0, rows * columns - terms.size)).reshape(1, rows, columns)


def from_three(block, shape):
    size = shape[0] * shape[1]
    terms = block.reshape(-1)[: 3 * size].reshape((3,) + shape).astype(F32)
    return (terms[0] + terms[1]) + terms[2]


class Pairs:
    BITS = {"core": 1, "x": 2, "zl": 4, "zh": 8}

    def __init__(self, rows, clips):
        self.chan = lax.axis_index("chan")
        self.dp = lax.axis_index("dp")
        self.core = self.bit("core")
        x = self.bit("x")
        other = (1 - self.chan) * rows
        piece = rows // 4
        here = [(self.core, x), (self.core, 1 - x), (1 - self.core, x), (1 - self.core, 1 - x)]
        self.piece = (self.core * 2 + x) * piece
        self.meta = jnp.stack(
            [self.chan, self.core, self.chan * rows, other]
            + [other + (c * 2 + b) * piece for c, b in here]
            + [self.chan * clips]
            + [other + self.core * 2 * piece, other + (1 - self.core) * 2 * piece]
        ).astype(jnp.int32)

    def bit(self, name):
        if name == "chan":
            return self.chan
        return (self.dp & self.BITS[name]) // self.BITS[name]

    def swap(self, value, name):
        if name == "chan":
            return lax.ppermute(value, "chan", [(0, 1), (1, 0)])
        mask = self.BITS[name]
        return lax.ppermute(value, "dp", [(i, i ^ mask) for i in range(16)])

    def swap_by_core(self, value, names):
        if names[0] == names[1]:
            return self.swap(value, names[0])
        pairs = []
        for place in range(32):
            name = names[(place // 2) & 1]
            pairs.append((place, place ^ (1 if name == "chan" else 2 * self.BITS[name])))
        return lax.ppermute(value, ("dp", "chan"), pairs)

    def bit_by_core(self, names):
        return jnp.where(self.core == 0, self.bit(names[0]), self.bit(names[1]))

    def piece_of(self, own):
        return lax.dynamic_slice_in_dim(own, self.piece, own.shape[1] // 4, 1)

    def half_of(self, own):
        half = own.shape[1] // 2
        return lax.dynamic_slice_in_dim(own, self.core * half, half, 1)

    def spread(self, near):
        far = self.swap(near, "x")
        return near, far, self.swap(near, "core"), self.swap(far, "core")

    def ordered(self, own, came):
        first = self.chan == 0
        return jnp.concatenate([jnp.where(first, own, came), jnp.where(first, came, own)])

    @property
    def bits(self):
        names = list(zip(*Reduction.ORDERS))
        gather = [[n for n in reversed(order) if n != "chan"] for order in Reduction.ORDERS]
        names += list(zip(*gather))
        return jnp.stack([self.bit_by_core(pair) for pair in names]).astype(jnp.int32)

    def start(self, grads):
        kept, sent = grads
        return Reduction(self, kept, self.swap(sent, "core"))


class Reduction:
    ORDERS = (("x", "zl", "chan", "zh"), ("zl", "x", "chan", "zh"))

    def __init__(self, links, kept, came):
        self.links = links
        gather = [[name for name in reversed(order) if name != "chan"] for order in self.ORDERS]
        self.steps = list(zip(*self.ORDERS)) + list(zip(*gather)) + [("core", "core")]
        self.at = 0
        self.terms = [kept]
        self.came = came
        self.value = None

    @property
    def done(self):
        return self.at == len(self.steps)

    @property
    def result(self):
        return [self.value, self.came]

    def operands(self):
        halvings = len(self.ORDERS[0])
        if self.at > halvings:
            return [self.value, self.came]
        self.terms.append(self.came)
        blocks = []
        for number, term in enumerate(self.terms):
            cuts = min(self.at + 1, halvings) - max(number - 1, 0)
            blocks.append(term.reshape((2,) * cuts + (-1, term.shape[-1])))
        return blocks

    def sent_shape(self, operands):
        rows, columns = operands[0].shape[-2:]
        return (rows, columns) if self.at <= len(self.ORDERS[0]) else (2, rows, columns)

    def fill(self, refs, out, bits):
        halvings = len(self.ORDERS[0])
        if self.at > halvings:
            place = bits[self.at - 1]
            out[place] = refs[0][...]
            out[1 - place] = refs[1][...]
            return
        sums = None
        for number, ref in enumerate(refs):
            first = max(number - 1, 0)
            where = [bits[cut] for cut in range(first, min(self.at + 1, halvings))]
            if self.at < halvings:
                where[-1] = 1 - where[-1]
            piece = ref[tuple(where)].astype(F32) if where else ref[...].astype(F32)
            sums = piece if sums is None else sums + piece
        out[...] = sums.astype(BF16)

    def send(self, sent):
        names = self.steps[self.at]
        sent = sent.reshape(-1, sent.shape[-1])
        if self.at >= len(self.ORDERS[0]):
            self.value = sent
        self.came = self.links.swap_by_core(sent, names)
        self.at += 1


def advance(after, *reductions):
    came = lax.optimization_barrier((tuple(r.came for r in reductions), tuple(after)))[0]
    arrays, counts, shapes = [], [], []
    for reduction, array in zip(reductions, came):
        reduction.came = array
        operands = reduction.operands()
        counts.append(len(operands))
        arrays += [held(operand) for operand in operands]
        shapes.append(pltpu.VMEM(reduction.sent_shape(operands), BF16))

    def body(bits_ref, *refs):
        taken = 0
        for number, (reduction, count) in enumerate(zip(reductions, counts)):
            out = refs[len(arrays) + number]
            reduction.fill(refs[taken : taken + count], out, bits_ref)
            taken += count

    sent = pl.pallas_call(
        body,
        out_shape=tuple(shapes),
        in_specs=[SMEM] + [VMEM] * len(arrays),
        out_specs=tuple(VMEM for _ in shapes),
        compiler_params=pltpu.CompilerParams(vmem_limit_bytes=8 * MIB),
        cost_estimate=pl.CostEstimate(
            flops=COVER["advance"], bytes_accessed=COVER["advance"], transcendentals=0
        ),
    )(reductions[0].links.bits, *arrays)
    for reduction, rows in zip(reductions, sent):
        reduction.send(rows)
    return list(sent)


def on_pairs(
    tokens,
    lengths,
    frame_mask,
    code_ids,
    cotangent,
    weights,
    biases,
    codebook,
):
    chan = 2
    rows = tokens.shape[1]
    frames = tokens.shape[2]
    dim = rows * chan
    clips = tokens.shape[0] // chan
    codes = codebook.shape[2]
    sizes = (clips, frames, dim)
    links = Pairs(rows, clips)
    meta = links.meta
    mine = functools.partial(
        lax.dynamic_slice_in_dim, start_index=links.chan * clips, slice_size=clips, axis=0
    )
    others = functools.partial(
        lax.dynamic_slice_in_dim, start_index=(1 - links.chan) * clips, slice_size=clips, axis=0
    )
    taps = [w.shape[0] for w in weights]
    own, other, pieces, halves = 2, 3, (4, 5, 6, 7), (9, 10)

    split = (taps[3] + 1) // 2
    lens = mine(lengths)
    mask = mine(frame_mask)
    ids = mine(code_ids).reshape(-1, frames)
    bias = jnp.stack(biases + (jnp.zeros_like(biases[0]),) * 2)
    first_pieces = lax.optimization_barrier(
        (
            links.piece_of(codebook),
            links.piece_of(weights[3][:split]),
            links.half_of(weights[3][split:]),
        )
    )
    near_book, near3a, near3b = (links.swap(piece, "chan") for piece in first_pieces)
    dec = jnp.concatenate([weights[4], weights[5]])
    enc = jnp.concatenate([weights[0], weights[1], weights[2]])
    far_book = links.spread(near_book)
    dec_piece = jnp.concatenate([links.piece_of(dec), in_three(bias, rows // 4, dim)])
    dec_piece = tie(dec_piece, near_book)
    near45 = links.swap(dec_piece, "chan")
    far3a = links.spread(near3a)
    enc_piece = tie(links.piece_of(enc), near_book)
    near012 = links.swap(enc_piece, "chan")
    cot_send = tie(others(tie(cotangent, near_book)), near3a, dec_piece, enc_piece)
    cot_other = links.swap(cot_send, "chan")
    book = [Piece(codebook, own)] + [Piece(a, s) for a, s in zip(far_book, pieces)]
    found = lookup(meta, lens, tie(ids, cot_send), book, *sizes)
    tok_send = tie(others(tokens), found.u3)
    tok_other = links.swap(tok_send, "chan")
    near3b, near45 = tie((near3b, near45), found.u3)
    far3b = near3b, links.swap(near3b, "core")
    bias_came = from_three(near45[taps[4] + taps[5] :], bias.shape)
    bias = links.ordered(bias.T, bias_came.T)
    w3 = [Piece(weights[3], own, 0, 0, split)]
    w3 += [Piece(a, s) for a, s in zip(far3a, pieces)]
    w3 += [Piece(weights[3], own, split, split, taps[3] - split)]
    w3 += [Piece(a, s, 0, split) for a, s in zip(far3b, halves)]
    far45_x = links.swap(near45, "x")
    dec_first = decoder_first(
        meta, lens, found.u3, w3, bias, *sizes
    )
    near45, far45_x = tie((near45, far45_x), dec_first.u4)
    far45 = near45, far45_x, links.swap(near45, "core"), links.swap(far45_x, "core")
    w45 = [Piece(weights[4], own), Piece(weights[5], own, 0, taps[4])]
    w45 += [Piece(a, s, 0, 0, taps[4] + taps[5]) for a, s in zip(far45, pieces)]
    out_rows = ((own, rows), (other, rows))
    dec_out = decoder_rest(
        meta, lens, dec_first.first, dec_first.u4, w45, bias, out_rows, *sizes
    )
    near012 = tie(near012, dec_out.u5)
    far012_x = links.swap(near012, "x")
    rows_of = Rows(dim, True)
    cot = [Piece(cotangent, own, clip=8, count=clips)]
    cot.append(Piece(tie(cot_other, near012), other))
    dec_back = decoder_backward(
        meta,
        lens,
        cot,
        found.u3_far,
        dec_first.u4,
        dec_out.u5,
        dec_out.t45,
        taps[3],
        rows_of,
        *sizes,
    )
    near012, far012_x = tie((near012, far012_x), dec_back.g3)
    far012 = near012, far012_x, links.swap(near012, "core"), links.swap(far012_x, "core")

    def enc_pieces(which):
        listed = []
        place = 0
        for number in which:
            listed.append(Piece(weights[number], own, 0, place))
            place += taps[number]
        start = sum(taps[: which[0]])
        listed += [Piece(a, s, start, 0, place) for a, s in zip(far012, pieces)]
        return listed

    red_a = links.start([dec_back.sums0, tie(dec_back.sums1, tok_other)])
    out_own, out_send = clip_results(dec_out, out_rows, clips)
    out_send[0] = tie(out_send[0], tok_other)
    out_came = [links.swap(out_send[0], "chan")]
    tok = [Piece(tokens, own, clip=8, count=clips)]
    tok.append(Piece(tie(tok_other, dec_back.g3, out_send[0]), other))
    enc_out = encoder_forward(
        meta,
        lens,
        mask,
        tok,
        [enc_pieces([0]), enc_pieces([1]), enc_pieces([2])],
        bias,
        found.q0,
        found.q1,
        w3,
        dec_back.g3,
        *sizes,
    )
    sent = advance([enc_out.u2], red_a)
    out_came.append(links.swap(tie(out_send[1], *sent), "chan"))
    lat = latent_backward(
        meta,
        lens,
        ids,
        tie(enc_out.g3_near, out_came[0], *sent),
        enc_out.next,
        enc_out.gq0,
        enc_out.gq1,
        enc_out.u2_near,
        taps[2],
        codes,
        enc_pieces([1, 2]),
        rows_of,
        *sizes,
    )
    red_c = links.start([lat.sums0, lat.sums1])
    sent = advance([lat.g2], red_a)
    enc_back = encoder_backward(
        meta,
        lens,
        lat.g2,
        tie(enc_out.u2, out_came[1], *sent),
        enc_out.u1,
        enc_out.u0,
        lat.next,
        taps[0],
        enc_pieces([0]),
        *sizes,
    )
    sent = advance([enc_back.g0], red_c)
    enc_sums = encoder_grads(
        meta,
        lens,
        tie(enc_back.g0, *sent),
        enc_back.u0_near,
        enc_back.g1,
        enc_back.u1_near,
        taps[0],
        rows_of,
        *sizes,
    )
    red_d = links.start([enc_sums.sums0, enc_sums.sums1])
    sent = advance([enc_sums.sums0], red_a)
    grad_own, grad_other = tokens_backward(
        meta,
        lens,
        tie(enc_back.g0, *sent),
        enc_back.u0_near,
        enc_back.g1,
        enc_back.next,
        out_rows,
        *sizes,
    )
    sent = advance(grad_other, red_a, red_c, red_d)
    grad_came = []
    shapes = {
        red_a: [(1, dim, True), (taps[4], dim, True), (taps[3], dim, True)],
        red_c: [(taps[2], dim, True), (LEVELS, codes, False)],
        red_d: [(taps[0], dim, True), (1, dim, True)],
    }
    results = {}
    while not red_d.done:
        for half, (begin, end) in enumerate(GRAD_SLOTS):
            if red_d.at == begin:
                grad_came.append(links.swap(tie(grad_other[half], *sent), "chan"))
        for half, (begin, end) in enumerate(GRAD_SLOTS):
            if red_d.at == end:
                sent = list(sent) + [grad_came[half]]
        active = [r for r in (red_a, red_c, red_d) if not r.done]
        ready = [r for r in (red_a, red_c) if r.done and r not in results]
        for r in ready:
            mine_rows, other_rows = r.result
            results[r] = unpack(meta, [tie(mine_rows, *sent), other_rows], shapes[r], rows)
            sent = list(sent) + list(results[r][:1])
        if red_d.at == OUT_SLOTS[0]:
            came = jnp.concatenate(tie(out_came, *sent))
            output = links.ordered(jnp.concatenate(out_own), came)
            sent = list(sent) + [output]
        if red_d.at == OUT_SLOTS[1]:
            came = jnp.concatenate(tie(grad_came, *sent)).astype(F32)
            tokens_grad = links.ordered(jnp.concatenate(grad_own).astype(F32), came)
            sent = list(sent) + [tokens_grad]
        sent = advance(sent, *active)
    for r in (red_c, red_d):
        if r not in results:
            results[r] = unpack(meta, r.result, shapes[r], rows)
    a, c, d = results[red_a], results[red_c], results[red_d]
    w_grads = [d[0], d[2], c[0], a[4], a[2], a[0]]
    b_grads = [v.reshape(rows) for v in (d[1], d[3], c[1], a[5], a[3], a[1])]
    grads = [g for pair in zip(w_grads, b_grads) for g in pair]
    return (output, tokens_grad, *grads, c[2])


def on_others(
    tokens,
    lengths,
    frame_mask,
    code_ids,
    cotangent,
    weights,
    biases,
    codebook,
):
    chan = lax.axis_size("chan")
    place = lax.axis_index("chan")
    rows = tokens.shape[1]
    frames = tokens.shape[2]
    dim = rows * chan
    clips = tokens.shape[0] // chan
    codes = codebook.shape[2]
    sizes = (clips, frames, dim)
    meta = jnp.zeros((9,), jnp.int32)
    mine = functools.partial(
        lax.dynamic_slice_in_dim, start_index=place * clips, slice_size=clips, axis=0
    )
    taps = [w.shape[0] for w in weights]

    def gathered(*arrays):
        return [Piece(lax.all_gather(jnp.concatenate(arrays), "chan", axis=1, tiled=True))]

    def part(pieces, start, count):
        return [Piece(pieces[0].array, None, start, 0, count)]

    def clips_in(array):
        return [Piece(lax.all_to_all(array, "chan", 0, 1, tiled=True))]

    def clips_out(array):
        return lax.all_to_all(array, "chan", 1, 0, tiled=True)

    def reduced(grads):
        part = lax.psum_scatter(grads.astype(F32), "chan", scatter_dimension=0, tiled=True)
        return lax.psum(part, "dp")

    def columns(total, offset, count, width):
        block = total[:, offset : offset + count * width].reshape(rows, count, width)
        return jnp.transpose(block, (1, 0, 2))

    bias = jnp.stack(biases + (jnp.zeros_like(biases[0]),) * 2, axis=1)
    bias = lax.all_gather(bias, "chan", axis=0, tiled=True)
    lens = mine(lengths)
    mask = mine(frame_mask)
    ids = mine(code_ids).reshape(-1, frames)
    w3 = gathered(weights[3])
    w45 = gathered(weights[4], weights[5])
    w012 = gathered(weights[0], weights[1], weights[2])
    rows_of = Rows(dim, False)
    out_rows = ((None, dim),)
    found = lookup(meta, lens, ids, gathered(codebook), *sizes)
    dec_first = decoder_first(meta, lens, found.u3, w3, bias, *sizes)
    dec_out = decoder_rest(
        meta, lens, dec_first.first, dec_first.u4, w45, bias, out_rows, *sizes
    )
    dec_back = decoder_backward(
        meta,
        lens,
        clips_in(cotangent),
        found.u3_far,
        dec_first.u4,
        dec_out.u5,
        dec_out.t45,
        taps[3],
        rows_of,
        *sizes,
    )
    enc_out = encoder_forward(
        meta,
        lens,
        mask,
        clips_in(tokens),
        [
            part(w012, 0, taps[0]),
            part(w012, taps[0], taps[1]),
            part(w012, taps[0] + taps[1], taps[2]),
        ],
        bias,
        found.q0,
        found.q1,
        w3,
        dec_back.g3,
        *sizes,
    )
    lat = latent_backward(
        meta,
        lens,
        ids,
        enc_out.g3_near,
        enc_out.next,
        enc_out.gq0,
        enc_out.gq1,
        enc_out.u2_near,
        taps[2],
        codes,
        part(w012, taps[0], 1 + taps[2]),
        rows_of,
        *sizes,
    )
    enc_back = encoder_backward(
        meta,
        lens,
        lat.g2,
        enc_out.u2,
        enc_out.u1,
        enc_out.u0,
        lat.next,
        taps[0],
        part(w012, 0, taps[0]),
        *sizes,
    )
    enc_sums = encoder_grads(
        meta,
        lens,
        enc_back.g0,
        enc_back.u0_near,
        enc_back.g1,
        enc_back.u1_near,
        taps[0],
        rows_of,
        *sizes,
    )
    ((grad,),) = tokens_backward(
        meta,
        lens,
        enc_back.g0,
        enc_back.u0_near,
        enc_back.g1,
        enc_back.next,
        out_rows,
        *sizes,
    )
    ((out,),) = clip_results(dec_out, out_rows, clips)
    a, c, d = (reduced(x.sums0) for x in (dec_back, lat, enc_sums))
    placed = (
        (d, 0, taps[0]),
        (d, taps[0] * dim + 128, 1),
        (c, 0, taps[2]),
        (a, (1 + taps[4]) * dim + 256, taps[3]),
        (a, dim + 128, taps[4]),
        (a, 0, 1),
    )
    grads = []
    for total, start, count in placed:
        grads.append(columns(total, start, count, dim))
        grads.append(total[:, start + count * dim])
    books = columns(c, taps[2] * dim + 128, LEVELS, codes)
    return (clips_out(out), clips_out(grad).astype(F32), *grads, books)


def on_device(step, tokens, lengths, frame_mask, code_ids, cotangent, *params):
    weights, biases = params[0:12:2], params[1:12:2]
    return step(
        tokens, lengths, frame_mask, code_ids, cotangent, weights, biases, params[12]
    )


def solution(mesh):
    paired = mesh.shape["chan"] == 2 and mesh.shape["dp"] == 16
    weight = P(None, "chan", None)
    vector = P("chan")
    clip_rows = P("dp", "chan", None)
    in_specs = (
        (clip_rows, P("dp"), P("dp", None), P("dp", None, None), clip_rows)
        + (weight, vector) * 6
        + (weight,)
    )
    out_specs = (clip_rows, clip_rows) + (weight, vector) * 6 + (weight,)
    return jax.shard_map(
        functools.partial(on_device, on_pairs if paired else on_others),
        mesh=mesh,
        in_specs=in_specs,
        out_specs=out_specs,
        check_vma=False,
    )
```

```python
import functools
import types

import jax
import jax.numpy as jnp
from jax import lax
from jax.experimental import pallas as pl
from jax.experimental.pallas import tpu as pltpu
from jax.sharding import PartitionSpec as P

LEVELS = 2
GW = 256
BETA = 0.25
F32 = jnp.float32
BF16 = jnp.bfloat16
MIB = 1024 * 1024
LIMIT = 28 * MIB
GRAD_SLOTS = ((1, 3), (2, 5))
OUT_SLOTS = (2, 6)
A_EARLY = False
COVER = {
    "lookup": 0.01,
    "decoder_first": 0.01,
    "decoder_rest": 0.01,
    "decoder_backward": 0.01,
    "encoder_forward": 10,
    "latent_backward": 10,
    "encoder_backward": 10,
    "encoder_grads": 10,
    "tokens_backward": 10,
    "advance": 0,
}

ANY = pl.BlockSpec(memory_space=pl.ANY)
VMEM = pl.BlockSpec(memory_space=pltpu.VMEM)
SMEM = pl.BlockSpec(memory_space=pltpu.SMEM)


def elu(value):
    return jnp.where(value > 0, value, jnp.exp(jnp.minimum(value, 0.0)) - 1.0)


def slope_of(activated):
    act = activated.astype(F32)
    return jnp.where(act > 0, 1.0, 1.0 + act)


def shifted(value, step):
    if step == 0:
        return value
    edge = jnp.zeros((value.shape[0], abs(step)), value.dtype)
    if step > 0:
        return jnp.concatenate([value[:, step:], edge], axis=1)
    return jnp.concatenate([edge, value[:, :step]], axis=1)


def lanes(blocks):
    return blocks[0] if len(blocks) == 1 else jnp.concatenate(blocks, axis=1)


def tie(value, *earlier):
    earlier = [array for array in earlier if array is not None]
    if not earlier:
        return value
    return lax.optimization_barrier((value, tuple(earlier)))[0]


def held(array):
    return pltpu.with_memory_space_constraint(array, pltpu.VMEM)


def struct(shape, dtype):
    return jax.ShapeDtypeStruct(shape, dtype)


class Copies:
    def __init__(self, sems):
        self.sems = sems
        self.used = 0
        self.open = []

    def start(self, source, target):
        copy = pltpu.make_async_copy(source, target, self.sems.at[self.used])
        self.used += 1
        copy.start()
        return copy

    def out(self, source, target):
        self.open.append(self.start(source, target))

    def finish(self):
        for copy in self.open:
            copy.wait()


def wait_all(copies):
    for copy in copies:
        copy.wait()


class Piece:
    def __init__(self, array, row=None, source=0, target=0, count=None, clip=None):
        self.array = array
        self.row = row
        self.source = source
        self.target = target
        self.count = array.shape[0] if count is None else count
        self.clip = clip

    def load(self, copies, ref, meta_ref, scratch):
        rows = ref.shape[1]
        row = 0 if self.row is None else pl.multiple_of(meta_ref[self.row], 16)
        first = self.source if self.clip is None else meta_ref[self.clip]
        return copies.start(
            ref.at[pl.ds(first, self.count)],
            scratch.at[pl.ds(self.target, self.count), pl.ds(row, rows), :],
        )


def load_pieces(copies, pieces, refs, meta_ref, scratch):
    return [p.load(copies, ref, meta_ref, scratch) for p, ref in zip(pieces, refs)]


def load_clips(copies, pieces, refs, meta_ref, scratch, groups):
    loads = []
    for group in groups:
        begun = []
        for p, ref in zip(pieces, refs):
            part = Piece(p.array, p.row, group[0], group[0], len(group))
            if p.clip is not None:
                start = meta_ref[p.clip]
                ref = ref.at[pl.ds(start, scratch.shape[0])]
            begun.append(part.load(copies, ref, meta_ref, scratch))
        loads.append(begun)
    return loads


def taps_of(pieces):
    return max(piece.target + piece.count for piece in pieces)


def arrays_of(pieces):
    return [piece.array for piece in pieces]


def run(kind, body, meta, lens, near, far, outs, scratch, sems, flops=0):
    names, arrays, specs, spread = ["meta", "lens"], [meta, lens], [SMEM, SMEM], {}
    for name, array in near.items():
        names.append(name)
        arrays.append(held(array) if array.size >= MIB else array)
        specs.append(VMEM)
    for name, group in far.items():
        many = isinstance(group, (list, tuple))
        spread[name] = len(group) if many else None
        for number, array in enumerate(group if many else [group]):
            names.append((name, number))
            arrays.append(pltpu.with_memory_space_constraint(array, pltpu.HBM))
            specs.append(ANY)
    shapes, out_specs = [], []
    for name, (shape, dtype, stays) in outs.items():
        names.append(name)
        shapes.append(pltpu.VMEM(shape, dtype) if stays else pltpu.HBM(shape, dtype))
        out_specs.append(VMEM if stays else ANY)
    names += list(scratch) + ["sems"]

    def kernel(*refs):
        found = dict(zip(names, refs))
        for name, count in spread.items():
            if count is None:
                found[name] = found[(name, 0)]
            else:
                found[name] = [found[(name, number)] for number in range(count)]
        found = {name: ref for name, ref in found.items() if isinstance(name, str)}
        copies = Copies(found["sems"])
        body(types.SimpleNamespace(**found), copies)
        copies.finish()

    moved = sum(a.size * a.dtype.itemsize for a in arrays)
    cover = COVER[kind]
    results = pl.pallas_call(
        kernel,
        out_shape=tuple(shapes),
        in_specs=specs,
        out_specs=tuple(out_specs),
        scratch_shapes=[pltpu.VMEM(shape, dtype) for shape, dtype in scratch.values()]
        + [pltpu.SemaphoreType.DMA((sems,))],
        compiler_params=pltpu.CompilerParams(vmem_limit_bytes=LIMIT),
        cost_estimate=pl.CostEstimate(
            flops=max(int(cover * flops), 1), bytes_accessed=int(cover * moved), transcendentals=0
        ),
    )(*arrays)
    return types.SimpleNamespace(**dict(zip(outs, results)))


def groups_of(clips):
    per = min(4, clips)
    return [tuple(range(first, first + per)) for first in range(0, clips, per)]


def span(clip_numbers, frames):
    return slice(clip_numbers[0] * frames, (clip_numbers[-1] + 1) * frames)


def mask_of(len_ref, clip_numbers, frames):
    position = lax.broadcasted_iota(jnp.int32, (1, frames), 1)
    return lanes([(position < len_ref[clip]).astype(F32) for clip in clip_numbers])


def counted_of(len_ref, mask_ref, clip_numbers, frames):
    inside = mask_of(len_ref, clip_numbers, frames)
    return inside * lanes([mask_ref[clip : clip + 1, :].astype(F32) for clip in clip_numbers])


def conv_forward(weight_ref, source_ref, clip_numbers, frames, taps, at=0, waits=()):
    blocks = [source_ref[:, span((clip,), frames)] for clip in clip_numbers]
    total = None
    waits = dict(waits)
    for tap in range(taps):
        wait_all(waits.get(tap, ()))
        moved = lanes([shifted(block, tap - taps // 2) for block in blocks])
        term = jnp.dot(weight_ref[at + tap], moved, preferred_element_type=F32)
        total = term if total is None else total + term
    return total


def conv_backward(weight_ref, grad_ref, clip_numbers, frames, taps, at=0, waits=()):
    blocks = [grad_ref[:, span((clip,), frames)] for clip in clip_numbers]
    total = None
    waits = dict(waits)
    for tap in range(taps):
        wait_all(waits.get(tap, ()))
        moved = lanes([shifted(block, taps // 2 - tap) for block in blocks])
        term = lax.dot_general(
            weight_ref[at + tap],
            moved,
            (((0,), (0,)), ((), ())),
            preferred_element_type=F32,
        )
        total = term if total is None else total + term
    return total


def lookup(meta, lens, ids, book, clips, frames, dim):
    codes = book[0].array.shape[2]
    wide = (dim, clips * frames)

    def body(r, copies):
        loads = load_pieces(copies, book, r.book, r.meta, r.table)
        every = tuple(range(clips))
        inside = mask_of(r.lens, every, frames)
        for group in range(dim // GW):
            rows = slice(group * GW, (group + 1) * GW)
            found = []
            for level, far in ((0, r.q0), (1, r.q1)):
                hot = r.hot.at[level]
                one_hot(r.ids, hot, level, group, clips, frames, dim)
                if group == 0 and level == 0:
                    wait_all(loads)
                value = jnp.dot(r.table[level, rows, :], hot[...], preferred_element_type=F32)
                r.found[level, rows, :] = value.astype(BF16)
                copies.out(r.found.at[level, rows], far.at[rows])
                found.append(value)
            r.u3[rows, :] = (inside * (found[0] + found[1])).astype(BF16)
            copies.out(r.u3.at[rows], r.u3_far.at[rows])

    return run(
        "lookup",
        body,
        meta,
        lens,
        {"ids": ids},
        {"book": arrays_of(book)},
        {
            "u3": (wide, BF16, True),
            "u3_far": (wide, BF16, False),
            "q0": (wide, BF16, False),
            "q1": (wide, BF16, False),
        },
        {
            "table": ((LEVELS, dim, codes), BF16),
            "hot": ((LEVELS, codes, clips * frames), BF16),
            "found": ((LEVELS,) + wide, BF16),
        },
        len(book) + 3 * LEVELS * (dim // GW),
        2 * LEVELS * dim * codes * clips * frames,
    )


def one_hot(ids_ref, hot, level, group, clips, frames, dim):
    number = lax.broadcasted_iota(jnp.int32, (hot.shape[0], frames), 0).astype(jnp.int16)
    one = jnp.ones((), BF16)
    zero = jnp.zeros((), BF16)
    for clip in range(clips):
        at = clip * LEVELS * (dim // GW) + group * LEVELS + level
        row = ids_ref[at : at + 1, :].astype(jnp.int16)
        hot[:, span((clip,), frames)] = jnp.where(number == row, one, zero)


def clip_outs(out_rows, clips, frames):
    return {
        "out%d_%d" % (number, group): ((len(members), count, frames), BF16, False)
        for number, (_, count) in enumerate(out_rows)
        for group, members in enumerate(groups_of(clips))
    }


def clip_results(result, out_rows, clips):
    groups = range(len(groups_of(clips)))
    return [
        [getattr(result, "out%d_%d" % (number, group)) for group in groups]
        for number in range(len(out_rows))
    ]


def put_clips(copies, r, scratch, number, group, value, frames, rows):
    for place, clip in enumerate(group):
        scratch[clip] = value[:, place * frames : (place + 1) * frames]
    at = pl.ds(group[0], len(group))
    for place, (start, count) in enumerate(rows):
        row = 0 if start is None else pl.multiple_of(r.meta[start], 16)
        ref = getattr(r, "out%d_%d" % (place, number))
        copies.out(scratch.at[at, pl.ds(row, count), :], ref)


def decoder_first(meta, lens, u3, w3, bias, clips, frames, dim):
    wide = (dim, clips * frames)
    taps3 = taps_of(w3)

    def body(r, copies):
        loads = load_pieces(copies, w3, r.w3, r.meta, r.t3)
        for number, group in enumerate(groups_of(clips)):
            here = span(group, frames)
            inside = mask_of(r.lens, group, frames)
            waits = waits_of(w3, loads) if number == 0 else ()
            first = conv_forward(r.t3, r.u3, group, frames, taps3, 0, waits) + r.bias[:, 3:4]
            r.first[:, here] = first
            r.u4[:, here] = (inside * elu(first)).astype(BF16)

    return run(
        "decoder_first",
        body,
        meta,
        lens,
        {"u3": u3, "bias": bias},
        {"w3": arrays_of(w3)},
        {"first": (wide, F32, True), "u4": (wide, BF16, True)},
        {"t3": ((taps3, dim, dim), BF16)},
        len(w3),
        2 * taps3 * dim * dim * clips * frames,
    )


def decoder_rest(meta, lens, first, u4, w45, bias, out_rows, clips, frames, dim):
    wide = (dim, clips * frames)
    taps4 = taps_of(w45) - 1
    outs = {"u5": (wide, BF16, True)}
    outs["t45"] = ((taps4 + 1, dim, dim), BF16, True)
    outs.update(clip_outs(out_rows, clips, frames))

    def body(r, copies):
        loads = load_pieces(copies, w45, r.w45, r.meta, r.t45)
        wait_all(loads)
        for number, group in enumerate(groups_of(clips)):
            here = span(group, frames)
            inside = mask_of(r.lens, group, frames)
            second = conv_forward(r.t45, r.u4, group, frames, taps4) + r.bias[:, 4:5]
            r.u5[:, here] = (inside * elu(second)).astype(BF16)
            third = conv_forward(r.t45, r.u5, group, frames, 1, taps4) + r.bias[:, 5:6]
            result = (inside * (r.first[:, here] + third)).astype(BF16)
            put_clips(copies, r, r.work, number, group, result, frames, out_rows)

    return run(
        "decoder_rest",
        body,
        meta,
        lens,
        {"first": first, "u4": u4, "bias": bias},
        {"w45": arrays_of(w45)},
        outs,
        {"work": ((clips, dim, frames), BF16)},
        len(w45) + len(out_rows) * len(groups_of(clips)),
        2 * (taps4 + 1) * dim * dim * clips * frames,
    )


def waits_of(pieces, loads):
    waits = {}
    for piece, load in zip(pieces, loads):
        waits.setdefault(piece.target, []).append(load)
    return waits


class Rows:
    def __init__(self, dim, paired, short=False):
        self.dim = dim
        self.short = short
        self.paired = paired
        self.count = 2 if paired else 1
        self.height = dim // self.count

    def outs(self, columns):
        return {
            "sums%d" % number: ((self.height, columns), BF16, self.paired)
            for number in range(self.count)
        }

    def scratch(self, columns):
        return {} if self.paired else {"sums": ((self.dim, columns), BF16)}

    def put(self, r, copies, at, value):
        if not self.paired:
            r.sums[:, at] = value
            copies.out(r.sums.at[:, at], r.sums0.at[:, at])
            return
        quarter = self.dim // 4
        first = r.meta[1] == 0
        if self.short:
            run_of = quarter // 2
            for i in range(2):
                for j in range(2):
                    row = (j * 4 + i) * run_of
                    zero = value[row : row + run_of]
                    row = (i * 4 + 2 + j) * run_of
                    one = value[row : row + run_of]
                    row = (i * 2 + j) * run_of
                    r.sums0[row : row + run_of, at] = jnp.where(first, zero, one)
                    r.sums1[row : row + run_of, at] = jnp.where(first, one, zero)
            return
        run_of = quarter // 4
        for half in range(2):
            for block in range(4):
                row = half * 2 * quarter + block * run_of
                zero = value[row : row + run_of]
                one = value[row + quarter : row + quarter + run_of]
                row = (block * 2 + half) * run_of
                r.sums0[row : row + run_of, at] = jnp.where(first, zero, one)
                r.sums1[row : row + run_of, at] = jnp.where(first, one, zero)


def weight_grads(r, copies, rows, g, u, taps, offset, clips, frames, dim):
    for tap in range(taps):
        step = taps // 2 - tap
        left = g[...]
        if step != 0:
            for clip in range(clips):
                at = span((clip,), frames)
                r.work[:, at] = shifted(g[:, at], step)
            left = r.work[...]
        value = lax.dot_general(
            left, u[...], (((1,), (1,)), ((), ())), preferred_element_type=F32
        )
        rows.put(r, copies, slice(offset, offset + dim), value.astype(BF16))
        offset += dim
    total = jnp.sum(g[...].astype(F32), axis=1, keepdims=True)
    total = jnp.broadcast_to(total, (dim, 128)).astype(BF16)
    rows.put(r, copies, slice(offset, offset + 128), total)
    return offset + 128


def decoder_backward(
    meta, lens, cotangent, u3, u4, u5, t45, taps3, rows, clips, frames, dim
):
    wide = (dim, clips * frames)
    taps4 = t45.shape[0] - 1
    columns = (taps3 + taps4 + 1) * dim + 3 * 128

    def body(r, copies):
        loads = load_clips(copies, cotangent, r.cot, r.meta, r.clips, groups_of(clips))
        late = copies.start(r.u3, r.s3)
        for group, begun in zip(groups_of(clips), loads):
            here = span(group, frames)
            wait_all(begun)
            inside = mask_of(r.lens, group, frames)
            out = lanes([r.clips[clip] for clip in group])
            out = jnp.where(inside > 0, out, jnp.zeros((), BF16))
            r.g5[:, here] = out
            back = conv_backward(r.t45, r.g5, group, frames, 1, taps4)
            r.g4[:, here] = (back * inside * slope_of(r.u5[:, here])).astype(BF16)
            back = conv_backward(r.t45, r.g4, group, frames, taps4)
            total = out.astype(F32) + back * inside * slope_of(r.u4[:, here])
            r.s_g3[:, here] = total.astype(BF16)
            copies.out(r.s_g3.at[:, here], r.g3.at[:, here])
        sizes = (clips, frames, dim)
        at = weight_grads(r, copies, rows, r.g5, r.u5, 1, 0, *sizes)
        at = weight_grads(r, copies, rows, r.g4, r.u4, taps4, at, *sizes)
        late.wait()
        weight_grads(r, copies, rows, r.s_g3, r.s3, taps3, at, *sizes)

    return run(
        "decoder_backward",
        body,
        meta,
        lens,
        {"u4": u4, "u5": u5, "t45": t45},
        {"cot": arrays_of(cotangent), "u3": u3},
        {"g3": (wide, BF16, False), **rows.outs(columns)},
        {
            "clips": ((clips, dim, frames), BF16),
            "s3": (wide, BF16),
            "g5": (wide, BF16),
            "g4": (wide, BF16),
            "s_g3": (wide, BF16),
            "work": (wide, BF16),
            **rows.scratch(columns),
        },
        (len(cotangent) + 1) * len(groups_of(clips))
        + 1
        + rows.count * (taps3 + taps4 + 4),
        2 * (taps3 + 2 * taps4 + 2) * dim * dim * clips * frames,
    )


def encoder_forward(
    meta, lens, mask, tokens, w012, bias, q0, q1, ahead, g3, clips, frames, dim
):
    wide = (dim, clips * frames)
    groups = groups_of(clips)
    taps0 = taps_of(w012[0])
    weights = [piece for layer in w012 for piece in layer]
    places = (0, taps0, taps0 + 1)

    def body(r, copies):
        loads = load_clips(copies, tokens, r.tokens, r.meta, r.clips, groups[:1])
        begun, refs = [], iter(r.w012)
        for place, layer in zip(places, w012):
            target = r.t.at[pl.ds(place, taps_of(layer))]
            begun.append([p.load(copies, next(refs), r.meta, target) for p in layer])
        loads += load_clips(copies, tokens, r.tokens, r.meta, r.clips, groups[1:])
        late = [copies.start(r.q0, r.s_q0), copies.start(r.q1, r.s_q1)]
        copies.open += load_pieces(copies, ahead, r.ahead, r.meta, r.next)
        copies.out(r.g3, r.g3_near)
        for number, group in enumerate(groups):
            here = span(group, frames)
            wait_all(loads[number])
            inside = mask_of(r.lens, group, frames)
            start = inside * lanes([r.clips[clip] for clip in group]).astype(F32)
            r.s0[:, here] = elu(start).astype(BF16)
            copies.out(r.s0.at[:, here], r.u0.at[:, here])
            if number == 0:
                wait_all(begun[0])
            first = conv_forward(r.t, r.s0, group, frames, taps0) + r.bias[:, 0:1]
            r.s1[:, here] = (inside * elu(first)).astype(BF16)
            copies.out(r.s1.at[:, here], r.u1.at[:, here])
            if number == 0:
                wait_all(begun[1])
                wait_all(begun[2])
            second = conv_forward(r.t, r.s1, group, frames, 1, taps0) + r.bias[:, 1:2]
            r.u2_near[:, here] = elu(inside * (start + second)).astype(BF16)
            copies.out(r.u2_near.at[:, here], r.u2.at[:, here])
            latent = conv_forward(r.t, r.u2_near, group, frames, taps0, taps0 + 1)
            latent = latent + r.bias[:, 2:3]
            if number == 0:
                wait_all(late)
            double = 2.0 * counted_of(r.lens, r.mask, group, frames)
            miss = r.s_q0[:, here].astype(F32) - latent
            r.gq0[:, here] = (double * miss).astype(BF16)
            r.gq1[:, here] = (double * (miss + r.s_q1[:, here].astype(F32))).astype(BF16)

    return run(
        "encoder_forward",
        body,
        meta,
        lens,
        {"mask": mask, "bias": bias},
        {
            "tokens": arrays_of(tokens),
            "w012": arrays_of(weights),
            "q0": q0,
            "q1": q1,
            "ahead": arrays_of(ahead),
            "g3": g3,
        },
        {
            "u0": (wide, BF16, False),
            "u1": (wide, BF16, False),
            "u2": (wide, BF16, False),
            "u2_near": (wide, BF16, True),
            "gq0": (wide, BF16, True),
            "gq1": (wide, BF16, True),
            "next": ((taps_of(ahead), dim, dim), BF16, True),
            "g3_near": (wide, BF16, True),
        },
        {
            "clips": ((clips, dim, frames), BF16),
            "t": ((2 * taps0 + 1, dim, dim), BF16),
            **{name: (wide, BF16) for name in ("s0", "s1", "s_q0", "s_q1")},
        },
        (len(tokens) + 3) * len(groups) + len(ahead) + len(weights) + 3,
        2 * (2 * taps0 + 1) * dim * dim * clips * frames,
    )


def latent_backward(
    meta, lens, ids, g3, t3, gq0, gq1, u2, taps2, codes, ahead, rows, clips, frames, dim
):
    wide = (dim, clips * frames)
    taps3 = t3.shape[0]
    columns = taps2 * dim + 128 + LEVELS * codes

    def body(r, copies):
        copies.open += load_pieces(copies, ahead, r.ahead, r.meta, r.next)
        for group in groups_of(clips):
            here = span(group, frames)
            inside = mask_of(r.lens, group, frames)
            back = conv_backward(r.t3, r.g3, group, frames, taps3)
            extra = BETA * r.gq1[:, here].astype(F32)
            r.g2[:, here] = (back * inside - extra).astype(BF16)
        sizes = (clips, frames, dim)
        offset = weight_grads(r, copies, rows, r.g2, r.u2, taps2, 0, *sizes)
        for level, grad in enumerate((r.gq0, r.gq1)):
            values = []
            for group in range(dim // GW):
                at = slice(group * GW, (group + 1) * GW)
                one_hot(r.ids, r.hot, level, group, clips, frames, dim)
                values.append(
                    lax.dot_general(
                        grad[at, :],
                        r.hot[...],
                        (((1,), (1,)), ((), ())),
                        preferred_element_type=F32,
                    ).astype(BF16)
                )
            value = jnp.concatenate(values, axis=0)
            rows.put(r, copies, slice(offset, offset + codes), value)
            offset += codes

    return run(
        "latent_backward",
        body,
        meta,
        lens,
        {"ids": ids, "g3": g3, "t3": t3, "gq0": gq0, "gq1": gq1, "u2": u2},
        {"ahead": arrays_of(ahead)},
        {
            "g2": (wide, BF16, True),
            "next": ((taps_of(ahead), dim, dim), BF16, True),
            **rows.outs(columns),
        },
        {
            "hot": ((codes, clips * frames), BF16),
            "work": (wide, BF16),
            **rows.scratch(columns),
        },
        len(ahead) + rows.count * (taps2 + 1 + LEVELS),
        2 * ((taps3 + taps2) * dim + LEVELS * codes) * dim * clips * frames,
    )


def encoder_backward(meta, lens, g2, u2, u1, u0, t, taps0, ahead, clips, frames, dim):
    wide = (dim, clips * frames)

    def body(r, copies):
        second = copies.start(r.u2, r.s2)
        first = copies.start(r.u1, r.u1_near)
        copies.out(r.u0, r.u0_near)
        copies.open += load_pieces(copies, ahead, r.ahead, r.meta, r.next)
        for number, group in enumerate(groups_of(clips)):
            here = span(group, frames)
            inside = mask_of(r.lens, group, frames)
            back = conv_backward(r.t, r.g2, group, frames, taps0, 1)
            if number == 0:
                second.wait()
            r.g1[:, here] = (back * inside * slope_of(r.s2[:, here])).astype(BF16)
            back = conv_backward(r.t, r.g1, group, frames, 1)
            if number == 0:
                first.wait()
            r.g0[:, here] = (back * inside * slope_of(r.u1_near[:, here])).astype(BF16)

    names = ("g1", "g0", "u1_near", "u0_near")
    return run(
        "encoder_backward",
        body,
        meta,
        lens,
        {"g2": g2, "t": t},
        {"u2": u2, "u1": u1, "u0": u0, "ahead": arrays_of(ahead)},
        {
            **{name: (wide, BF16, True) for name in names},
            "next": ((taps_of(ahead), dim, dim), BF16, True),
        },
        {"s2": (wide, BF16)},
        len(ahead) + 3,
        2 * (taps0 + 1) * dim * dim * clips * frames,
    )


def encoder_grads(meta, lens, g0, u0, g1, u1, taps0, rows, clips, frames, dim):
    columns = (taps0 + 1) * dim + 2 * 128

    def body(r, copies):
        sizes = (clips, frames, dim)
        at = weight_grads(r, copies, rows, r.g0, r.u0, taps0, 0, *sizes)
        weight_grads(r, copies, rows, r.g1, r.u1, 1, at, *sizes)

    return run(
        "encoder_grads",
        body,
        meta,
        lens,
        {"g0": g0, "u0": u0, "g1": g1, "u1": u1},
        {},
        rows.outs(columns),
        {"work": ((dim, clips * frames), BF16), **rows.scratch(columns)},
        1 + rows.count * (taps0 + 3),
        2 * (taps0 + 1) * dim * dim * clips * frames,
    )


def tokens_backward(meta, lens, g0, u0, g1, t, out_rows, clips, frames, dim):
    taps0 = t.shape[0]

    def body(r, copies):
        for number, group in enumerate(groups_of(clips)):
            here = span(group, frames)
            inside = mask_of(r.lens, group, frames)
            back = conv_backward(r.t, r.g0, group, frames, taps0)
            total = r.g1[:, here].astype(F32) + back * inside * slope_of(r.u0[:, here])
            total = (inside * total).astype(BF16)
            put_clips(copies, r, r.work, number, group, total, frames, out_rows)

    result = run(
        "tokens_backward",
        body,
        meta,
        lens,
        {"g0": g0, "g1": g1, "u0": u0, "t": t},
        {},
        clip_outs(out_rows, clips, frames),
        {"work": ((clips, dim, frames), BF16)},
        len(out_rows) * len(groups_of(clips)),
        2 * taps0 * dim * dim * clips * frames,
    )
    return clip_results(result, out_rows, clips)


def unpack(meta, pieces, blocks, half):
    outs = []
    for taps, width, has_bias in blocks:
        outs.append(struct((taps, half, width), F32))
        if has_bias:
            outs.append(struct((1, half), F32))

    def body(meta_ref, mine_ref, other_ref, *refs):
        take = iter(refs)
        first = meta_ref[1] == 0

        def columns(at):
            mine, other = mine_ref[:, at], other_ref[:, at]
            return jnp.concatenate(
                [jnp.where(first, mine, other), jnp.where(first, other, mine)], axis=0
            ).astype(F32)

        offset = 0
        for taps, width, has_bias in blocks:
            out = next(take)
            for tap in range(taps):
                out[tap] = columns(slice(offset, offset + width))
                offset += width
            if has_bias:
                next(take)[...] = columns(slice(offset, offset + 128)).T[0:1]
                offset += 128

    return pl.pallas_call(
        body,
        out_shape=tuple(outs),
        in_specs=[SMEM, VMEM, VMEM],
        out_specs=tuple(VMEM for _ in outs),
        compiler_params=pltpu.CompilerParams(vmem_limit_bytes=LIMIT),
    )(meta, *pieces)


def in_three(array, rows, columns):
    terms = []
    for _ in range(3):
        term = lax.reduce_precision(array, exponent_bits=8, mantissa_bits=7)
        terms.append(term.astype(BF16).reshape(-1))
        array = array - term
    terms = jnp.concatenate(terms)
    return jnp.pad(terms, (0, rows * columns - terms.size)).reshape(1, rows, columns)


def from_three(block, shape):
    size = shape[0] * shape[1]
    terms = block.reshape(-1)[: 3 * size].reshape((3,) + shape).astype(F32)
    return (terms[0] + terms[1]) + terms[2]


class Pairs:
    BITS = {"core": 1, "x": 2, "zl": 4, "zh": 8}

    def __init__(self, rows, clips):
        self.chan = lax.axis_index("chan")
        self.dp = lax.axis_index("dp")
        self.core = self.bit("core")
        x = self.bit("x")
        other = (1 - self.chan) * rows
        piece = rows // 4
        here = [(self.core, x), (self.core, 1 - x), (1 - self.core, x), (1 - self.core, 1 - x)]
        self.piece = (self.core * 2 + x) * piece
        self.meta = jnp.stack(
            [self.chan, self.core, self.chan * rows, other]
            + [other + (c * 2 + b) * piece for c, b in here]
            + [self.chan * clips]
            + [other + self.core * 2 * piece, other + (1 - self.core) * 2 * piece]
        ).astype(jnp.int32)

    def bit(self, name):
        if name == "chan":
            return self.chan
        return (self.dp & self.BITS[name]) // self.BITS[name]

    def swap(self, value, name):
        if name == "chan":
            return lax.ppermute(value, "chan", [(0, 1), (1, 0)])
        mask = self.BITS[name]
        return lax.ppermute(value, "dp", [(i, i ^ mask) for i in range(16)])

    def swap_by_core(self, value, names):
        pairs = []
        for place in range(32):
            other = place
            for name in names[(place // 2) & 1].split("+"):
                other ^= 1 if name == "chan" else 2 * self.BITS[name]
            pairs.append((place, other))
        return lax.ppermute(value, ("dp", "chan"), pairs)

    def bit_by_core(self, names):
        return jnp.where(self.core == 0, self.bit(names[0]), self.bit(names[1]))

    def piece_of(self, own):
        return lax.dynamic_slice_in_dim(own, self.piece, own.shape[1] // 4, 1)

    def half_of(self, own):
        half = own.shape[1] // 2
        return lax.dynamic_slice_in_dim(own, self.core * half, half, 1)

    def spread(self, near):
        far = self.swap(near, "x")
        return near, far, self.swap(near, "core"), self.swap(far, "core")

    def ordered(self, own, came):
        first = self.chan == 0
        return jnp.concatenate([jnp.where(first, own, came), jnp.where(first, came, own)])

    @property
    def bits(self):
        return jnp.stack([self.bit_by_core(pair) for pair in PAIRS]).astype(jnp.int32)

    def start(self, grads, steps):
        kept, sent = grads
        return Reduction(self, kept, self.swap(sent, "core"), steps)


XZ, ZX, CC, HH = ("x", "zl"), ("zl", "x"), ("chan", "chan"), ("zh", "zh")
PAIRS = (XZ, ZX, CC, HH)
START = (("halve", XZ), ("halve2", ZX, CC), ("keep", HH))
STEPS_2 = START + (("double", ZX), ("double", XZ), ("double", ("core", "core")))
STEPS_4 = START + (("double2", ZX, XZ), ("double", ("core", "core")))
STEPS = STEPS_2, STEPS_2, STEPS_4


class Reduction:
    def __init__(self, links, kept, came, steps):
        self.links = links
        self.steps = steps
        self.at = 0
        self.terms = [(kept, 0)]
        self.came = [came]
        self.value = None
        self.cuts = [PAIRS.index(n) for kind, *names in steps if "halve" in kind for n in names]
        self.cut = 0

    @property
    def done(self):
        return self.at == len(self.steps)

    @property
    def result(self):
        return [self.value] + self.came

    def plan(self):
        if self.value is not None:
            how = self.steps[self.at - 1][0]
            lead = {"keep": (), "double": (2,), "double2": (2, 2)}[how]
            return how, [self.value] + self.came, [lead + self.value.shape]
        self.terms += [(array, self.cut) for array in self.came]
        how = self.steps[self.at][0]
        last = self.cut + {"halve": 1, "halve2": 2}.get(how, 0)
        blocks = [
            term.reshape((2,) * (last - first) + (-1, term.shape[-1]))
            for term, first in self.terms
        ]
        return how, blocks, [blocks[0].shape[-2:]] * (3 if how == "halve2" else 1)

    def fill(self, how, refs, outs, bits):
        if self.value is not None:
            places = [bits[PAIRS.index(n)] for n in self.steps[self.at - 1][1:] if n in PAIRS]
            if how == "keep":
                total = refs[0][...].astype(F32) + refs[1][...].astype(F32)
                outs[0][...] = total.astype(BF16)
            elif how == "double":
                outs[0][places[0]] = refs[0][...]
                outs[0][1 - places[0]] = refs[1][...]
            else:
                inner, outer = places
                outs[0][outer, inner] = refs[0][...]
                outs[0][outer, 1 - inner] = refs[1][...]
                outs[0][1 - outer, inner] = refs[2][...]
                outs[0][1 - outer, 1 - inner] = refs[3][...]
            return
        flips = {"halve": ((1,),), "halve2": ((1, 0), (0, 1), (1, 1))}.get(how, ((),))
        for out, flip in zip(outs, flips):
            place = [bits[cut] for cut in self.cuts[: self.cut]]
            for cut, turned in zip(self.cuts[self.cut :], flip):
                place.append(1 - bits[cut] if turned else bits[cut])
            sums = None
            for ref, (_, first) in zip(refs, self.terms):
                where = tuple(place[first:])
                piece = (ref[where] if where else ref[...]).astype(F32)
                sums = piece if sums is None else sums + piece
            out[...] = sums.astype(BF16)

    def send(self, sent):
        kind, *names = self.steps[self.at]
        sent = [array.reshape(-1, array.shape[-1]) for array in sent]
        if "halve" in kind:
            self.cut += len(names)
        else:
            self.value = sent[0]
        if len(names) == 2:
            names.append(tuple(a + "+" + b for a, b in zip(*names)))
        sent = sent * len(names) if len(sent) == 1 else sent
        self.came = [self.links.swap_by_core(a, n) for a, n in zip(sent, names)]
        self.at += 1


def advance(after, *reductions):
    came = lax.optimization_barrier((tuple(r.came for r in reductions), tuple(after)))[0]
    arrays, counts, shapes, widths, hows = [], [], [], [], []
    for reduction, array in zip(reductions, came):
        reduction.came = list(array)
        how, operands, targets = reduction.plan()
        hows.append(how)
        counts.append(len(operands))
        widths.append(len(targets))
        arrays += [held(operand) for operand in operands]
        shapes += [pltpu.VMEM(target, BF16) for target in targets]

    def body(bits_ref, *refs):
        taken, filled = 0, len(arrays)
        for reduction, how, count, width in zip(reductions, hows, counts, widths):
            outs = refs[filled : filled + width]
            reduction.fill(how, refs[taken : taken + count], outs, bits_ref)
            taken += count
            filled += width

    sent = pl.pallas_call(
        body,
        out_shape=tuple(shapes),
        in_specs=[SMEM] + [VMEM] * len(arrays),
        out_specs=tuple(VMEM for _ in shapes),
        compiler_params=pltpu.CompilerParams(vmem_limit_bytes=8 * MIB),
        cost_estimate=pl.CostEstimate(
            flops=COVER["advance"], bytes_accessed=COVER["advance"], transcendentals=0
        ),
    )(reductions[0].links.bits, *arrays)
    filled = 0
    for reduction, width in zip(reductions, widths):
        reduction.send(sent[filled : filled + width])
        filled += width
    return list(sent)


def on_pairs(
    tokens,
    lengths,
    frame_mask,
    code_ids,
    cotangent,
    weights,
    biases,
    codebook,
):
    chan = 2
    rows = tokens.shape[1]
    frames = tokens.shape[2]
    dim = rows * chan
    clips = tokens.shape[0] // chan
    codes = codebook.shape[2]
    sizes = (clips, frames, dim)
    links = Pairs(rows, clips)
    meta = links.meta
    mine = functools.partial(
        lax.dynamic_slice_in_dim, start_index=links.chan * clips, slice_size=clips, axis=0
    )
    others = functools.partial(
        lax.dynamic_slice_in_dim, start_index=(1 - links.chan) * clips, slice_size=clips, axis=0
    )
    taps = [w.shape[0] for w in weights]
    own, other, pieces, halves = 2, 3, (4, 5, 6, 7), (9, 10)

    split = (taps[3] + 1) // 2
    lens = mine(lengths)
    mask = mine(frame_mask)
    ids = mine(code_ids).reshape(-1, frames)
    bias = jnp.stack(biases + (jnp.zeros_like(biases[0]),) * 2)
    first_pieces = lax.optimization_barrier(
        (
            links.piece_of(codebook),
            links.piece_of(weights[3][:split]),
            links.half_of(weights[3][split:]),
        )
    )
    near_book, near3a, near3b = (links.swap(piece, "chan") for piece in first_pieces)
    dec = jnp.concatenate([weights[4], weights[5]])
    enc = jnp.concatenate([weights[0], weights[1], weights[2]])
    far_book = links.spread(near_book)
    dec_piece = jnp.concatenate([links.piece_of(dec), in_three(bias, rows // 4, dim)])
    dec_piece = tie(dec_piece, near_book)
    near45 = links.swap(dec_piece, "chan")
    far3a = links.spread(near3a)
    enc_piece = tie(links.piece_of(enc), near_book)
    near012 = links.swap(enc_piece, "chan")
    cot_send = tie(others(tie(cotangent, near_book)), near3a, dec_piece, enc_piece)
    cot_other = links.swap(cot_send, "chan")
    book = [Piece(codebook, own)] + [Piece(a, s) for a, s in zip(far_book, pieces)]
    tok_send = others(tie(tokens, near3a))
    found = lookup(meta, lens, tie(ids, cot_send, tok_send), book, *sizes)
    tok_send = tie(tok_send, found.u3)
    tok_other = links.swap(tok_send, "chan")
    near3b, near45 = tie((near3b, near45), found.u3)
    far3b = near3b, links.swap(near3b, "core")
    bias_came = from_three(near45[taps[4] + taps[5] :], bias.shape)
    bias = links.ordered(bias.T, bias_came.T)
    w3 = [Piece(weights[3], own, 0, 0, split)]
    w3 += [Piece(a, s) for a, s in zip(far3a, pieces)]
    w3 += [Piece(weights[3], own, split, split, taps[3] - split)]
    w3 += [Piece(a, s, 0, split) for a, s in zip(far3b, halves)]
    far45_x = links.swap(near45, "x")
    dec_first = decoder_first(
        meta, lens, found.u3, w3, bias, *sizes
    )
    near45, far45_x = tie((near45, far45_x), dec_first.u4)
    far45 = near45, far45_x, links.swap(near45, "core"), links.swap(far45_x, "core")
    w45 = [Piece(weights[4], own), Piece(weights[5], own, 0, taps[4])]
    w45 += [Piece(a, s, 0, 0, taps[4] + taps[5]) for a, s in zip(far45, pieces)]
    out_rows = ((own, rows), (other, rows))
    dec_out = decoder_rest(
        meta, lens, dec_first.first, dec_first.u4, w45, bias, out_rows, *sizes
    )
    near012 = tie(near012, dec_out.u5)
    far012_x = links.swap(near012, "x")
    rows_a = rows_c = rows_d = Rows(dim, True)
    cot = [Piece(cotangent, own, clip=8, count=clips)]
    cot.append(Piece(tie(cot_other, near012), other))
    dec_back = decoder_backward(
        meta,
        lens,
        cot,
        found.u3_far,
        dec_first.u4,
        dec_out.u5,
        dec_out.t45,
        taps[3],
        rows_a,
        *sizes,
    )
    near012, far012_x = tie((near012, far012_x), dec_back.g3)
    far012 = near012, far012_x, links.swap(near012, "core"), links.swap(far012_x, "core")

    def enc_pieces(which):
        listed = []
        place = 0
        for number in which:
            listed.append(Piece(weights[number], own, 0, place))
            place += taps[number]
        start = sum(taps[: which[0]])
        listed += [Piece(a, s, start, 0, place) for a, s in zip(far012, pieces)]
        return listed

    red_a = links.start([dec_back.sums0, tie(dec_back.sums1, tok_other)], STEPS[0])
    out_own, out_send = clip_results(dec_out, out_rows, clips)
    out_send[0] = tie(out_send[0], tok_other)
    out_came = [links.swap(out_send[0], "chan")]
    tok = [Piece(tokens, own, clip=8, count=clips)]
    tok.append(Piece(tie(tok_other, dec_back.g3, out_send[0]), other))
    enc_out = encoder_forward(
        meta,
        lens,
        mask,
        tok,
        [enc_pieces([0]), enc_pieces([1]), enc_pieces([2])],
        bias,
        found.q0,
        found.q1,
        w3,
        dec_back.g3,
        *sizes,
    )
    sent = advance([enc_out.u2], red_a)
    out_came.append(links.swap(tie(out_send[1], *sent), "chan"))
    lat = latent_backward(
        meta,
        lens,
        ids,
        tie(enc_out.g3_near, out_came[0], *sent),
        enc_out.next,
        enc_out.gq0,
        enc_out.gq1,
        enc_out.u2_near,
        taps[2],
        codes,
        enc_pieces([1, 2]),
        rows_c,
        *sizes,
    )
    red_c = links.start([lat.sums0, lat.sums1], STEPS[1])
    sent = advance([lat.g2], red_a)
    enc_back = encoder_backward(
        meta,
        lens,
        lat.g2,
        tie(enc_out.u2, out_came[1], *sent),
        enc_out.u1,
        enc_out.u0,
        lat.next,
        taps[0],
        enc_pieces([0]),
        *sizes,
    )
    sent = advance([enc_back.g0], red_c)
    enc_sums = encoder_grads(
        meta,
        lens,
        tie(enc_back.g0, *sent),
        enc_back.u0_near,
        enc_back.g1,
        enc_back.u1_near,
        taps[0],
        rows_d,
        *sizes,
    )
    red_d = links.start([enc_sums.sums0, enc_sums.sums1], STEPS[2])
    sent = advance([enc_sums.sums0], red_a)
    grad_own, grad_other = tokens_backward(
        meta,
        lens,
        tie(enc_back.g0, *sent),
        enc_back.u0_near,
        enc_back.g1,
        enc_back.next,
        out_rows,
        *sizes,
    )
    sent = advance(grad_other, *([red_a] if A_EARLY else []), red_c, red_d)
    grad_came = []
    shapes = {
        red_a: [(1, dim, True), (taps[4], dim, True), (taps[3], dim, True)],
        red_c: [(taps[2], dim, True), (LEVELS, codes, False)],
        red_d: [(taps[0], dim, True), (1, dim, True)],
    }
    results = {}
    slot = 0
    groups = (red_a, red_c, red_d)
    while not all(r.done for r in groups):
        slot += 1
        for half, (begin, end) in enumerate(GRAD_SLOTS):
            if slot == begin:
                grad_came.append(links.swap(tie(grad_other[half], *sent), "chan"))
        for half, (begin, end) in enumerate(GRAD_SLOTS):
            if slot == end:
                sent = list(sent) + [grad_came[half]]
        active = [r for r in groups if not r.done]
        for r in groups:
            if r.done and r not in results:
                mine_rows, other_rows = r.result
                mine_rows = tie(mine_rows, *sent)
                results[r] = unpack(meta, [mine_rows, other_rows], shapes[r], rows)
                sent = list(sent) + list(results[r][:1])
        if slot == OUT_SLOTS[0]:
            came = jnp.concatenate(tie(out_came, *sent))
            output = links.ordered(jnp.concatenate(out_own), came)
            sent = list(sent) + [output]
        if slot == OUT_SLOTS[1]:
            came = jnp.concatenate(tie(grad_came, *sent)).astype(F32)
            tokens_grad = links.ordered(jnp.concatenate(grad_own).astype(F32), came)
            sent = list(sent) + [tokens_grad]
        sent = advance(sent, *active)
    if slot < OUT_SLOTS[1]:
        came = jnp.concatenate(tie(grad_came, *sent)).astype(F32)
        tokens_grad = links.ordered(jnp.concatenate(grad_own).astype(F32), came)
    for r in groups:
        if r not in results:
            results[r] = unpack(meta, r.result, shapes[r], rows)
    a, c, d = results[red_a], results[red_c], results[red_d]
    w_grads = [d[0], d[2], c[0], a[4], a[2], a[0]]
    b_grads = [v.reshape(rows) for v in (d[1], d[3], c[1], a[5], a[3], a[1])]
    grads = [g for pair in zip(w_grads, b_grads) for g in pair]
    return (output, tokens_grad, *grads, c[2])


def on_others(
    tokens,
    lengths,
    frame_mask,
    code_ids,
    cotangent,
    weights,
    biases,
    codebook,
):
    chan = lax.axis_size("chan")
    place = lax.axis_index("chan")
    rows = tokens.shape[1]
    frames = tokens.shape[2]
    dim = rows * chan
    clips = tokens.shape[0] // chan
    codes = codebook.shape[2]
    sizes = (clips, frames, dim)
    meta = jnp.zeros((9,), jnp.int32)
    mine = functools.partial(
        lax.dynamic_slice_in_dim, start_index=place * clips, slice_size=clips, axis=0
    )
    taps = [w.shape[0] for w in weights]

    def gathered(*arrays):
        return [Piece(lax.all_gather(jnp.concatenate(arrays), "chan", axis=1, tiled=True))]

    def part(pieces, start, count):
        return [Piece(pieces[0].array, None, start, 0, count)]

    def clips_in(array):
        return [Piece(lax.all_to_all(array, "chan", 0, 1, tiled=True))]

    def clips_out(array):
        return lax.all_to_all(array, "chan", 1, 0, tiled=True)

    def reduced(grads):
        part = lax.psum_scatter(grads.astype(F32), "chan", scatter_dimension=0, tiled=True)
        return lax.psum(part, "dp")

    def columns(total, offset, count, width):
        block = total[:, offset : offset + count * width].reshape(rows, count, width)
        return jnp.transpose(block, (1, 0, 2))

    bias = jnp.stack(biases + (jnp.zeros_like(biases[0]),) * 2, axis=1)
    bias = lax.all_gather(bias, "chan", axis=0, tiled=True)
    lens = mine(lengths)
    mask = mine(frame_mask)
    ids = mine(code_ids).reshape(-1, frames)
    w3 = gathered(weights[3])
    w45 = gathered(weights[4], weights[5])
    w012 = gathered(weights[0], weights[1], weights[2])
    rows_of = Rows(dim, False)
    out_rows = ((None, dim),)
    found = lookup(meta, lens, ids, gathered(codebook), *sizes)
    dec_first = decoder_first(meta, lens, found.u3, w3, bias, *sizes)
    dec_out = decoder_rest(
        meta, lens, dec_first.first, dec_first.u4, w45, bias, out_rows, *sizes
    )
    dec_back = decoder_backward(
        meta,
        lens,
        clips_in(cotangent),
        found.u3_far,
        dec_first.u4,
        dec_out.u5,
        dec_out.t45,
        taps[3],
        rows_of,
        *sizes,
    )
    enc_out = encoder_forward(
        meta,
        lens,
        mask,
        clips_in(tokens),
        [
            part(w012, 0, taps[0]),
            part(w012, taps[0], taps[1]),
            part(w012, taps[0] + taps[1], taps[2]),
        ],
        bias,
        found.q0,
        found.q1,
        w3,
        dec_back.g3,
        *sizes,
    )
    lat = latent_backward(
        meta,
        lens,
        ids,
        enc_out.g3_near,
        enc_out.next,
        enc_out.gq0,
        enc_out.gq1,
        enc_out.u2_near,
        taps[2],
        codes,
        part(w012, taps[0], 1 + taps[2]),
        rows_of,
        *sizes,
    )
    enc_back = encoder_backward(
        meta,
        lens,
        lat.g2,
        enc_out.u2,
        enc_out.u1,
        enc_out.u0,
        lat.next,
        taps[0],
        part(w012, 0, taps[0]),
        *sizes,
    )
    enc_sums = encoder_grads(
        meta,
        lens,
        enc_back.g0,
        enc_back.u0_near,
        enc_back.g1,
        enc_back.u1_near,
        taps[0],
        rows_of,
        *sizes,
    )
    ((grad,),) = tokens_backward(
        meta,
        lens,
        enc_back.g0,
        enc_back.u0_near,
        enc_back.g1,
        enc_back.next,
        out_rows,
        *sizes,
    )
    ((out,),) = clip_results(dec_out, out_rows, clips)
    a, c, d = (reduced(x.sums0) for x in (dec_back, lat, enc_sums))
    placed = (
        (d, 0, taps[0]),
        (d, taps[0] * dim + 128, 1),
        (c, 0, taps[2]),
        (a, (1 + taps[4]) * dim + 256, taps[3]),
        (a, dim + 128, taps[4]),
        (a, 0, 1),
    )
    grads = []
    for total, start, count in placed:
        grads.append(columns(total, start, count, dim))
        grads.append(total[:, start + count * dim])
    books = columns(c, taps[2] * dim + 128, LEVELS, codes)
    return (clips_out(out), clips_out(grad).astype(F32), *grads, books)


def on_device(step, tokens, lengths, frame_mask, code_ids, cotangent, *params):
    weights, biases = params[0:12:2], params[1:12:2]
    return step(
        tokens, lengths, frame_mask, code_ids, cotangent, weights, biases, params[12]
    )


def solution(mesh):
    paired = mesh.shape["chan"] == 2 and mesh.shape["dp"] == 16
    weight = P(None, "chan", None)
    vector = P("chan")
    clip_rows = P("dp", "chan", None)
    in_specs = (
        (clip_rows, P("dp"), P("dp", None), P("dp", None, None), clip_rows)
        + (weight, vector) * 6
        + (weight,)
    )
    out_specs = (clip_rows, clip_rows) + (weight, vector) * 6 + (weight,)
    return jax.shard_map(
        functools.partial(on_device, on_pairs if paired else on_others),
        mesh=mesh,
        in_specs=in_specs,
        out_specs=out_specs,
        check_vma=False,
    )
```

```python
import functools
import types

import jax
import jax.numpy as jnp
from jax import lax
from jax.experimental import pallas as pl
from jax.experimental.pallas import tpu as pltpu
from jax.sharding import PartitionSpec as P

LEVELS = 2
GW = 256
BETA = 0.25
F32 = jnp.float32
BF16 = jnp.bfloat16
MIB = 1024 * 1024
LIMIT = 28 * MIB
GRAD_SLOTS = ((1, 3), (2, 5))
OUT_SLOTS = (2, 6)
A_EARLY = False
COVER = {
    "lookup": 0.01,
    "decoder_first": 0.01,
    "decoder_rest": 0.01,
    "decoder_backward": 0.01,
    "encoder_forward": 10,
    "latent_backward": 10,
    "encoder_backward": 10,
    "encoder_grads": 10,
    "tokens_backward": 10,
    "advance": 0,
}

ANY = pl.BlockSpec(memory_space=pl.ANY)
VMEM = pl.BlockSpec(memory_space=pltpu.VMEM)
SMEM = pl.BlockSpec(memory_space=pltpu.SMEM)


def elu(value):
    return jnp.where(value > 0, value, jnp.exp(jnp.minimum(value, 0.0)) - 1.0)


def slope_of(activated):
    act = activated.astype(F32)
    return jnp.where(act > 0, 1.0, 1.0 + act)


def shifted(value, step):
    if step == 0:
        return value
    edge = jnp.zeros((value.shape[0], abs(step)), value.dtype)
    if step > 0:
        return jnp.concatenate([value[:, step:], edge], axis=1)
    return jnp.concatenate([edge, value[:, :step]], axis=1)


def lanes(blocks):
    return blocks[0] if len(blocks) == 1 else jnp.concatenate(blocks, axis=1)


def tie(value, *earlier):
    earlier = [array for array in earlier if array is not None]
    if not earlier:
        return value
    return lax.optimization_barrier((value, tuple(earlier)))[0]


def held(array):
    return pltpu.with_memory_space_constraint(array, pltpu.VMEM)


def struct(shape, dtype):
    return jax.ShapeDtypeStruct(shape, dtype)


class Copies:
    def __init__(self, sems):
        self.sems = sems
        self.used = 0
        self.open = []

    def start(self, source, target):
        copy = pltpu.make_async_copy(source, target, self.sems.at[self.used])
        self.used += 1
        copy.start()
        return copy

    def out(self, source, target):
        self.open.append(self.start(source, target))

    def finish(self):
        for copy in self.open:
            copy.wait()


def wait_all(copies):
    for copy in copies:
        copy.wait()


class Piece:
    def __init__(self, array, row=None, source=0, target=0, count=None, clip=None):
        self.array = array
        self.row = row
        self.source = source
        self.target = target
        self.count = array.shape[0] if count is None else count
        self.clip = clip

    def load(self, copies, ref, meta_ref, scratch):
        rows = ref.shape[1]
        row = 0 if self.row is None else pl.multiple_of(meta_ref[self.row], 16)
        first = self.source if self.clip is None else meta_ref[self.clip]
        return copies.start(
            ref.at[pl.ds(first, self.count)],
            scratch.at[pl.ds(self.target, self.count), pl.ds(row, rows), :],
        )


def load_pieces(copies, pieces, refs, meta_ref, scratch):
    return [p.load(copies, ref, meta_ref, scratch) for p, ref in zip(pieces, refs)]


def load_clips(copies, pieces, refs, meta_ref, scratch, groups):
    loads = []
    for group in groups:
        begun = []
        for p, ref in zip(pieces, refs):
            part = Piece(p.array, p.row, group[0], group[0], len(group))
            if p.clip is not None:
                start = meta_ref[p.clip]
                ref = ref.at[pl.ds(start, scratch.shape[0])]
            begun.append(part.load(copies, ref, meta_ref, scratch))
        loads.append(begun)
    return loads


def taps_of(pieces):
    return max(piece.target + piece.count for piece in pieces)


def arrays_of(pieces):
    return [piece.array for piece in pieces]


def run(kind, body, meta, lens, near, far, outs, scratch, sems, flops=0):
    names, arrays, specs, spread = ["meta", "lens"], [meta, lens], [SMEM, SMEM], {}
    for name, array in near.items():
        names.append(name)
        arrays.append(held(array) if array.size >= MIB else array)
        specs.append(VMEM)
    for name, group in far.items():
        many = isinstance(group, (list, tuple))
        spread[name] = len(group) if many else None
        for number, array in enumerate(group if many else [group]):
            names.append((name, number))
            arrays.append(pltpu.with_memory_space_constraint(array, pltpu.HBM))
            specs.append(ANY)
    shapes, out_specs = [], []
    for name, (shape, dtype, stays) in outs.items():
        names.append(name)
        shapes.append(pltpu.VMEM(shape, dtype) if stays else pltpu.HBM(shape, dtype))
        out_specs.append(VMEM if stays else ANY)
    names += list(scratch) + ["sems"]

    def kernel(*refs):
        found = dict(zip(names, refs))
        for name, count in spread.items():
            if count is None:
                found[name] = found[(name, 0)]
            else:
                found[name] = [found[(name, number)] for number in range(count)]
        found = {name: ref for name, ref in found.items() if isinstance(name, str)}
        copies = Copies(found["sems"])
        body(types.SimpleNamespace(**found), copies)
        copies.finish()

    moved = sum(a.size * a.dtype.itemsize for a in arrays)
    cover = COVER[kind]
    results = pl.pallas_call(
        kernel,
        out_shape=tuple(shapes),
        in_specs=specs,
        out_specs=tuple(out_specs),
        scratch_shapes=[pltpu.VMEM(shape, dtype) for shape, dtype in scratch.values()]
        + [pltpu.SemaphoreType.DMA((sems,))],
        compiler_params=pltpu.CompilerParams(vmem_limit_bytes=LIMIT),
        cost_estimate=pl.CostEstimate(
            flops=max(int(cover * flops), 1), bytes_accessed=int(cover * moved), transcendentals=0
        ),
    )(*arrays)
    return types.SimpleNamespace(**dict(zip(outs, results)))


def groups_of(clips):
    per = min(4, clips)
    return [tuple(range(first, first + per)) for first in range(0, clips, per)]


def span(clip_numbers, frames):
    return slice(clip_numbers[0] * frames, (clip_numbers[-1] + 1) * frames)


def mask_of(len_ref, clip_numbers, frames):
    position = lax.broadcasted_iota(jnp.int32, (1, frames), 1)
    return lanes([(position < len_ref[clip]).astype(F32) for clip in clip_numbers])


def counted_of(len_ref, mask_ref, clip_numbers, frames):
    inside = mask_of(len_ref, clip_numbers, frames)
    return inside * lanes([mask_ref[clip : clip + 1, :].astype(F32) for clip in clip_numbers])


def conv_forward(weight_ref, source_ref, clip_numbers, frames, taps, at=0, waits=()):
    blocks = [source_ref[:, span((clip,), frames)] for clip in clip_numbers]
    total = None
    waits = dict(waits)
    for tap in range(taps):
        wait_all(waits.get(tap, ()))
        moved = lanes([shifted(block, tap - taps // 2) for block in blocks])
        term = jnp.dot(weight_ref[at + tap], moved, preferred_element_type=F32)
        total = term if total is None else total + term
    return total


def conv_backward(weight_ref, grad_ref, clip_numbers, frames, taps, at=0, waits=()):
    blocks = [grad_ref[:, span((clip,), frames)] for clip in clip_numbers]
    total = None
    waits = dict(waits)
    for tap in range(taps):
        wait_all(waits.get(tap, ()))
        moved = lanes([shifted(block, taps // 2 - tap) for block in blocks])
        term = lax.dot_general(
            weight_ref[at + tap],
            moved,
            (((0,), (0,)), ((), ())),
            preferred_element_type=F32,
        )
        total = term if total is None else total + term
    return total


def lookup(meta, lens, ids, book, clips, frames, dim):
    codes = book[0].array.shape[2]
    wide = (dim, clips * frames)

    def body(r, copies):
        loads = load_pieces(copies, book, r.book, r.meta, r.table)
        every = tuple(range(clips))
        inside = mask_of(r.lens, every, frames)
        for group in range(dim // GW):
            rows = slice(group * GW, (group + 1) * GW)
            found = []
            for level, far in ((0, r.q0), (1, r.q1)):
                hot = r.hot.at[level]
                one_hot(r.ids, hot, level, group, clips, frames, dim)
                if group == 0 and level == 0:
                    wait_all(loads)
                value = jnp.dot(r.table[level, rows, :], hot[...], preferred_element_type=F32)
                r.found[level, rows, :] = value.astype(BF16)
                copies.out(r.found.at[level, rows], far.at[rows])
                found.append(value)
            r.u3[rows, :] = (inside * (found[0] + found[1])).astype(BF16)
            copies.out(r.u3.at[rows], r.u3_far.at[rows])

    return run(
        "lookup",
        body,
        meta,
        lens,
        {"ids": ids},
        {"book": arrays_of(book)},
        {
            "u3": (wide, BF16, True),
            "u3_far": (wide, BF16, False),
            "q0": (wide, BF16, False),
            "q1": (wide, BF16, False),
        },
        {
            "table": ((LEVELS, dim, codes), BF16),
            "hot": ((LEVELS, codes, clips * frames), BF16),
            "found": ((LEVELS,) + wide, BF16),
        },
        len(book) + 3 * LEVELS * (dim // GW),
        2 * LEVELS * dim * codes * clips * frames,
    )


def one_hot(ids_ref, hot, level, group, clips, frames, dim):
    number = lax.broadcasted_iota(jnp.int32, (hot.shape[0], frames), 0).astype(jnp.int16)
    one = jnp.ones((), BF16)
    zero = jnp.zeros((), BF16)
    for clip in range(clips):
        at = clip * LEVELS * (dim // GW) + group * LEVELS + level
        row = ids_ref[at : at + 1, :].astype(jnp.int16)
        hot[:, span((clip,), frames)] = jnp.where(number == row, one, zero)


def clip_outs(out_rows, clips, frames):
    return {
        "out%d_%d" % (number, group): ((len(members), count, frames), BF16, False)
        for number, (_, count) in enumerate(out_rows)
        for group, members in enumerate(groups_of(clips))
    }


def clip_results(result, out_rows, clips):
    groups = range(len(groups_of(clips)))
    return [
        [getattr(result, "out%d_%d" % (number, group)) for group in groups]
        for number in range(len(out_rows))
    ]


def put_clips(copies, r, scratch, number, group, value, frames, rows):
    for place, clip in enumerate(group):
        scratch[clip] = value[:, place * frames : (place + 1) * frames]
    at = pl.ds(group[0], len(group))
    for place, (start, count) in enumerate(rows):
        row = 0 if start is None else pl.multiple_of(r.meta[start], 16)
        ref = getattr(r, "out%d_%d" % (place, number))
        copies.out(scratch.at[at, pl.ds(row, count), :], ref)


def decoder_first(meta, lens, u3, w3, bias, clips, frames, dim):
    wide = (dim, clips * frames)
    taps3 = taps_of(w3)

    def body(r, copies):
        loads = load_pieces(copies, w3, r.w3, r.meta, r.t3)
        for number, group in enumerate(groups_of(clips)):
            here = span(group, frames)
            inside = mask_of(r.lens, group, frames)
            waits = waits_of(w3, loads) if number == 0 else ()
            first = conv_forward(r.t3, r.u3, group, frames, taps3, 0, waits) + r.bias[:, 3:4]
            r.first[:, here] = first
            r.u4[:, here] = (inside * elu(first)).astype(BF16)

    return run(
        "decoder_first",
        body,
        meta,
        lens,
        {"u3": u3, "bias": bias},
        {"w3": arrays_of(w3)},
        {"first": (wide, F32, True), "u4": (wide, BF16, True)},
        {"t3": ((taps3, dim, dim), BF16)},
        len(w3),
        2 * taps3 * dim * dim * clips * frames,
    )


def decoder_rest(meta, lens, first, u4, w45, bias, out_rows, clips, frames, dim):
    wide = (dim, clips * frames)
    taps4 = taps_of(w45) - 1
    outs = {"u5": (wide, BF16, True)}
    outs["t45"] = ((taps4 + 1, dim, dim), BF16, True)
    outs.update(clip_outs(out_rows, clips, frames))

    def body(r, copies):
        loads = load_pieces(copies, w45, r.w45, r.meta, r.t45)
        wait_all(loads)
        for number, group in enumerate(groups_of(clips)):
            here = span(group, frames)
            inside = mask_of(r.lens, group, frames)
            second = conv_forward(r.t45, r.u4, group, frames, taps4) + r.bias[:, 4:5]
            r.u5[:, here] = (inside * elu(second)).astype(BF16)
            third = conv_forward(r.t45, r.u5, group, frames, 1, taps4) + r.bias[:, 5:6]
            result = (inside * (r.first[:, here] + third)).astype(BF16)
            put_clips(copies, r, r.work, number, group, result, frames, out_rows)

    return run(
        "decoder_rest",
        body,
        meta,
        lens,
        {"first": first, "u4": u4, "bias": bias},
        {"w45": arrays_of(w45)},
        outs,
        {"work": ((clips, dim, frames), BF16)},
        len(w45) + len(out_rows) * len(groups_of(clips)),
        2 * (taps4 + 1) * dim * dim * clips * frames,
    )


def waits_of(pieces, loads):
    waits = {}
    for piece, load in zip(pieces, loads):
        waits.setdefault(piece.target, []).append(load)
    return waits


class Rows:
    def __init__(self, dim, paired, short=False):
        self.dim = dim
        self.short = short
        self.paired = paired
        self.count = 2 if paired else 1
        self.height = dim // self.count

    def outs(self, columns):
        return {
            "sums%d" % number: ((self.height, columns), BF16, self.paired)
            for number in range(self.count)
        }

    def scratch(self, columns):
        return {} if self.paired else {"sums": ((self.dim, columns), BF16)}

    def put(self, r, copies, at, value):
        if not self.paired:
            r.sums[:, at] = value
            copies.out(r.sums.at[:, at], r.sums0.at[:, at])
            return
        quarter = self.dim // 4
        first = r.meta[1] == 0
        if self.short:
            run_of = quarter // 2
            for i in range(2):
                for j in range(2):
                    row = (j * 4 + i) * run_of
                    zero = value[row : row + run_of]
                    row = (i * 4 + 2 + j) * run_of
                    one = value[row : row + run_of]
                    row = (i * 2 + j) * run_of
                    r.sums0[row : row + run_of, at] = jnp.where(first, zero, one)
                    r.sums1[row : row + run_of, at] = jnp.where(first, one, zero)
            return
        run_of = quarter // 4
        for half in range(2):
            for block in range(4):
                row = half * 2 * quarter + block * run_of
                zero = value[row : row + run_of]
                one = value[row + quarter : row + quarter + run_of]
                row = (block * 2 + half) * run_of
                r.sums0[row : row + run_of, at] = jnp.where(first, zero, one)
                r.sums1[row : row + run_of, at] = jnp.where(first, one, zero)


def weight_grads(r, copies, rows, g, u, taps, offset, clips, frames, dim):
    for tap in range(taps):
        step = taps // 2 - tap
        left = g[...]
        if step != 0:
            for clip in range(clips):
                at = span((clip,), frames)
                r.work[:, at] = shifted(g[:, at], step)
            left = r.work[...]
        value = lax.dot_general(
            left, u[...], (((1,), (1,)), ((), ())), preferred_element_type=F32
        )
        rows.put(r, copies, slice(offset, offset + dim), value.astype(BF16))
        offset += dim
    total = jnp.sum(g[...].astype(F32), axis=1, keepdims=True)
    total = jnp.broadcast_to(total, (dim, 128)).astype(BF16)
    rows.put(r, copies, slice(offset, offset + 128), total)
    return offset + 128


def decoder_backward(
    meta, lens, cotangent, u3, u4, u5, t45, taps3, rows, clips, frames, dim
):
    wide = (dim, clips * frames)
    taps4 = t45.shape[0] - 1
    columns = (taps3 + taps4 + 1) * dim + 3 * 128

    def body(r, copies):
        loads = load_clips(copies, cotangent, r.cot, r.meta, r.clips, groups_of(clips))
        late = copies.start(r.u3, r.s3)
        for group, begun in zip(groups_of(clips), loads):
            here = span(group, frames)
            wait_all(begun)
            inside = mask_of(r.lens, group, frames)
            out = lanes([r.clips[clip] for clip in group])
            out = jnp.where(inside > 0, out, jnp.zeros((), BF16))
            r.g5[:, here] = out
            back = conv_backward(r.t45, r.g5, group, frames, 1, taps4)
            r.g4[:, here] = (back * inside * slope_of(r.u5[:, here])).astype(BF16)
            back = conv_backward(r.t45, r.g4, group, frames, taps4)
            total = out.astype(F32) + back * inside * slope_of(r.u4[:, here])
            r.s_g3[:, here] = total.astype(BF16)
            copies.out(r.s_g3.at[:, here], r.g3.at[:, here])
        sizes = (clips, frames, dim)
        at = weight_grads(r, copies, rows, r.g5, r.u5, 1, 0, *sizes)
        at = weight_grads(r, copies, rows, r.g4, r.u4, taps4, at, *sizes)
        late.wait()
        weight_grads(r, copies, rows, r.s_g3, r.s3, taps3, at, *sizes)

    return run(
        "decoder_backward",
        body,
        meta,
        lens,
        {"u4": u4, "u5": u5, "t45": t45},
        {"cot": arrays_of(cotangent), "u3": u3},
        {"g3": (wide, BF16, False), **rows.outs(columns)},
        {
            "clips": ((clips, dim, frames), BF16),
            "s3": (wide, BF16),
            "g5": (wide, BF16),
            "g4": (wide, BF16),
            "s_g3": (wide, BF16),
            "work": (wide, BF16),
            **rows.scratch(columns),
        },
        (len(cotangent) + 1) * len(groups_of(clips))
        + 1
        + rows.count * (taps3 + taps4 + 4),
        2 * (taps3 + 2 * taps4 + 2) * dim * dim * clips * frames,
    )


def encoder_forward(
    meta, lens, mask, tokens, w012, bias, q0, q1, ahead, g3, clips, frames, dim
):
    wide = (dim, clips * frames)
    groups = groups_of(clips)
    taps0 = taps_of(w012[0])
    weights = [piece for layer in w012 for piece in layer]
    places = (0, taps0, taps0 + 1)

    def body(r, copies):
        loads = load_clips(copies, tokens, r.tokens, r.meta, r.clips, groups[:1])
        begun, refs = [], iter(r.w012)
        for place, layer in zip(places, w012):
            target = r.t.at[pl.ds(place, taps_of(layer))]
            begun.append([p.load(copies, next(refs), r.meta, target) for p in layer])
        loads += load_clips(copies, tokens, r.tokens, r.meta, r.clips, groups[1:])
        late = [copies.start(r.q0, r.s_q0), copies.start(r.q1, r.s_q1)]
        copies.open += load_pieces(copies, ahead, r.ahead, r.meta, r.next)
        copies.out(r.g3, r.g3_near)
        for number, group in enumerate(groups):
            here = span(group, frames)
            wait_all(loads[number])
            inside = mask_of(r.lens, group, frames)
            start = inside * lanes([r.clips[clip] for clip in group]).astype(F32)
            r.s0[:, here] = elu(start).astype(BF16)
            copies.out(r.s0.at[:, here], r.u0.at[:, here])
            if number == 0:
                wait_all(begun[0])
            first = conv_forward(r.t, r.s0, group, frames, taps0) + r.bias[:, 0:1]
            r.s1[:, here] = (inside * elu(first)).astype(BF16)
            copies.out(r.s1.at[:, here], r.u1.at[:, here])
            if number == 0:
                wait_all(begun[1])
                wait_all(begun[2])
            second = conv_forward(r.t, r.s1, group, frames, 1, taps0) + r.bias[:, 1:2]
            r.u2_near[:, here] = elu(inside * (start + second)).astype(BF16)
            copies.out(r.u2_near.at[:, here], r.u2.at[:, here])
            latent = conv_forward(r.t, r.u2_near, group, frames, taps0, taps0 + 1)
            latent = latent + r.bias[:, 2:3]
            if number == 0:
                wait_all(late)
            double = 2.0 * counted_of(r.lens, r.mask, group, frames)
            miss = r.s_q0[:, here].astype(F32) - latent
            r.gq0[:, here] = (double * miss).astype(BF16)
            r.gq1[:, here] = (double * (miss + r.s_q1[:, here].astype(F32))).astype(BF16)

    return run(
        "encoder_forward",
        body,
        meta,
        lens,
        {"mask": mask, "bias": bias},
        {
            "tokens": arrays_of(tokens),
            "w012": arrays_of(weights),
            "q0": q0,
            "q1": q1,
            "ahead": arrays_of(ahead),
            "g3": g3,
        },
        {
            "u0": (wide, BF16, False),
            "u1": (wide, BF16, False),
            "u2": (wide, BF16, False),
            "u2_near": (wide, BF16, True),
            "gq0": (wide, BF16, True),
            "gq1": (wide, BF16, True),
            "next": ((taps_of(ahead), dim, dim), BF16, True),
            "g3_near": (wide, BF16, True),
        },
        {
            "clips": ((clips, dim, frames), BF16),
            "t": ((2 * taps0 + 1, dim, dim), BF16),
            **{name: (wide, BF16) for name in ("s0", "s1", "s_q0", "s_q1")},
        },
        (len(tokens) + 3) * len(groups) + len(ahead) + len(weights) + 3,
        2 * (2 * taps0 + 1) * dim * dim * clips * frames,
    )


def latent_backward(
    meta, lens, ids, g3, t3, gq0, gq1, u2, taps2, codes, ahead, rows, clips, frames, dim
):
    wide = (dim, clips * frames)
    taps3 = t3.shape[0]
    columns = taps2 * dim + 128 + LEVELS * codes

    def body(r, copies):
        copies.open += load_pieces(copies, ahead, r.ahead, r.meta, r.next)
        for group in groups_of(clips):
            here = span(group, frames)
            inside = mask_of(r.lens, group, frames)
            back = conv_backward(r.t3, r.g3, group, frames, taps3)
            extra = BETA * r.gq1[:, here].astype(F32)
            r.g2[:, here] = (back * inside - extra).astype(BF16)
        sizes = (clips, frames, dim)
        offset = weight_grads(r, copies, rows, r.g2, r.u2, taps2, 0, *sizes)
        for level, grad in enumerate((r.gq0, r.gq1)):
            values = []
            for group in range(dim // GW):
                at = slice(group * GW, (group + 1) * GW)
                one_hot(r.ids, r.hot, level, group, clips, frames, dim)
                values.append(
                    lax.dot_general(
                        grad[at, :],
                        r.hot[...],
                        (((1,), (1,)), ((), ())),
                        preferred_element_type=F32,
                    ).astype(BF16)
                )
            value = jnp.concatenate(values, axis=0)
            rows.put(r, copies, slice(offset, offset + codes), value)
            offset += codes

    return run(
        "latent_backward",
        body,
        meta,
        lens,
        {"ids": ids, "g3": g3, "t3": t3, "gq0": gq0, "gq1": gq1, "u2": u2},
        {"ahead": arrays_of(ahead)},
        {
            "g2": (wide, BF16, True),
            "next": ((taps_of(ahead), dim, dim), BF16, True),
            **rows.outs(columns),
        },
        {
            "hot": ((codes, clips * frames), BF16),
            "work": (wide, BF16),
            **rows.scratch(columns),
        },
        len(ahead) + rows.count * (taps2 + 1 + LEVELS),
        2 * ((taps3 + taps2) * dim + LEVELS * codes) * dim * clips * frames,
    )


def encoder_backward(meta, lens, g2, u2, u1, u0, t, taps0, ahead, clips, frames, dim):
    wide = (dim, clips * frames)

    def body(r, copies):
        second = copies.start(r.u2, r.s2)
        first = copies.start(r.u1, r.u1_near)
        copies.out(r.u0, r.u0_near)
        copies.open += load_pieces(copies, ahead, r.ahead, r.meta, r.next)
        for number, group in enumerate(groups_of(clips)):
            here = span(group, frames)
            inside = mask_of(r.lens, group, frames)
            back = conv_backward(r.t, r.g2, group, frames, taps0, 1)
            if number == 0:
                second.wait()
            r.g1[:, here] = (back * inside * slope_of(r.s2[:, here])).astype(BF16)
            back = conv_backward(r.t, r.g1, group, frames, 1)
            if number == 0:
                first.wait()
            r.g0[:, here] = (back * inside * slope_of(r.u1_near[:, here])).astype(BF16)

    names = ("g1", "g0", "u1_near", "u0_near")
    return run(
        "encoder_backward",
        body,
        meta,
        lens,
        {"g2": g2, "t": t},
        {"u2": u2, "u1": u1, "u0": u0, "ahead": arrays_of(ahead)},
        {
            **{name: (wide, BF16, True) for name in names},
            "next": ((taps_of(ahead), dim, dim), BF16, True),
        },
        {"s2": (wide, BF16)},
        len(ahead) + 3,
        2 * (taps0 + 1) * dim * dim * clips * frames,
    )


def encoder_grads(meta, lens, g0, u0, g1, u1, taps0, rows, clips, frames, dim):
    columns = (taps0 + 1) * dim + 2 * 128

    def body(r, copies):
        sizes = (clips, frames, dim)
        at = weight_grads(r, copies, rows, r.g0, r.u0, taps0, 0, *sizes)
        weight_grads(r, copies, rows, r.g1, r.u1, 1, at, *sizes)

    return run(
        "encoder_grads",
        body,
        meta,
        lens,
        {"g0": g0, "u0": u0, "g1": g1, "u1": u1},
        {},
        rows.outs(columns),
        {"work": ((dim, clips * frames), BF16), **rows.scratch(columns)},
        1 + rows.count * (taps0 + 3),
        2 * (taps0 + 1) * dim * dim * clips * frames,
    )


def tokens_backward(meta, lens, g0, u0, g1, t, out_rows, clips, frames, dim):
    taps0 = t.shape[0]

    def body(r, copies):
        for number, group in enumerate(groups_of(clips)):
            here = span(group, frames)
            inside = mask_of(r.lens, group, frames)
            back = conv_backward(r.t, r.g0, group, frames, taps0)
            total = r.g1[:, here].astype(F32) + back * inside * slope_of(r.u0[:, here])
            total = (inside * total).astype(BF16)
            put_clips(copies, r, r.work, number, group, total, frames, out_rows)

    result = run(
        "tokens_backward",
        body,
        meta,
        lens,
        {"g0": g0, "g1": g1, "u0": u0, "t": t},
        {},
        clip_outs(out_rows, clips, frames),
        {"work": ((clips, dim, frames), BF16)},
        len(out_rows) * len(groups_of(clips)),
        2 * taps0 * dim * dim * clips * frames,
    )
    return clip_results(result, out_rows, clips)


def unpack(meta, pieces, blocks, half):
    outs = []
    for taps, width, has_bias in blocks:
        outs.append(struct((taps, half, width), F32))
        if has_bias:
            outs.append(struct((1, half), F32))

    def body(meta_ref, mine_ref, other_ref, *refs):
        take = iter(refs)
        first = meta_ref[1] == 0

        def columns(at):
            mine, other = mine_ref[:, at], other_ref[:, at]
            return jnp.concatenate(
                [jnp.where(first, mine, other), jnp.where(first, other, mine)], axis=0
            ).astype(F32)

        offset = 0
        for taps, width, has_bias in blocks:
            out = next(take)
            for tap in range(taps):
                out[tap] = columns(slice(offset, offset + width))
                offset += width
            if has_bias:
                next(take)[...] = columns(slice(offset, offset + 128)).T[0:1]
                offset += 128

    return pl.pallas_call(
        body,
        out_shape=tuple(outs),
        in_specs=[SMEM, VMEM, VMEM],
        out_specs=tuple(VMEM for _ in outs),
        compiler_params=pltpu.CompilerParams(vmem_limit_bytes=LIMIT),
    )(meta, *pieces)


def in_three(array, rows, columns):
    terms = []
    for _ in range(3):
        term = lax.reduce_precision(array, exponent_bits=8, mantissa_bits=7)
        terms.append(term.astype(BF16).reshape(-1))
        array = array - term
    terms = jnp.concatenate(terms)
    return jnp.pad(terms, (0, rows * columns - terms.size)).reshape(1, rows, columns)


def from_three(block, shape):
    size = shape[0] * shape[1]
    terms = block.reshape(-1)[: 3 * size].reshape((3,) + shape).astype(F32)
    return (terms[0] + terms[1]) + terms[2]


class Pairs:
    BITS = {"core": 1, "x": 2, "zl": 4, "zh": 8}

    def __init__(self, rows, clips):
        self.chan = lax.axis_index("chan")
        self.dp = lax.axis_index("dp")
        self.core = self.bit("core")
        x = self.bit("x")
        other = (1 - self.chan) * rows
        piece = rows // 4
        here = [(self.core, x), (self.core, 1 - x), (1 - self.core, x), (1 - self.core, 1 - x)]
        self.piece = (self.core * 2 + x) * piece
        self.meta = jnp.stack(
            [self.chan, self.core, self.chan * rows, other]
            + [other + (c * 2 + b) * piece for c, b in here]
            + [self.chan * clips]
            + [other + self.core * 2 * piece, other + (1 - self.core) * 2 * piece]
        ).astype(jnp.int32)

    def bit(self, name):
        if name == "chan":
            return self.chan
        return (self.dp & self.BITS[name]) // self.BITS[name]

    def swap(self, value, name):
        if name == "chan":
            return lax.ppermute(value, "chan", [(0, 1), (1, 0)])
        mask = self.BITS[name]
        return lax.ppermute(value, "dp", [(i, i ^ mask) for i in range(16)])

    def swap_by_core(self, value, names):
        pairs = []
        for place in range(32):
            other = place
            for name in names[(place // 2) & 1].split("+"):
                other ^= 1 if name == "chan" else 2 * self.BITS[name]
            pairs.append((place, other))
        return lax.ppermute(value, ("dp", "chan"), pairs)

    def bit_by_core(self, names):
        return jnp.where(self.core == 0, self.bit(names[0]), self.bit(names[1]))

    def piece_of(self, own):
        return lax.dynamic_slice_in_dim(own, self.piece, own.shape[1] // 4, 1)

    def half_of(self, own):
        half = own.shape[1] // 2
        return lax.dynamic_slice_in_dim(own, self.core * half, half, 1)

    def spread(self, near):
        far = self.swap(near, "x")
        return near, far, self.swap(near, "core"), self.swap(far, "core")

    def ordered(self, own, came):
        first = self.chan == 0
        return jnp.concatenate([jnp.where(first, own, came), jnp.where(first, came, own)])

    @property
    def bits(self):
        return jnp.stack([self.bit_by_core(pair) for pair in PAIRS]).astype(jnp.int32)

    def start(self, grads, steps):
        kept, sent = grads
        return Reduction(self, kept, self.swap(sent, "core"), steps)


XZ, ZX, CC, HH = ("x", "zl"), ("zl", "x"), ("chan", "chan"), ("zh", "zh")
PAIRS = (XZ, ZX, CC, HH)
START = (("halve", XZ), ("halve2", ZX, CC), ("keep", HH))
STEPS_2 = START + (("double", ZX), ("double", XZ), ("double", ("core", "core")))
STEPS_4 = START + (("double2", ZX, XZ), ("double", ("core", "core")))
STEPS = STEPS_2, STEPS_2, STEPS_4


class Reduction:
    def __init__(self, links, kept, came, steps):
        self.links = links
        self.steps = steps
        self.at = 0
        self.terms = [(kept, 0)]
        self.came = [came]
        self.value = None
        self.cuts = [PAIRS.index(n) for kind, *names in steps if "halve" in kind for n in names]
        self.cut = 0

    @property
    def done(self):
        return self.at == len(self.steps)

    @property
    def result(self):
        return [self.value] + self.came

    def plan(self):
        if self.value is not None:
            how = self.steps[self.at - 1][0]
            lead = {"keep": (), "double": (2,), "double2": (2, 2)}[how]
            return how, [self.value] + self.came, [lead + self.value.shape]
        self.terms += [(array, self.cut) for array in self.came]
        how = self.steps[self.at][0]
        last = self.cut + {"halve": 1, "halve2": 2}.get(how, 0)
        blocks = [
            term.reshape((2,) * (last - first) + (-1, term.shape[-1]))
            for term, first in self.terms
        ]
        return how, blocks, [blocks[0].shape[-2:]] * (3 if how == "halve2" else 1)

    def fill(self, how, refs, outs, bits):
        if self.value is not None:
            places = [bits[PAIRS.index(n)] for n in self.steps[self.at - 1][1:] if n in PAIRS]
            if how == "keep":
                total = refs[0][...].astype(F32) + refs[1][...].astype(F32)
                outs[0][...] = total.astype(BF16)
            elif how == "double":
                outs[0][places[0]] = refs[0][...]
                outs[0][1 - places[0]] = refs[1][...]
            else:
                inner, outer = places
                outs[0][outer, inner] = refs[0][...]
                outs[0][outer, 1 - inner] = refs[1][...]
                outs[0][1 - outer, inner] = refs[2][...]
                outs[0][1 - outer, 1 - inner] = refs[3][...]
            return
        flips = {"halve": ((1,),), "halve2": ((1, 0), (0, 1), (1, 1))}.get(how, ((),))
        for out, flip in zip(outs, flips):
            place = [bits[cut] for cut in self.cuts[: self.cut]]
            for cut, turned in zip(self.cuts[self.cut :], flip):
                place.append(1 - bits[cut] if turned else bits[cut])
            sums = None
            for ref, (_, first) in zip(refs, self.terms):
                where = tuple(place[first:])
                piece = (ref[where] if where else ref[...]).astype(F32)
                sums = piece if sums is None else sums + piece
            out[...] = sums.astype(BF16)

    def send(self, sent):
        kind, *names = self.steps[self.at]
        sent = [array.reshape(-1, array.shape[-1]) for array in sent]
        if "halve" in kind:
            self.cut += len(names)
        else:
            self.value = sent[0]
        if len(names) == 2:
            names.append(tuple(a + "+" + b for a, b in zip(*names)))
        sent = sent * len(names) if len(sent) == 1 else sent
        self.came = [self.links.swap_by_core(a, n) for a, n in zip(sent, names)]
        self.at += 1


def advance(after, *reductions):
    came = lax.optimization_barrier((tuple(r.came for r in reductions), tuple(after)))[0]
    arrays, counts, shapes, widths, hows = [], [], [], [], []
    for reduction, array in zip(reductions, came):
        reduction.came = list(array)
        how, operands, targets = reduction.plan()
        hows.append(how)
        counts.append(len(operands))
        widths.append(len(targets))
        arrays += [held(operand) for operand in operands]
        shapes += [pltpu.VMEM(target, BF16) for target in targets]

    def body(bits_ref, *refs):
        taken, filled = 0, len(arrays)
        for reduction, how, count, width in zip(reductions, hows, counts, widths):
            outs = refs[filled : filled + width]
            reduction.fill(how, refs[taken : taken + count], outs, bits_ref)
            taken += count
            filled += width

    sent = pl.pallas_call(
        body,
        out_shape=tuple(shapes),
        in_specs=[SMEM] + [VMEM] * len(arrays),
        out_specs=tuple(VMEM for _ in shapes),
        compiler_params=pltpu.CompilerParams(vmem_limit_bytes=8 * MIB),
        cost_estimate=pl.CostEstimate(
            flops=COVER["advance"], bytes_accessed=COVER["advance"], transcendentals=0
        ),
    )(reductions[0].links.bits, *arrays)
    filled = 0
    for reduction, width in zip(reductions, widths):
        reduction.send(sent[filled : filled + width])
        filled += width
    return list(sent)


def on_pairs(
    tokens,
    lengths,
    frame_mask,
    code_ids,
    cotangent,
    weights,
    biases,
    codebook,
):
    chan = 2
    rows = tokens.shape[1]
    frames = tokens.shape[2]
    dim = rows * chan
    clips = tokens.shape[0] // chan
    codes = codebook.shape[2]
    sizes = (clips, frames, dim)
    links = Pairs(rows, clips)
    meta = links.meta
    mine = functools.partial(
        lax.dynamic_slice_in_dim, start_index=links.chan * clips, slice_size=clips, axis=0
    )
    others = functools.partial(
        lax.dynamic_slice_in_dim, start_index=(1 - links.chan) * clips, slice_size=clips, axis=0
    )
    taps = [w.shape[0] for w in weights]
    own, other, pieces, halves = 2, 3, (4, 5, 6, 7), (9, 10)

    split = taps[3] - 1
    lens = mine(lengths)
    mask = mine(frame_mask)
    ids = mine(code_ids).reshape(-1, frames)
    bias = jnp.stack(biases + (jnp.zeros_like(biases[0]),) * 2)
    first_pieces = lax.optimization_barrier(
        (
            links.piece_of(codebook),
            links.piece_of(weights[3][:split]),
            links.half_of(weights[3][split:]),
        )
    )
    near_book, near3a, near3b = (links.swap(piece, "chan") for piece in first_pieces)
    dec = jnp.concatenate([weights[4], weights[5]])
    dec_piece = jnp.concatenate([links.piece_of(dec), in_three(bias, rows // 4, dim)])
    enc = jnp.concatenate([weights[0], weights[1], weights[2]])
    near_book, dec_piece, enc_piece, cot_send, tok_send = lax.optimization_barrier(
        (near_book, dec_piece, links.piece_of(enc), others(cotangent), others(tokens))
    )
    far_book = links.spread(near_book)
    near45 = links.swap(dec_piece, "chan")
    far3a = links.spread(near3a)
    near012 = links.swap(enc_piece, "chan")
    cot_send = tie(cot_send, near3a)
    cot_other = links.swap(cot_send, "chan")
    book = [Piece(codebook, own)] + [Piece(a, s) for a, s in zip(far_book, pieces)]
    found = lookup(meta, lens, tie(ids, cot_send, tok_send), book, *sizes)
    tok_send = tie(tok_send, found.u3)
    tok_other = links.swap(tok_send, "chan")
    near3b, near45 = tie((near3b, near45), found.u3)
    far3b = near3b, links.swap(near3b, "core")
    bias_came = from_three(near45[taps[4] + taps[5] :], bias.shape)
    bias = links.ordered(bias.T, bias_came.T)
    w3 = [Piece(weights[3], own, 0, 0, split)]
    w3 += [Piece(a, s) for a, s in zip(far3a, pieces)]
    w3 += [Piece(weights[3], own, split, split, taps[3] - split)]
    w3 += [Piece(a, s, 0, split) for a, s in zip(far3b, halves)]
    far45_x = links.swap(near45, "x")
    dec_first = decoder_first(
        meta, lens, found.u3, w3, bias, *sizes
    )
    near45, far45_x = tie((near45, far45_x), dec_first.u4)
    far45 = near45, far45_x, links.swap(near45, "core"), links.swap(far45_x, "core")
    w45 = [Piece(weights[4], own), Piece(weights[5], own, 0, taps[4])]
    w45 += [Piece(a, s, 0, 0, taps[4] + taps[5]) for a, s in zip(far45, pieces)]
    out_rows = ((own, rows), (other, rows))
    dec_out = decoder_rest(
        meta, lens, dec_first.first, dec_first.u4, w45, bias, out_rows, *sizes
    )
    near012 = tie(near012, dec_out.u5)
    far012_x = links.swap(near012, "x")
    rows_a = rows_c = rows_d = Rows(dim, True)
    cot = [Piece(cotangent, own, clip=8, count=clips)]
    cot.append(Piece(tie(cot_other, near012), other))
    dec_back = decoder_backward(
        meta,
        lens,
        cot,
        found.u3_far,
        dec_first.u4,
        dec_out.u5,
        dec_out.t45,
        taps[3],
        rows_a,
        *sizes,
    )
    near012, far012_x = tie((near012, far012_x), dec_back.g3)
    far012 = near012, far012_x, links.swap(near012, "core"), links.swap(far012_x, "core")

    def enc_pieces(which):
        listed = []
        place = 0
        for number in which:
            listed.append(Piece(weights[number], own, 0, place))
            place += taps[number]
        start = sum(taps[: which[0]])
        listed += [Piece(a, s, start, 0, place) for a, s in zip(far012, pieces)]
        return listed

    red_a = links.start([dec_back.sums0, tie(dec_back.sums1, tok_other)], STEPS[0])
    out_own, out_send = clip_results(dec_out, out_rows, clips)
    out_send[0] = tie(out_send[0], tok_other)
    out_came = [links.swap(out_send[0], "chan")]
    tok = [Piece(tokens, own, clip=8, count=clips)]
    tok.append(Piece(tie(tok_other, dec_back.g3, out_send[0]), other))
    enc_out = encoder_forward(
        meta,
        lens,
        mask,
        tok,
        [enc_pieces([0]), enc_pieces([1]), enc_pieces([2])],
        bias,
        found.q0,
        found.q1,
        w3,
        dec_back.g3,
        *sizes,
    )
    sent = advance([enc_out.u2], red_a)
    out_came.append(links.swap(tie(out_send[1], *sent), "chan"))
    lat = latent_backward(
        meta,
        lens,
        ids,
        tie(enc_out.g3_near, out_came[0], *sent),
        enc_out.next,
        enc_out.gq0,
        enc_out.gq1,
        enc_out.u2_near,
        taps[2],
        codes,
        enc_pieces([1, 2]),
        rows_c,
        *sizes,
    )
    red_c = links.start([lat.sums0, lat.sums1], STEPS[1])
    sent = advance([lat.g2], red_a)
    enc_back = encoder_backward(
        meta,
        lens,
        lat.g2,
        tie(enc_out.u2, out_came[1], *sent),
        enc_out.u1,
        enc_out.u0,
        lat.next,
        taps[0],
        enc_pieces([0]),
        *sizes,
    )
    sent = advance([enc_back.g0], red_c)
    enc_sums = encoder_grads(
        meta,
        lens,
        tie(enc_back.g0, *sent),
        enc_back.u0_near,
        enc_back.g1,
        enc_back.u1_near,
        taps[0],
        rows_d,
        *sizes,
    )
    red_d = links.start([enc_sums.sums0, enc_sums.sums1], STEPS[2])
    sent = advance([enc_sums.sums0], red_a)
    grad_own, grad_other = tokens_backward(
        meta,
        lens,
        tie(enc_back.g0, *sent),
        enc_back.u0_near,
        enc_back.g1,
        enc_back.next,
        out_rows,
        *sizes,
    )
    sent = advance(grad_other, *([red_a] if A_EARLY else []), red_c, red_d)
    grad_came = []
    if len(GRAD_SLOTS) == 4:
        grad_other = [g[at : at + clips // 4] for g in grad_other for at in (0, clips // 4)]
    shapes = {
        red_a: [(1, dim, True), (taps[4], dim, True), (taps[3], dim, True)],
        red_c: [(taps[2], dim, True), (LEVELS, codes, False)],
        red_d: [(taps[0], dim, True), (1, dim, True)],
    }
    results = {}
    slot = 0
    groups = (red_a, red_c, red_d)
    while not all(r.done for r in groups):
        slot += 1
        for half, (begin, end) in enumerate(GRAD_SLOTS):
            if slot == begin:
                grad_came.append(links.swap(tie(grad_other[half], *sent), "chan"))
        for half, (begin, end) in enumerate(GRAD_SLOTS):
            if slot == end:
                sent = list(sent) + [grad_came[half]]
        active = [r for r in groups if not r.done]
        for r in groups:
            if r.done and r not in results:
                mine_rows, other_rows = r.result
                mine_rows = tie(mine_rows, *sent)
                results[r] = unpack(meta, [mine_rows, other_rows], shapes[r], rows)
                sent = list(sent) + list(results[r][:1])
        if slot == OUT_SLOTS[0]:
            came = jnp.concatenate(tie(out_came, *sent))
            output = links.ordered(jnp.concatenate(out_own), came)
            sent = list(sent) + [output]
        if slot == OUT_SLOTS[1]:
            came = jnp.concatenate(tie(grad_came, *sent)).astype(F32)
            tokens_grad = links.ordered(jnp.concatenate(grad_own).astype(F32), came)
            sent = list(sent) + [tokens_grad]
        sent = advance(sent, *active)
    if slot < OUT_SLOTS[1]:
        came = jnp.concatenate(tie(grad_came, *sent)).astype(F32)
        tokens_grad = links.ordered(jnp.concatenate(grad_own).astype(F32), came)
    for r in groups:
        if r not in results:
            results[r] = unpack(meta, r.result, shapes[r], rows)
    a, c, d = results[red_a], results[red_c], results[red_d]
    w_grads = [d[0], d[2], c[0], a[4], a[2], a[0]]
    b_grads = [v.reshape(rows) for v in (d[1], d[3], c[1], a[5], a[3], a[1])]
    grads = [g for pair in zip(w_grads, b_grads) for g in pair]
    return (output, tokens_grad, *grads, c[2])


def on_others(
    tokens,
    lengths,
    frame_mask,
    code_ids,
    cotangent,
    weights,
    biases,
    codebook,
):
    chan = lax.axis_size("chan")
    place = lax.axis_index("chan")
    rows = tokens.shape[1]
    frames = tokens.shape[2]
    dim = rows * chan
    clips = tokens.shape[0] // chan
    codes = codebook.shape[2]
    sizes = (clips, frames, dim)
    meta = jnp.zeros((9,), jnp.int32)
    mine = functools.partial(
        lax.dynamic_slice_in_dim, start_index=place * clips, slice_size=clips, axis=0
    )
    taps = [w.shape[0] for w in weights]

    def gathered(*arrays):
        return [Piece(lax.all_gather(jnp.concatenate(arrays), "chan", axis=1, tiled=True))]

    def part(pieces, start, count):
        return [Piece(pieces[0].array, None, start, 0, count)]

    def clips_in(array):
        return [Piece(lax.all_to_all(array, "chan", 0, 1, tiled=True))]

    def clips_out(array):
        return lax.all_to_all(array, "chan", 1, 0, tiled=True)

    def reduced(grads):
        part = lax.psum_scatter(grads.astype(F32), "chan", scatter_dimension=0, tiled=True)
        return lax.psum(part, "dp")

    def columns(total, offset, count, width):
        block = total[:, offset : offset + count * width].reshape(rows, count, width)
        return jnp.transpose(block, (1, 0, 2))

    bias = jnp.stack(biases + (jnp.zeros_like(biases[0]),) * 2, axis=1)
    bias = lax.all_gather(bias, "chan", axis=0, tiled=True)
    lens = mine(lengths)
    mask = mine(frame_mask)
    ids = mine(code_ids).reshape(-1, frames)
    w3 = gathered(weights[3])
    w45 = gathered(weights[4], weights[5])
    w012 = gathered(weights[0], weights[1], weights[2])
    rows_of = Rows(dim, False)
    out_rows = ((None, dim),)
    found = lookup(meta, lens, ids, gathered(codebook), *sizes)
    dec_first = decoder_first(meta, lens, found.u3, w3, bias, *sizes)
    dec_out = decoder_rest(
        meta, lens, dec_first.first, dec_first.u4, w45, bias, out_rows, *sizes
    )
    dec_back = decoder_backward(
        meta,
        lens,
        clips_in(cotangent),
        found.u3_far,
        dec_first.u4,
        dec_out.u5,
        dec_out.t45,
        taps[3],
        rows_of,
        *sizes,
    )
    enc_out = encoder_forward(
        meta,
        lens,
        mask,
        clips_in(tokens),
        [
            part(w012, 0, taps[0]),
            part(w012, taps[0], taps[1]),
            part(w012, taps[0] + taps[1], taps[2]),
        ],
        bias,
        found.q0,
        found.q1,
        w3,
        dec_back.g3,
        *sizes,
    )
    lat = latent_backward(
        meta,
        lens,
        ids,
        enc_out.g3_near,
        enc_out.next,
        enc_out.gq0,
        enc_out.gq1,
        enc_out.u2_near,
        taps[2],
        codes,
        part(w012, taps[0], 1 + taps[2]),
        rows_of,
        *sizes,
    )
    enc_back = encoder_backward(
        meta,
        lens,
        lat.g2,
        enc_out.u2,
        enc_out.u1,
        enc_out.u0,
        lat.next,
        taps[0],
        part(w012, 0, taps[0]),
        *sizes,
    )
    enc_sums = encoder_grads(
        meta,
        lens,
        enc_back.g0,
        enc_back.u0_near,
        enc_back.g1,
        enc_back.u1_near,
        taps[0],
        rows_of,
        *sizes,
    )
    ((grad,),) = tokens_backward(
        meta,
        lens,
        enc_back.g0,
        enc_back.u0_near,
        enc_back.g1,
        enc_back.next,
        out_rows,
        *sizes,
    )
    ((out,),) = clip_results(dec_out, out_rows, clips)
    a, c, d = (reduced(x.sums0) for x in (dec_back, lat, enc_sums))
    placed = (
        (d, 0, taps[0]),
        (d, taps[0] * dim + 128, 1),
        (c, 0, taps[2]),
        (a, (1 + taps[4]) * dim + 256, taps[3]),
        (a, dim + 128, taps[4]),
        (a, 0, 1),
    )
    grads = []
    for total, start, count in placed:
        grads.append(columns(total, start, count, dim))
        grads.append(total[:, start + count * dim])
    books = columns(c, taps[2] * dim + 128, LEVELS, codes)
    return (clips_out(out), clips_out(grad).astype(F32), *grads, books)


def on_device(step, tokens, lengths, frame_mask, code_ids, cotangent, *params):
    weights, biases = params[0:12:2], params[1:12:2]
    return step(
        tokens, lengths, frame_mask, code_ids, cotangent, weights, biases, params[12]
    )


def solution(mesh):
    paired = mesh.shape["chan"] == 2 and mesh.shape["dp"] == 16
    weight = P(None, "chan", None)
    vector = P("chan")
    clip_rows = P("dp", "chan", None)
    in_specs = (
        (clip_rows, P("dp"), P("dp", None), P("dp", None, None), clip_rows)
        + (weight, vector) * 6
        + (weight,)
    )
    out_specs = (clip_rows, clip_rows) + (weight, vector) * 6 + (weight,)
    return jax.shard_map(
        functools.partial(on_device, on_pairs if paired else on_others),
        mesh=mesh,
        in_specs=in_specs,
        out_specs=out_specs,
        check_vma=False,
    )
```

```python
import functools
import types

import jax
import jax.numpy as jnp
from jax import lax
from jax.experimental import pallas as pl
from jax.experimental.pallas import tpu as pltpu
from jax.sharding import PartitionSpec as P

LEVELS = 2
GW = 256
BETA = 0.25
F32 = jnp.float32
BF16 = jnp.bfloat16
MIB = 1024 * 1024
LIMIT = 28 * MIB
GRAD_SLOTS = ((1, 3), (2, 5))
OUT_SLOTS = (2, 6)
A_EARLY = False
COVER = {
    "lookup": 0.01,
    "decoder_first": 0.01,
    "decoder_rest": 0.01,
    "decoder_backward": 0.01,
    "encoder_forward": 10,
    "latent_backward": 10,
    "encoder_backward": 10,
    "encoder_grads": 10,
    "tokens_backward": 10,
    "advance": 0,
}

ANY = pl.BlockSpec(memory_space=pl.ANY)
VMEM = pl.BlockSpec(memory_space=pltpu.VMEM)
SMEM = pl.BlockSpec(memory_space=pltpu.SMEM)


def elu(value):
    return jnp.where(value > 0, value, jnp.exp(jnp.minimum(value, 0.0)) - 1.0)


def slope_of(activated):
    act = activated.astype(F32)
    return jnp.where(act > 0, 1.0, 1.0 + act)


def shifted(value, step):
    if step == 0:
        return value
    edge = jnp.zeros((value.shape[0], abs(step)), value.dtype)
    if step > 0:
        return jnp.concatenate([value[:, step:], edge], axis=1)
    return jnp.concatenate([edge, value[:, :step]], axis=1)


def lanes(blocks):
    return blocks[0] if len(blocks) == 1 else jnp.concatenate(blocks, axis=1)


def tie(value, *earlier):
    earlier = [array for array in earlier if array is not None]
    if not earlier:
        return value
    return lax.optimization_barrier((value, tuple(earlier)))[0]


def held(array):
    return pltpu.with_memory_space_constraint(array, pltpu.VMEM)


def struct(shape, dtype):
    return jax.ShapeDtypeStruct(shape, dtype)


class Copies:
    def __init__(self, sems):
        self.sems = sems
        self.used = 0
        self.open = []

    def start(self, source, target):
        copy = pltpu.make_async_copy(source, target, self.sems.at[self.used])
        self.used += 1
        copy.start()
        return copy

    def out(self, source, target):
        self.open.append(self.start(source, target))

    def finish(self):
        for copy in self.open:
            copy.wait()


def wait_all(copies):
    for copy in copies:
        copy.wait()


class Piece:
    def __init__(self, array, row=None, source=0, target=0, count=None, clip=None):
        self.array = array
        self.row = row
        self.source = source
        self.target = target
        self.count = array.shape[0] if count is None else count
        self.clip = clip

    def load(self, copies, ref, meta_ref, scratch):
        rows = ref.shape[1]
        row = 0 if self.row is None else pl.multiple_of(meta_ref[self.row], 16)
        first = self.source if self.clip is None else meta_ref[self.clip]
        return copies.start(
            ref.at[pl.ds(first, self.count)],
            scratch.at[pl.ds(self.target, self.count), pl.ds(row, rows), :],
        )


def load_pieces(copies, pieces, refs, meta_ref, scratch):
    return [p.load(copies, ref, meta_ref, scratch) for p, ref in zip(pieces, refs)]


def load_clips(copies, pieces, refs, meta_ref, scratch, groups):
    loads = []
    for group in groups:
        begun = []
        for p, ref in zip(pieces, refs):
            part = Piece(p.array, p.row, group[0], group[0], len(group))
            if p.clip is not None:
                start = meta_ref[p.clip]
                ref = ref.at[pl.ds(start, scratch.shape[0])]
            begun.append(part.load(copies, ref, meta_ref, scratch))
        loads.append(begun)
    return loads


def taps_of(pieces):
    return max(piece.target + piece.count for piece in pieces)


def arrays_of(pieces):
    return [piece.array for piece in pieces]


def run(kind, body, meta, lens, near, far, outs, scratch, sems, flops=0):
    names, arrays, specs, spread = ["meta", "lens"], [meta, lens], [SMEM, SMEM], {}
    for name, array in near.items():
        names.append(name)
        arrays.append(held(array) if array.size >= MIB else array)
        specs.append(VMEM)
    for name, group in far.items():
        many = isinstance(group, (list, tuple))
        spread[name] = len(group) if many else None
        for number, array in enumerate(group if many else [group]):
            names.append((name, number))
            arrays.append(pltpu.with_memory_space_constraint(array, pltpu.HBM))
            specs.append(ANY)
    shapes, out_specs = [], []
    for name, (shape, dtype, stays) in outs.items():
        names.append(name)
        shapes.append(pltpu.VMEM(shape, dtype) if stays else pltpu.HBM(shape, dtype))
        out_specs.append(VMEM if stays else ANY)
    names += list(scratch) + ["sems"]

    def kernel(*refs):
        found = dict(zip(names, refs))
        for name, count in spread.items():
            if count is None:
                found[name] = found[(name, 0)]
            else:
                found[name] = [found[(name, number)] for number in range(count)]
        found = {name: ref for name, ref in found.items() if isinstance(name, str)}
        copies = Copies(found["sems"])
        body(types.SimpleNamespace(**found), copies)
        copies.finish()

    moved = sum(a.size * a.dtype.itemsize for a in arrays)
    cover = COVER[kind]
    results = pl.pallas_call(
        kernel,
        out_shape=tuple(shapes),
        in_specs=specs,
        out_specs=tuple(out_specs),
        scratch_shapes=[pltpu.VMEM(shape, dtype) for shape, dtype in scratch.values()]
        + [pltpu.SemaphoreType.DMA((sems,))],
        compiler_params=pltpu.CompilerParams(vmem_limit_bytes=LIMIT),
        cost_estimate=pl.CostEstimate(
            flops=max(int(cover * flops), 1), bytes_accessed=int(cover * moved), transcendentals=0
        ),
    )(*arrays)
    return types.SimpleNamespace(**dict(zip(outs, results)))


def groups_of(clips):
    per = min(4, clips)
    return [tuple(range(first, first + per)) for first in range(0, clips, per)]


def span(clip_numbers, frames):
    return slice(clip_numbers[0] * frames, (clip_numbers[-1] + 1) * frames)


def mask_of(len_ref, clip_numbers, frames):
    position = lax.broadcasted_iota(jnp.int32, (1, frames), 1)
    return lanes([(position < len_ref[clip]).astype(F32) for clip in clip_numbers])


def counted_of(len_ref, mask_ref, clip_numbers, frames):
    inside = mask_of(len_ref, clip_numbers, frames)
    return inside * lanes([mask_ref[clip : clip + 1, :].astype(F32) for clip in clip_numbers])


def conv_forward(weight_ref, source_ref, clip_numbers, frames, taps, at=0, waits=()):
    blocks = [source_ref[:, span((clip,), frames)] for clip in clip_numbers]
    total = None
    waits = dict(waits)
    for tap in range(taps):
        wait_all(waits.get(tap, ()))
        moved = lanes([shifted(block, tap - taps // 2) for block in blocks])
        term = jnp.dot(weight_ref[at + tap], moved, preferred_element_type=F32)
        total = term if total is None else total + term
    return total


def conv_backward(weight_ref, grad_ref, clip_numbers, frames, taps, at=0, waits=()):
    blocks = [grad_ref[:, span((clip,), frames)] for clip in clip_numbers]
    total = None
    waits = dict(waits)
    for tap in range(taps):
        wait_all(waits.get(tap, ()))
        moved = lanes([shifted(block, taps // 2 - tap) for block in blocks])
        term = lax.dot_general(
            weight_ref[at + tap],
            moved,
            (((0,), (0,)), ((), ())),
            preferred_element_type=F32,
        )
        total = term if total is None else total + term
    return total


def lookup(meta, lens, ids, book, clips, frames, dim):
    codes = book[0].array.shape[2]
    wide = (dim, clips * frames)

    def body(r, copies):
        loads = load_pieces(copies, book, r.book, r.meta, r.table)
        every = tuple(range(clips))
        inside = mask_of(r.lens, every, frames)
        for group in range(dim // GW):
            rows = slice(group * GW, (group + 1) * GW)
            found = []
            for level, far in ((0, r.q0), (1, r.q1)):
                hot = r.hot.at[level]
                one_hot(r.ids, hot, level, group, clips, frames, dim)
                if group == 0:
                    wait_all(waits_of(book, loads).get(level, ()))
                value = jnp.dot(r.table[level, rows, :], hot[...], preferred_element_type=F32)
                r.found[level, rows, :] = value.astype(BF16)
                copies.out(r.found.at[level, rows], far.at[rows])
                found.append(value)
            r.u3[rows, :] = (inside * (found[0] + found[1])).astype(BF16)
            copies.out(r.u3.at[rows], r.u3_far.at[rows])

    return run(
        "lookup",
        body,
        meta,
        lens,
        {"ids": ids},
        {"book": arrays_of(book)},
        {
            "u3": (wide, BF16, True),
            "u3_far": (wide, BF16, False),
            "q0": (wide, BF16, False),
            "q1": (wide, BF16, False),
        },
        {
            "table": ((LEVELS, dim, codes), BF16),
            "hot": ((LEVELS, codes, clips * frames), BF16),
            "found": ((LEVELS,) + wide, BF16),
        },
        len(book) + 3 * LEVELS * (dim // GW),
        2 * LEVELS * dim * codes * clips * frames,
    )


def one_hot(ids_ref, hot, level, group, clips, frames, dim):
    number = lax.broadcasted_iota(jnp.int32, (hot.shape[0], frames), 0).astype(jnp.int16)
    one = jnp.ones((), BF16)
    zero = jnp.zeros((), BF16)
    for clip in range(clips):
        at = clip * LEVELS * (dim // GW) + group * LEVELS + level
        row = ids_ref[at : at + 1, :].astype(jnp.int16)
        hot[:, span((clip,), frames)] = jnp.where(number == row, one, zero)


def clip_outs(out_rows, clips, frames):
    return {
        "out%d_%d" % (number, group): ((len(members), count, frames), BF16, False)
        for number, (_, count) in enumerate(out_rows)
        for group, members in enumerate(groups_of(clips))
    }


def clip_results(result, out_rows, clips):
    groups = range(len(groups_of(clips)))
    return [
        [getattr(result, "out%d_%d" % (number, group)) for group in groups]
        for number in range(len(out_rows))
    ]


def put_clips(copies, r, scratch, number, group, value, frames, rows):
    for place, clip in enumerate(group):
        scratch[clip] = value[:, place * frames : (place + 1) * frames]
    at = pl.ds(group[0], len(group))
    for place, (start, count) in enumerate(rows):
        row = 0 if start is None else pl.multiple_of(r.meta[start], 16)
        ref = getattr(r, "out%d_%d" % (place, number))
        copies.out(scratch.at[at, pl.ds(row, count), :], ref)


def decoder_first(meta, lens, u3, w3, bias, clips, frames, dim):
    wide = (dim, clips * frames)
    taps3 = taps_of(w3)

    def body(r, copies):
        loads = load_pieces(copies, w3, r.w3, r.meta, r.t3)
        for number, group in enumerate(groups_of(clips)):
            here = span(group, frames)
            inside = mask_of(r.lens, group, frames)
            waits = waits_of(w3, loads) if number == 0 else ()
            first = conv_forward(r.t3, r.u3, group, frames, taps3, 0, waits) + r.bias[:, 3:4]
            r.first[:, here] = first
            r.u4[:, here] = (inside * elu(first)).astype(BF16)

    return run(
        "decoder_first",
        body,
        meta,
        lens,
        {"u3": u3, "bias": bias},
        {"w3": arrays_of(w3)},
        {"first": (wide, F32, True), "u4": (wide, BF16, True)},
        {"t3": ((taps3, dim, dim), BF16)},
        len(w3),
        2 * taps3 * dim * dim * clips * frames,
    )


def decoder_rest(meta, lens, first, u4, w45, bias, out_rows, clips, frames, dim):
    wide = (dim, clips * frames)
    taps4 = taps_of(w45) - 1
    outs = {"u5": (wide, BF16, True)}
    outs["t45"] = ((taps4 + 1, dim, dim), BF16, True)
    outs.update(clip_outs(out_rows, clips, frames))

    def body(r, copies):
        loads = load_pieces(copies, w45, r.w45, r.meta, r.t45)
        wait_all(loads)
        for number, group in enumerate(groups_of(clips)):
            here = span(group, frames)
            inside = mask_of(r.lens, group, frames)
            second = conv_forward(r.t45, r.u4, group, frames, taps4) + r.bias[:, 4:5]
            r.u5[:, here] = (inside * elu(second)).astype(BF16)
            third = conv_forward(r.t45, r.u5, group, frames, 1, taps4) + r.bias[:, 5:6]
            result = (inside * (r.first[:, here] + third)).astype(BF16)
            put_clips(copies, r, r.work, number, group, result, frames, out_rows)

    return run(
        "decoder_rest",
        body,
        meta,
        lens,
        {"first": first, "u4": u4, "bias": bias},
        {"w45": arrays_of(w45)},
        outs,
        {"work": ((clips, dim, frames), BF16)},
        len(w45) + len(out_rows) * len(groups_of(clips)),
        2 * (taps4 + 1) * dim * dim * clips * frames,
    )


def waits_of(pieces, loads):
    waits = {}
    for piece, load in zip(pieces, loads):
        waits.setdefault(piece.target, []).append(load)
    return waits


class Rows:
    def __init__(self, dim, paired, short=False):
        self.dim = dim
        self.short = short
        self.paired = paired
        self.count = 2 if paired else 1
        self.height = dim // self.count

    def outs(self, columns):
        return {
            "sums%d" % number: ((self.height, columns), BF16, self.paired)
            for number in range(self.count)
        }

    def scratch(self, columns):
        return {} if self.paired else {"sums": ((self.dim, columns), BF16)}

    def put(self, r, copies, at, value):
        if not self.paired:
            r.sums[:, at] = value
            copies.out(r.sums.at[:, at], r.sums0.at[:, at])
            return
        quarter = self.dim // 4
        first = r.meta[1] == 0
        if self.short:
            run_of = quarter // 2
            for i in range(2):
                for j in range(2):
                    row = (j * 4 + i) * run_of
                    zero = value[row : row + run_of]
                    row = (i * 4 + 2 + j) * run_of
                    one = value[row : row + run_of]
                    row = (i * 2 + j) * run_of
                    r.sums0[row : row + run_of, at] = jnp.where(first, zero, one)
                    r.sums1[row : row + run_of, at] = jnp.where(first, one, zero)
            return
        run_of = quarter // 4
        for half in range(2):
            for block in range(4):
                row = half * 2 * quarter + block * run_of
                zero = value[row : row + run_of]
                one = value[row + quarter : row + quarter + run_of]
                row = (block * 2 + half) * run_of
                r.sums0[row : row + run_of, at] = jnp.where(first, zero, one)
                r.sums1[row : row + run_of, at] = jnp.where(first, one, zero)


def weight_grads(r, copies, rows, g, u, taps, offset, clips, frames, dim):
    for tap in range(taps):
        step = taps // 2 - tap
        left = g[...]
        if step != 0:
            for clip in range(clips):
                at = span((clip,), frames)
                r.work[:, at] = shifted(g[:, at], step)
            left = r.work[...]
        value = lax.dot_general(
            left, u[...], (((1,), (1,)), ((), ())), preferred_element_type=F32
        )
        rows.put(r, copies, slice(offset, offset + dim), value.astype(BF16))
        offset += dim
    total = jnp.sum(g[...].astype(F32), axis=1, keepdims=True)
    total = jnp.broadcast_to(total, (dim, 128)).astype(BF16)
    rows.put(r, copies, slice(offset, offset + 128), total)
    return offset + 128


def decoder_backward(
    meta, lens, cotangent, u3, u4, u5, t45, taps3, rows, clips, frames, dim
):
    wide = (dim, clips * frames)
    taps4 = t45.shape[0] - 1
    columns = (taps3 + taps4 + 1) * dim + 3 * 128

    def body(r, copies):
        loads = load_clips(copies, cotangent, r.cot, r.meta, r.clips, groups_of(clips))
        late = copies.start(r.u3, r.s3)
        for group, begun in zip(groups_of(clips), loads):
            here = span(group, frames)
            wait_all(begun)
            inside = mask_of(r.lens, group, frames)
            out = lanes([r.clips[clip] for clip in group])
            out = jnp.where(inside > 0, out, jnp.zeros((), BF16))
            r.g5[:, here] = out
            back = conv_backward(r.t45, r.g5, group, frames, 1, taps4)
            r.g4[:, here] = (back * inside * slope_of(r.u5[:, here])).astype(BF16)
            back = conv_backward(r.t45, r.g4, group, frames, taps4)
            total = out.astype(F32) + back * inside * slope_of(r.u4[:, here])
            r.s_g3[:, here] = total.astype(BF16)
            copies.out(r.s_g3.at[:, here], r.g3.at[:, here])
        sizes = (clips, frames, dim)
        at = weight_grads(r, copies, rows, r.g5, r.u5, 1, 0, *sizes)
        at = weight_grads(r, copies, rows, r.g4, r.u4, taps4, at, *sizes)
        late.wait()
        weight_grads(r, copies, rows, r.s_g3, r.s3, taps3, at, *sizes)

    return run(
        "decoder_backward",
        body,
        meta,
        lens,
        {"u4": u4, "u5": u5, "t45": t45},
        {"cot": arrays_of(cotangent), "u3": u3},
        {"g3": (wide, BF16, False), **rows.outs(columns)},
        {
            "clips": ((clips, dim, frames), BF16),
            "s3": (wide, BF16),
            "g5": (wide, BF16),
            "g4": (wide, BF16),
            "s_g3": (wide, BF16),
            "work": (wide, BF16),
            **rows.scratch(columns),
        },
        (len(cotangent) + 1) * len(groups_of(clips))
        + 1
        + rows.count * (taps3 + taps4 + 4),
        2 * (taps3 + 2 * taps4 + 2) * dim * dim * clips * frames,
    )


def encoder_forward(
    meta, lens, mask, tokens, w012, bias, q0, q1, ahead, g3, clips, frames, dim
):
    wide = (dim, clips * frames)
    groups = groups_of(clips)
    taps0 = taps_of(w012[0])
    weights = [piece for layer in w012 for piece in layer]
    places = (0, taps0, taps0 + 1)

    def body(r, copies):
        loads = load_clips(copies, tokens, r.tokens, r.meta, r.clips, groups[:1])
        begun, refs = [], iter(r.w012)
        for place, layer in zip(places, w012):
            target = r.t.at[pl.ds(place, taps_of(layer))]
            begun.append([p.load(copies, next(refs), r.meta, target) for p in layer])
        loads += load_clips(copies, tokens, r.tokens, r.meta, r.clips, groups[1:])
        late = [copies.start(r.q0, r.s_q0), copies.start(r.q1, r.s_q1)]
        copies.open += load_pieces(copies, ahead, r.ahead, r.meta, r.next)
        copies.out(r.g3, r.g3_near)
        for number, group in enumerate(groups):
            here = span(group, frames)
            wait_all(loads[number])
            inside = mask_of(r.lens, group, frames)
            start = inside * lanes([r.clips[clip] for clip in group]).astype(F32)
            r.s0[:, here] = elu(start).astype(BF16)
            copies.out(r.s0.at[:, here], r.u0.at[:, here])
            if number == 0:
                wait_all(begun[0])
            first = conv_forward(r.t, r.s0, group, frames, taps0) + r.bias[:, 0:1]
            r.s1[:, here] = (inside * elu(first)).astype(BF16)
            copies.out(r.s1.at[:, here], r.u1.at[:, here])
            if number == 0:
                wait_all(begun[1])
                wait_all(begun[2])
            second = conv_forward(r.t, r.s1, group, frames, 1, taps0) + r.bias[:, 1:2]
            r.u2_near[:, here] = elu(inside * (start + second)).astype(BF16)
            copies.out(r.u2_near.at[:, here], r.u2.at[:, here])
            latent = conv_forward(r.t, r.u2_near, group, frames, taps0, taps0 + 1)
            latent = latent + r.bias[:, 2:3]
            if number == 0:
                wait_all(late)
            double = 2.0 * counted_of(r.lens, r.mask, group, frames)
            miss = r.s_q0[:, here].astype(F32) - latent
            r.gq0[:, here] = (double * miss).astype(BF16)
            r.gq1[:, here] = (double * (miss + r.s_q1[:, here].astype(F32))).astype(BF16)

    return run(
        "encoder_forward",
        body,
        meta,
        lens,
        {"mask": mask, "bias": bias},
        {
            "tokens": arrays_of(tokens),
            "w012": arrays_of(weights),
            "q0": q0,
            "q1": q1,
            "ahead": arrays_of(ahead),
            "g3": g3,
        },
        {
            "u0": (wide, BF16, False),
            "u1": (wide, BF16, False),
            "u2": (wide, BF16, False),
            "u2_near": (wide, BF16, True),
            "gq0": (wide, BF16, True),
            "gq1": (wide, BF16, True),
            "next": ((taps_of(ahead), dim, dim), BF16, True),
            "g3_near": (wide, BF16, True),
        },
        {
            "clips": ((clips, dim, frames), BF16),
            "t": ((2 * taps0 + 1, dim, dim), BF16),
            **{name: (wide, BF16) for name in ("s0", "s1", "s_q0", "s_q1")},
        },
        (len(tokens) + 3) * len(groups) + len(ahead) + len(weights) + 3,
        2 * (2 * taps0 + 1) * dim * dim * clips * frames,
    )


def latent_backward(
    meta, lens, ids, g3, t3, gq0, gq1, u2, taps2, codes, ahead, rows, clips, frames, dim
):
    wide = (dim, clips * frames)
    taps3 = t3.shape[0]
    columns = taps2 * dim + 128 + LEVELS * codes

    def body(r, copies):
        copies.open += load_pieces(copies, ahead, r.ahead, r.meta, r.next)
        for group in groups_of(clips):
            here = span(group, frames)
            inside = mask_of(r.lens, group, frames)
            back = conv_backward(r.t3, r.g3, group, frames, taps3)
            extra = BETA * r.gq1[:, here].astype(F32)
            r.g2[:, here] = (back * inside - extra).astype(BF16)
        sizes = (clips, frames, dim)
        offset = weight_grads(r, copies, rows, r.g2, r.u2, taps2, 0, *sizes)
        for level, grad in enumerate((r.gq0, r.gq1)):
            values = []
            for group in range(dim // GW):
                at = slice(group * GW, (group + 1) * GW)
                one_hot(r.ids, r.hot, level, group, clips, frames, dim)
                values.append(
                    lax.dot_general(
                        grad[at, :],
                        r.hot[...],
                        (((1,), (1,)), ((), ())),
                        preferred_element_type=F32,
                    ).astype(BF16)
                )
            value = jnp.concatenate(values, axis=0)
            rows.put(r, copies, slice(offset, offset + codes), value)
            offset += codes

    return run(
        "latent_backward",
        body,
        meta,
        lens,
        {"ids": ids, "g3": g3, "t3": t3, "gq0": gq0, "gq1": gq1, "u2": u2},
        {"ahead": arrays_of(ahead)},
        {
            "g2": (wide, BF16, True),
            "next": ((taps_of(ahead), dim, dim), BF16, True),
            **rows.outs(columns),
        },
        {
            "hot": ((codes, clips * frames), BF16),
            "work": (wide, BF16),
            **rows.scratch(columns),
        },
        len(ahead) + rows.count * (taps2 + 1 + LEVELS),
        2 * ((taps3 + taps2) * dim + LEVELS * codes) * dim * clips * frames,
    )


def encoder_backward(meta, lens, g2, u2, u1, u0, t, taps0, ahead, clips, frames, dim):
    wide = (dim, clips * frames)

    def body(r, copies):
        second = copies.start(r.u2, r.s2)
        first = copies.start(r.u1, r.u1_near)
        copies.out(r.u0, r.u0_near)
        copies.open += load_pieces(copies, ahead, r.ahead, r.meta, r.next)
        for number, group in enumerate(groups_of(clips)):
            here = span(group, frames)
            inside = mask_of(r.lens, group, frames)
            back = conv_backward(r.t, r.g2, group, frames, taps0, 1)
            if number == 0:
                second.wait()
            r.g1[:, here] = (back * inside * slope_of(r.s2[:, here])).astype(BF16)
            back = conv_backward(r.t, r.g1, group, frames, 1)
            if number == 0:
                first.wait()
            r.g0[:, here] = (back * inside * slope_of(r.u1_near[:, here])).astype(BF16)

    names = ("g1", "g0", "u1_near", "u0_near")
    return run(
        "encoder_backward",
        body,
        meta,
        lens,
        {"g2": g2, "t": t},
        {"u2": u2, "u1": u1, "u0": u0, "ahead": arrays_of(ahead)},
        {
            **{name: (wide, BF16, True) for name in names},
            "next": ((taps_of(ahead), dim, dim), BF16, True),
        },
        {"s2": (wide, BF16)},
        len(ahead) + 3,
        2 * (taps0 + 1) * dim * dim * clips * frames,
    )


def encoder_grads(meta, lens, g0, u0, g1, u1, taps0, rows, clips, frames, dim):
    columns = (taps0 + 1) * dim + 2 * 128

    def body(r, copies):
        sizes = (clips, frames, dim)
        at = weight_grads(r, copies, rows, r.g0, r.u0, taps0, 0, *sizes)
        weight_grads(r, copies, rows, r.g1, r.u1, 1, at, *sizes)

    return run(
        "encoder_grads",
        body,
        meta,
        lens,
        {"g0": g0, "u0": u0, "g1": g1, "u1": u1},
        {},
        rows.outs(columns),
        {"work": ((dim, clips * frames), BF16), **rows.scratch(columns)},
        1 + rows.count * (taps0 + 3),
        2 * (taps0 + 1) * dim * dim * clips * frames,
    )


def tokens_backward(meta, lens, g0, u0, g1, t, out_rows, clips, frames, dim):
    taps0 = t.shape[0]

    def body(r, copies):
        for number, group in enumerate(groups_of(clips)):
            here = span(group, frames)
            inside = mask_of(r.lens, group, frames)
            back = conv_backward(r.t, r.g0, group, frames, taps0)
            total = r.g1[:, here].astype(F32) + back * inside * slope_of(r.u0[:, here])
            total = (inside * total).astype(BF16)
            put_clips(copies, r, r.work, number, group, total, frames, out_rows)

    result = run(
        "tokens_backward",
        body,
        meta,
        lens,
        {"g0": g0, "g1": g1, "u0": u0, "t": t},
        {},
        clip_outs(out_rows, clips, frames),
        {"work": ((clips, dim, frames), BF16)},
        len(out_rows) * len(groups_of(clips)),
        2 * taps0 * dim * dim * clips * frames,
    )
    return clip_results(result, out_rows, clips)


def unpack(meta, pieces, blocks, half):
    outs = []
    for taps, width, has_bias in blocks:
        outs.append(struct((taps, half, width), F32))
        if has_bias:
            outs.append(struct((1, half), F32))

    def body(meta_ref, mine_ref, other_ref, *refs):
        take = iter(refs)
        first = meta_ref[1] == 0

        def columns(at):
            mine, other = mine_ref[:, at], other_ref[:, at]
            return jnp.concatenate(
                [jnp.where(first, mine, other), jnp.where(first, other, mine)], axis=0
            ).astype(F32)

        offset = 0
        for taps, width, has_bias in blocks:
            out = next(take)
            for tap in range(taps):
                out[tap] = columns(slice(offset, offset + width))
                offset += width
            if has_bias:
                next(take)[...] = columns(slice(offset, offset + 128)).T[0:1]
                offset += 128

    return pl.pallas_call(
        body,
        out_shape=tuple(outs),
        in_specs=[SMEM, VMEM, VMEM],
        out_specs=tuple(VMEM for _ in outs),
        compiler_params=pltpu.CompilerParams(vmem_limit_bytes=LIMIT),
    )(meta, *pieces)


def in_three(array, rows, columns):
    terms = []
    for _ in range(3):
        term = lax.reduce_precision(array, exponent_bits=8, mantissa_bits=7)
        terms.append(term.astype(BF16).reshape(-1))
        array = array - term
    terms = jnp.concatenate(terms)
    return jnp.pad(terms, (0, rows * columns - terms.size)).reshape(1, rows, columns)


def from_three(block, shape):
    size = shape[0] * shape[1]
    terms = block.reshape(-1)[: 3 * size].reshape((3,) + shape).astype(F32)
    return (terms[0] + terms[1]) + terms[2]


class Pairs:
    BITS = {"core": 1, "x": 2, "zl": 4, "zh": 8}

    def __init__(self, rows, clips):
        self.chan = lax.axis_index("chan")
        self.dp = lax.axis_index("dp")
        self.core = self.bit("core")
        x = self.bit("x")
        other = (1 - self.chan) * rows
        piece = rows // 4
        here = [(self.core, x), (self.core, 1 - x), (1 - self.core, x), (1 - self.core, 1 - x)]
        self.piece = (self.core * 2 + x) * piece
        self.meta = jnp.stack(
            [self.chan, self.core, self.chan * rows, other]
            + [other + (c * 2 + b) * piece for c, b in here]
            + [self.chan * clips]
            + [other + self.core * 2 * piece, other + (1 - self.core) * 2 * piece]
        ).astype(jnp.int32)

    def bit(self, name):
        if name == "chan":
            return self.chan
        return (self.dp & self.BITS[name]) // self.BITS[name]

    def swap(self, value, name):
        if name == "chan":
            return lax.ppermute(value, "chan", [(0, 1), (1, 0)])
        mask = self.BITS[name]
        return lax.ppermute(value, "dp", [(i, i ^ mask) for i in range(16)])

    def swap_by_core(self, value, names):
        pairs = []
        for place in range(32):
            other = place
            for name in names[(place // 2) & 1].split("+"):
                other ^= 1 if name == "chan" else 2 * self.BITS[name]
            pairs.append((place, other))
        return lax.ppermute(value, ("dp", "chan"), pairs)

    def bit_by_core(self, names):
        return jnp.where(self.core == 0, self.bit(names[0]), self.bit(names[1]))

    def piece_of(self, own):
        return lax.dynamic_slice_in_dim(own, self.piece, own.shape[1] // 4, 1)

    def half_of(self, own):
        half = own.shape[1] // 2
        return lax.dynamic_slice_in_dim(own, self.core * half, half, 1)

    def spread(self, near):
        far = self.swap(near, "x")
        return near, far, self.swap(near, "core"), self.swap(far, "core")

    def ordered(self, own, came):
        first = self.chan == 0
        return jnp.concatenate([jnp.where(first, own, came), jnp.where(first, came, own)])

    @property
    def bits(self):
        return jnp.stack([self.bit_by_core(pair) for pair in PAIRS]).astype(jnp.int32)

    def start(self, grads, steps):
        kept, sent = grads
        return Reduction(self, kept, self.swap(sent, "core"), steps)


XZ, ZX, CC, HH = ("x", "zl"), ("zl", "x"), ("chan", "chan"), ("zh", "zh")
PAIRS = (XZ, ZX, CC, HH)
START = (("halve", XZ), ("halve2", ZX, CC), ("keep", HH))
STEPS_2 = START + (("double", ZX), ("double", XZ), ("double", ("core", "core")))
STEPS_4 = START + (("double2", ZX, XZ), ("double", ("core", "core")))
STEPS = STEPS_2, STEPS_2, STEPS_4


class Reduction:
    def __init__(self, links, kept, came, steps):
        self.links = links
        self.steps = steps
        self.at = 0
        self.terms = [(kept, 0)]
        self.came = [came]
        self.value = None
        self.cuts = [PAIRS.index(n) for kind, *names in steps if "halve" in kind for n in names]
        self.cut = 0

    @property
    def done(self):
        return self.at == len(self.steps)

    @property
    def result(self):
        return [self.value] + self.came

    def plan(self):
        if self.value is not None:
            how = self.steps[self.at - 1][0]
            lead = {"keep": (), "double": (2,), "double2": (2, 2)}[how]
            return how, [self.value] + self.came, [lead + self.value.shape]
        self.terms += [(array, self.cut) for array in self.came]
        how = self.steps[self.at][0]
        last = self.cut + {"halve": 1, "halve2": 2}.get(how, 0)
        blocks = [
            term.reshape((2,) * (last - first) + (-1, term.shape[-1]))
            for term, first in self.terms
        ]
        return how, blocks, [blocks[0].shape[-2:]] * (3 if how == "halve2" else 1)

    def fill(self, how, refs, outs, bits):
        if self.value is not None:
            places = [bits[PAIRS.index(n)] for n in self.steps[self.at - 1][1:] if n in PAIRS]
            if how == "keep":
                total = refs[0][...].astype(F32) + refs[1][...].astype(F32)
                outs[0][...] = total.astype(BF16)
            elif how == "double":
                outs[0][places[0]] = refs[0][...]
                outs[0][1 - places[0]] = refs[1][...]
            else:
                inner, outer = places
                outs[0][outer, inner] = refs[0][...]
                outs[0][outer, 1 - inner] = refs[1][...]
                outs[0][1 - outer, inner] = refs[2][...]
                outs[0][1 - outer, 1 - inner] = refs[3][...]
            return
        flips = {"halve": ((1,),), "halve2": ((1, 0), (0, 1), (1, 1))}.get(how, ((),))
        for out, flip in zip(outs, flips):
            place = [bits[cut] for cut in self.cuts[: self.cut]]
            for cut, turned in zip(self.cuts[self.cut :], flip):
                place.append(1 - bits[cut] if turned else bits[cut])
            sums = None
            for ref, (_, first) in zip(refs, self.terms):
                where = tuple(place[first:])
                piece = (ref[where] if where else ref[...]).astype(F32)
                sums = piece if sums is None else sums + piece
            out[...] = sums.astype(BF16)

    def send(self, sent):
        kind, *names = self.steps[self.at]
        sent = [array.reshape(-1, array.shape[-1]) for array in sent]
        if "halve" in kind:
            self.cut += len(names)
        else:
            self.value = sent[0]
        if len(names) == 2:
            names.append(tuple(a + "+" + b for a, b in zip(*names)))
        sent = sent * len(names) if len(sent) == 1 else sent
        self.came = [self.links.swap_by_core(a, n) for a, n in zip(sent, names)]
        self.at += 1


def advance(after, *reductions):
    came = lax.optimization_barrier((tuple(r.came for r in reductions), tuple(after)))[0]
    arrays, counts, shapes, widths, hows = [], [], [], [], []
    for reduction, array in zip(reductions, came):
        reduction.came = list(array)
        how, operands, targets = reduction.plan()
        hows.append(how)
        counts.append(len(operands))
        widths.append(len(targets))
        arrays += [held(operand) for operand in operands]
        shapes += [pltpu.VMEM(target, BF16) for target in targets]

    def body(bits_ref, *refs):
        taken, filled = 0, len(arrays)
        for reduction, how, count, width in zip(reductions, hows, counts, widths):
            outs = refs[filled : filled + width]
            reduction.fill(how, refs[taken : taken + count], outs, bits_ref)
            taken += count
            filled += width

    sent = pl.pallas_call(
        body,
        out_shape=tuple(shapes),
        in_specs=[SMEM] + [VMEM] * len(arrays),
        out_specs=tuple(VMEM for _ in shapes),
        compiler_params=pltpu.CompilerParams(vmem_limit_bytes=8 * MIB),
        cost_estimate=pl.CostEstimate(
            flops=COVER["advance"], bytes_accessed=COVER["advance"], transcendentals=0
        ),
    )(reductions[0].links.bits, *arrays)
    filled = 0
    for reduction, width in zip(reductions, widths):
        reduction.send(sent[filled : filled + width])
        filled += width
    return list(sent)


def on_pairs(
    tokens,
    lengths,
    frame_mask,
    code_ids,
    cotangent,
    weights,
    biases,
    codebook,
):
    chan = 2
    rows = tokens.shape[1]
    frames = tokens.shape[2]
    dim = rows * chan
    clips = tokens.shape[0] // chan
    codes = codebook.shape[2]
    sizes = (clips, frames, dim)
    links = Pairs(rows, clips)
    meta = links.meta
    mine = functools.partial(
        lax.dynamic_slice_in_dim, start_index=links.chan * clips, slice_size=clips, axis=0
    )
    others = functools.partial(
        lax.dynamic_slice_in_dim, start_index=(1 - links.chan) * clips, slice_size=clips, axis=0
    )
    taps = [w.shape[0] for w in weights]
    own, other, pieces, halves = 2, 3, (4, 5, 6, 7), (9, 10)

    split = taps[3] - 1
    lens = mine(lengths)
    mask = mine(frame_mask)
    ids = mine(code_ids).reshape(-1, frames)
    bias = jnp.stack(biases + (jnp.zeros_like(biases[0]),) * 2)
    first_pieces = lax.optimization_barrier(
        (
            links.piece_of(codebook),
            links.piece_of(weights[3][:split]),
            links.half_of(weights[3][split:]),
        )
    )
    near_book, near3a, near3b = (links.swap(piece, "chan") for piece in first_pieces)
    dec = jnp.concatenate([weights[4], weights[5]])
    dec_piece = jnp.concatenate([links.piece_of(dec), in_three(bias, rows // 4, dim)])
    enc = jnp.concatenate([weights[0], weights[1], weights[2]])
    near_book, dec_piece, enc_piece, cot_send, tok_send = lax.optimization_barrier(
        (near_book, dec_piece, links.piece_of(enc), others(cotangent), others(tokens))
    )
    far_book = links.spread(near_book)
    near45 = links.swap(dec_piece, "chan")
    far3a = links.spread(near3a)
    near012 = links.swap(enc_piece, "chan")
    cot_send = tie(cot_send, near3a)
    cot_other = links.swap(cot_send, "chan")
    book = []
    for level in range(LEVELS):
        book.append(Piece(codebook, own, level, level, 1))
        book += [Piece(a, s, level, level, 1) for a, s in zip(far_book, pieces)]
    found = lookup(meta, lens, tie(ids, cot_send, tok_send), book, *sizes)
    tok_send = tie(tok_send, found.u3)
    tok_other = links.swap(tok_send, "chan")
    near3b, near45 = tie((near3b, near45), found.u3)
    far3b = near3b, links.swap(near3b, "core")
    bias_came = from_three(near45[taps[4] + taps[5] :], bias.shape)
    bias = links.ordered(bias.T, bias_came.T)
    w3 = []
    for first, last in ((0, 1), (1, 3), (3, split)):
        w3.append(Piece(weights[3], own, first, first, last - first))
        w3 += [Piece(a, s, first, first, last - first) for a, s in zip(far3a, pieces)]
    w3 += [Piece(weights[3], own, split, split, taps[3] - split)]
    w3 += [Piece(a, s, 0, split) for a, s in zip(far3b, halves)]
    far45_x = links.swap(near45, "x")
    dec_first = decoder_first(
        meta, lens, found.u3, w3, bias, *sizes
    )
    near45, far45_x = tie((near45, far45_x), dec_first.u4)
    far45 = near45, far45_x, links.swap(near45, "core"), links.swap(far45_x, "core")
    w45 = [Piece(weights[4], own), Piece(weights[5], own, 0, taps[4])]
    w45 += [Piece(a, s, 0, 0, taps[4] + taps[5]) for a, s in zip(far45, pieces)]
    out_rows = ((own, rows), (other, rows))
    dec_out = decoder_rest(
        meta, lens, dec_first.first, dec_first.u4, w45, bias, out_rows, *sizes
    )
    near012 = tie(near012, dec_out.u5)
    far012_x = links.swap(near012, "x")
    rows_a = rows_c = rows_d = Rows(dim, True)
    cot = [Piece(cotangent, own, clip=8, count=clips)]
    cot.append(Piece(tie(cot_other, near012), other))
    dec_back = decoder_backward(
        meta,
        lens,
        cot,
        found.u3_far,
        dec_first.u4,
        dec_out.u5,
        dec_out.t45,
        taps[3],
        rows_a,
        *sizes,
    )
    near012, far012_x = tie((near012, far012_x), dec_back.g3)
    far012 = near012, far012_x, links.swap(near012, "core"), links.swap(far012_x, "core")

    def enc_pieces(which):
        listed = []
        place = 0
        for number in which:
            listed.append(Piece(weights[number], own, 0, place))
            place += taps[number]
        start = sum(taps[: which[0]])
        listed += [Piece(a, s, start, 0, place) for a, s in zip(far012, pieces)]
        return listed

    red_a = links.start([dec_back.sums0, tie(dec_back.sums1, tok_other)], STEPS[0])
    out_own, out_send = clip_results(dec_out, out_rows, clips)
    out_send[0] = tie(out_send[0], tok_other)
    out_came = [links.swap(out_send[0], "chan")]
    tok = [Piece(tokens, own, clip=8, count=clips)]
    tok.append(Piece(tie(tok_other, dec_back.g3, out_send[0]), other))
    enc_out = encoder_forward(
        meta,
        lens,
        mask,
        tok,
        [enc_pieces([0]), enc_pieces([1]), enc_pieces([2])],
        bias,
        found.q0,
        found.q1,
        w3,
        dec_back.g3,
        *sizes,
    )
    sent = advance([enc_out.u2], red_a)
    out_came.append(links.swap(tie(out_send[1], *sent), "chan"))
    lat = latent_backward(
        meta,
        lens,
        ids,
        tie(enc_out.g3_near, out_came[0], *sent),
        enc_out.next,
        enc_out.gq0,
        enc_out.gq1,
        enc_out.u2_near,
        taps[2],
        codes,
        enc_pieces([1, 2]),
        rows_c,
        *sizes,
    )
    red_c = links.start([lat.sums0, lat.sums1], STEPS[1])
    sent = advance([lat.g2], red_a)
    enc_back = encoder_backward(
        meta,
        lens,
        lat.g2,
        tie(enc_out.u2, out_came[1], *sent),
        enc_out.u1,
        enc_out.u0,
        lat.next,
        taps[0],
        enc_pieces([0]),
        *sizes,
    )
    sent = advance([enc_back.g0], red_c)
    enc_sums = encoder_grads(
        meta,
        lens,
        tie(enc_back.g0, *sent),
        enc_back.u0_near,
        enc_back.g1,
        enc_back.u1_near,
        taps[0],
        rows_d,
        *sizes,
    )
    red_d = links.start([enc_sums.sums0, enc_sums.sums1], STEPS[2])
    sent = advance([enc_sums.sums0], red_a)
    grad_own, grad_other = tokens_backward(
        meta,
        lens,
        tie(enc_back.g0, *sent),
        enc_back.u0_near,
        enc_back.g1,
        enc_back.next,
        out_rows,
        *sizes,
    )
    sent = advance(grad_other, *([red_a] if A_EARLY else []), red_c, red_d)
    grad_came = []
    if len(GRAD_SLOTS) == 4:
        grad_other = [g[at : at + clips // 4] for g in grad_other for at in (0, clips // 4)]
    shapes = {
        red_a: [(1, dim, True), (taps[4], dim, True), (taps[3], dim, True)],
        red_c: [(taps[2], dim, True), (LEVELS, codes, False)],
        red_d: [(taps[0], dim, True), (1, dim, True)],
    }
    results = {}
    slot = 0
    groups = (red_a, red_c, red_d)
    while not all(r.done for r in groups):
        slot += 1
        for half, (begin, end) in enumerate(GRAD_SLOTS):
            if slot == begin:
                grad_came.append(links.swap(tie(grad_other[half], *sent), "chan"))
        for half, (begin, end) in enumerate(GRAD_SLOTS):
            if slot == end:
                sent = list(sent) + [grad_came[half]]
        active = [r for r in groups if not r.done]
        for r in groups:
            if r.done and r not in results:
                mine_rows, other_rows = r.result
                mine_rows = tie(mine_rows, *sent)
                results[r] = unpack(meta, [mine_rows, other_rows], shapes[r], rows)
                sent = list(sent) + list(results[r][:1])
        if slot == OUT_SLOTS[0]:
            came = jnp.concatenate(tie(out_came, *sent))
            output = links.ordered(jnp.concatenate(out_own), came)
            sent = list(sent) + [output]
        if slot == OUT_SLOTS[1]:
            came = jnp.concatenate(tie(grad_came, *sent)).astype(F32)
            tokens_grad = links.ordered(jnp.concatenate(grad_own).astype(F32), came)
            sent = list(sent) + [tokens_grad]
        sent = advance(sent, *active)
    if slot < OUT_SLOTS[1]:
        came = jnp.concatenate(tie(grad_came, *sent)).astype(F32)
        tokens_grad = links.ordered(jnp.concatenate(grad_own).astype(F32), came)
    for r in groups:
        if r not in results:
            results[r] = unpack(meta, r.result, shapes[r], rows)
    a, c, d = results[red_a], results[red_c], results[red_d]
    w_grads = [d[0], d[2], c[0], a[4], a[2], a[0]]
    b_grads = [v.reshape(rows) for v in (d[1], d[3], c[1], a[5], a[3], a[1])]
    grads = [g for pair in zip(w_grads, b_grads) for g in pair]
    return (output, tokens_grad, *grads, c[2])


def on_others(
    tokens,
    lengths,
    frame_mask,
    code_ids,
    cotangent,
    weights,
    biases,
    codebook,
):
    chan = lax.axis_size("chan")
    place = lax.axis_index("chan")
    rows = tokens.shape[1]
    frames = tokens.shape[2]
    dim = rows * chan
    clips = tokens.shape[0] // chan
    codes = codebook.shape[2]
    sizes = (clips, frames, dim)
    meta = jnp.zeros((9,), jnp.int32)
    mine = functools.partial(
        lax.dynamic_slice_in_dim, start_index=place * clips, slice_size=clips, axis=0
    )
    taps = [w.shape[0] for w in weights]

    def gathered(*arrays):
        return [Piece(lax.all_gather(jnp.concatenate(arrays), "chan", axis=1, tiled=True))]

    def part(pieces, start, count):
        return [Piece(pieces[0].array, None, start, 0, count)]

    def clips_in(array):
        return [Piece(lax.all_to_all(array, "chan", 0, 1, tiled=True))]

    def clips_out(array):
        return lax.all_to_all(array, "chan", 1, 0, tiled=True)

    def reduced(grads):
        part = lax.psum_scatter(grads.astype(F32), "chan", scatter_dimension=0, tiled=True)
        return lax.psum(part, "dp")

    def columns(total, offset, count, width):
        block = total[:, offset : offset + count * width].reshape(rows, count, width)
        return jnp.transpose(block, (1, 0, 2))

    bias = jnp.stack(biases + (jnp.zeros_like(biases[0]),) * 2, axis=1)
    bias = lax.all_gather(bias, "chan", axis=0, tiled=True)
    lens = mine(lengths)
    mask = mine(frame_mask)
    ids = mine(code_ids).reshape(-1, frames)
    w3 = gathered(weights[3])
    w45 = gathered(weights[4], weights[5])
    w012 = gathered(weights[0], weights[1], weights[2])
    rows_of = Rows(dim, False)
    out_rows = ((None, dim),)
    found = lookup(meta, lens, ids, gathered(codebook), *sizes)
    dec_first = decoder_first(meta, lens, found.u3, w3, bias, *sizes)
    dec_out = decoder_rest(
        meta, lens, dec_first.first, dec_first.u4, w45, bias, out_rows, *sizes
    )
    dec_back = decoder_backward(
        meta,
        lens,
        clips_in(cotangent),
        found.u3_far,
        dec_first.u4,
        dec_out.u5,
        dec_out.t45,
        taps[3],
        rows_of,
        *sizes,
    )
    enc_out = encoder_forward(
        meta,
        lens,
        mask,
        clips_in(tokens),
        [
            part(w012, 0, taps[0]),
            part(w012, taps[0], taps[1]),
            part(w012, taps[0] + taps[1], taps[2]),
        ],
        bias,
        found.q0,
        found.q1,
        w3,
        dec_back.g3,
        *sizes,
    )
    lat = latent_backward(
        meta,
        lens,
        ids,
        enc_out.g3_near,
        enc_out.next,
        enc_out.gq0,
        enc_out.gq1,
        enc_out.u2_near,
        taps[2],
        codes,
        part(w012, taps[0], 1 + taps[2]),
        rows_of,
        *sizes,
    )
    enc_back = encoder_backward(
        meta,
        lens,
        lat.g2,
        enc_out.u2,
        enc_out.u1,
        enc_out.u0,
        lat.next,
        taps[0],
        part(w012, 0, taps[0]),
        *sizes,
    )
    enc_sums = encoder_grads(
        meta,
        lens,
        enc_back.g0,
        enc_back.u0_near,
        enc_back.g1,
        enc_back.u1_near,
        taps[0],
        rows_of,
        *sizes,
    )
    ((grad,),) = tokens_backward(
        meta,
        lens,
        enc_back.g0,
        enc_back.u0_near,
        enc_back.g1,
        enc_back.next,
        out_rows,
        *sizes,
    )
    ((out,),) = clip_results(dec_out, out_rows, clips)
    a, c, d = (reduced(x.sums0) for x in (dec_back, lat, enc_sums))
    placed = (
        (d, 0, taps[0]),
        (d, taps[0] * dim + 128, 1),
        (c, 0, taps[2]),
        (a, (1 + taps[4]) * dim + 256, taps[3]),
        (a, dim + 128, taps[4]),
        (a, 0, 1),
    )
    grads = []
    for total, start, count in placed:
        grads.append(columns(total, start, count, dim))
        grads.append(total[:, start + count * dim])
    books = columns(c, taps[2] * dim + 128, LEVELS, codes)
    return (clips_out(out), clips_out(grad).astype(F32), *grads, books)


def on_device(step, tokens, lengths, frame_mask, code_ids, cotangent, *params):
    weights, biases = params[0:12:2], params[1:12:2]
    return step(
        tokens, lengths, frame_mask, code_ids, cotangent, weights, biases, params[12]
    )


def solution(mesh):
    paired = mesh.shape["chan"] == 2 and mesh.shape["dp"] == 16
    weight = P(None, "chan", None)
    vector = P("chan")
    clip_rows = P("dp", "chan", None)
    in_specs = (
        (clip_rows, P("dp"), P("dp", None), P("dp", None, None), clip_rows)
        + (weight, vector) * 6
        + (weight,)
    )
    out_specs = (clip_rows, clip_rows) + (weight, vector) * 6 + (weight,)
    return jax.shard_map(
        functools.partial(on_device, on_pairs if paired else on_others),
        mesh=mesh,
        in_specs=in_specs,
        out_specs=out_specs,
        check_vma=False,
    )
```
